128 devices in a mesh: gx: 4 (over y), gy: 8 (over x_hi, z), gz: 4 (over x_lo, core).
Axes of the slice: x: 4 (x_hi: 2, x_lo: 2; x = x_hi * 2 + x_lo), y: 4, z: 4, core: 2. Of those that a mesh axis runs over, the one named last changes fastest.
Arguments:
- volume: bfloat16 [16, 32, 128, 256], P(None, 'gx', 'gy', 'gz'), may hold values from -6 to 6
- w_fine: bfloat16 [27, 16, 16], replicated, may hold values from -0.3125 to 0.3125
- w_down: bfloat16 [27, 16, 32], replicated, may hold values from -0.875 to 0.875
- w_lift: bfloat16 [32, 256], replicated, may hold values from -2 to 2
- w_coarse: bfloat16 [27, 256, 256], replicated, may hold values from -0.078125 to 0.078125
- w_proj: bfloat16 [256, 32], replicated, may hold values from -0.75 to 0.75
- w_up: bfloat16 [27, 32, 16], replicated, may hold values from -0.21875 to 0.21875
- cotangent: bfloat16 [16, 32, 128, 256], P(None, 'gx', 'gy', 'gz'), may hold values from -6 to 6
Outputs:
- decoded: bfloat16 [16, 32, 128, 256], P(None, 'gx', 'gy', 'gz')
- grad_w_fine: float32 [27, 16, 16], replicated
- grad_w_down: float32 [27, 16, 32], replicated
- grad_w_lift: float32 [32, 256], replicated
- grad_w_coarse: float32 [27, 256, 256], replicated
- grad_w_proj: float32 [256, 32], replicated
- grad_w_up: float32 [27, 32, 16], replicated
The draws below stay inside these ranges and needn't reach their ends.
All inputs are finite; a program needn't handle non-finite values.
Results may differ from the reference program's by a relative error of at most 0.035.
Values may be sent and summed in bfloat16 or wider, within the bound.
A program may use at most 128 MiB of HBM per device.

```python
import math
import jax
import jax.numpy as jnp
from jax import lax

C1 = 16
C2 = 32
C3 = 256
NX = 32
NY = 128
NZ = 256


def steps_of(own_key, shape, shards, smallest, top_value):
    factor_of = 1.0
    for axis_at, blocks in shards:
        draws = jax.random.uniform(jax.random.fold_in(jax.random.fold_in(own_key, 6), axis_at), (blocks,), jnp.float32, smallest / len(shards), top_value / len(shards))
        factor_of = factor_of * jnp.repeat(jnp.exp(draws), shape[axis_at] // blocks).reshape((-1,) + (1,) * (len(shape) - 1 - axis_at))
    return factor_of


def noise(own_key, shape, spread, most, cuts=(), kind=jnp.bfloat16):
    loudness = steps_of(own_key, shape, cuts, -0.22, 0.18) if cuts else 1.0
    array = jax.random.normal(own_key, shape, jnp.float32) * spread * loudness
    return jnp.minimum(jnp.maximum(array, -most), most).astype(kind)


def setup_inputs(seed: int = 0) -> dict:
    splits = jax.random.split(jax.random.key(seed), 9)
    volume = noise(splits[0], (C1, NX, NY, NZ), 1.0, 6.0, ((1, 4), (2, 8), (3, 4)))
    w_fine = noise(splits[1], (27, C1, C1), (27 * C1) ** -0.5, 0.3125)
    w_down = noise(splits[2], (27, C1, C2), (27 * C1 // 8) ** -0.5, 0.875)
    w_lift = noise(splits[3], (C2, C3), (C2 // 4) ** -0.5, 2.0)
    w_coarse = noise(splits[4], (27, C3, C3), (27 * C3) ** -0.5, 0.078125)
    w_proj = noise(splits[5], (C3, C2), (C3 // 4) ** -0.5, 0.75)
    w_up = noise(splits[6], (27, C2, C1), (27 * C2) ** -0.5, 0.21875)
    cotangent = noise(splits[7], (C1, NX, NY, NZ), 1.0, 6.0, ((1, 4), (2, 8), (3, 4)))
    return {"volume": volume, "w_fine": w_fine, "w_down": w_down, "w_lift": w_lift, "w_coarse": w_coarse, "w_proj": w_proj, "w_up": w_up, "cotangent": cotangent}


def silu_grad(values):
    sig = jax.nn.sigmoid(values)
    return sig * (1.0 + values * (1.0 - sig))

def shifted(padded, row_tap, col_tap, depth_tap, extent, channels_last):
    if channels_last:
        return padded[row_tap:row_tap + extent[0], col_tap:col_tap + extent[1], depth_tap:depth_tap + extent[2], :]
    return padded[:, row_tap:row_tap + extent[0], col_tap:col_tap + extent[1], depth_tap:depth_tap + extent[2]]

def apply_taps(padded, weight, extent, channels_last):
    result = None
    for row_tap in range(3):
        for col_tap in range(3):
            stacked = jnp.stack([shifted(padded, row_tap, col_tap, depth_tap, extent, channels_last) for depth_tap in range(3)]).astype(jnp.float32)
            first = 9 * row_tap + 3 * col_tap
            tap_weights = weight[first:first + 3].astype(jnp.float32)
            if channels_last:
                product = jnp.einsum('kxyzc,kco->xyzo', stacked, tap_weights)
            else:
                product = jnp.einsum('kcxyz,kco->oxyz', stacked, tap_weights)
            result = product if result is None else result + product
    return result

def gather_taps(padded, grad, extent, channels_last):
    pieces = []
    grad_wide = grad.astype(jnp.float32)
    for row_tap in range(3):
        for col_tap in range(3):
            stacked = jnp.stack([shifted(padded, row_tap, col_tap, depth_tap, extent, channels_last) for depth_tap in range(3)]).astype(jnp.float32)
            if channels_last:
                pieces.append(jnp.einsum('kxyzc,xyzo->kco', stacked, grad_wide))
            else:
                pieces.append(jnp.einsum('kcxyz,oxyz->kco', stacked, grad_wide))
    return jnp.concatenate(pieces, axis=0)

def flipped(weight):
    return jnp.transpose(jnp.flip(weight, 0), (0, 2, 1))

def pad_first(values):
    return jnp.pad(values, ((0, 0), (1, 1), (1, 1), (1, 1)))

def pad_last(values):
    return jnp.pad(values, ((1, 1), (1, 1), (1, 1), (0, 0)))

def pool_sum(values, factor):
    chans, depth, height, width = values.shape
    shaped = values.astype(jnp.float32).reshape(chans, depth // factor, factor, height // factor, factor, width // factor, factor)
    return lax.optimization_barrier(jnp.sum(shaped, axis=(2, 4, 6)))

def pool_mean(values, factor):
    return pool_sum(values, factor) / float(factor ** 3)

def upsample(values, factor):
    return jnp.repeat(jnp.repeat(jnp.repeat(values, factor, axis=1), factor, axis=2), factor, axis=3)

def reference(volume, w_fine, w_down, w_lift, w_coarse, w_proj, w_up, cotangent):
    fine_extent = volume.shape[1:]
    padded_fine = pad_first(volume)
    pre_fine = apply_taps(padded_fine, w_fine, fine_extent, False)
    act_fine = jax.nn.silu(pre_fine).astype(jnp.bfloat16)
    pool_mid = pool_mean(act_fine, 2).astype(jnp.bfloat16)
    mid_extent = pool_mid.shape[1:]
    padded_pool = pad_first(pool_mid)
    pre_mid = apply_taps(padded_pool, w_down, mid_extent, False)
    act_mid = jax.nn.silu(pre_mid).astype(jnp.bfloat16)
    pool_coarse = pool_mean(act_mid, 4).astype(jnp.bfloat16)
    pre_lift = jnp.einsum('cxyz,cd->xyzd', pool_coarse.astype(jnp.float32), w_lift.astype(jnp.float32))
    act_lift = jax.nn.silu(pre_lift).astype(jnp.bfloat16)
    coarse_extent = act_lift.shape[:3]
    padded_lift = pad_last(act_lift)
    pre_coarse = apply_taps(padded_lift, w_coarse, coarse_extent, True)
    act_coarse = jax.nn.silu(pre_coarse).astype(jnp.bfloat16)
    coarse_out = jnp.einsum('xyzd,dc->cxyz', act_coarse.astype(jnp.float32), w_proj.astype(jnp.float32))
    joined = (act_mid.astype(jnp.float32) + upsample(coarse_out, 4)).astype(jnp.bfloat16)
    padded_joined = pad_first(joined)
    pre_up = apply_taps(padded_joined, w_up, mid_extent, False)
    decoded = (act_fine.astype(jnp.float32) + upsample(jax.nn.silu(pre_up), 2)).astype(jnp.bfloat16)
    grad_out = cotangent.astype(jnp.float32) * jnp.float32(1.0 / math.sqrt(NX * NY * NZ))
    grad_pre_up = (pool_sum(grad_out, 2) * silu_grad(pre_up)).astype(jnp.bfloat16)
    grad_w_up = gather_taps(padded_joined, grad_pre_up, mid_extent, False)
    grad_joined = apply_taps(pad_first(grad_pre_up), flipped(w_up), mid_extent, False)
    grad_coarse_out = pool_sum(grad_joined, 4).astype(jnp.bfloat16)
    grad_w_proj = jnp.einsum('xyzd,cxyz->dc', act_coarse.astype(jnp.float32), grad_coarse_out.astype(jnp.float32))
    grad_act_coarse = jnp.einsum('cxyz,dc->xyzd', grad_coarse_out.astype(jnp.float32), w_proj.astype(jnp.float32))
    grad_pre_coarse = (grad_act_coarse * silu_grad(pre_coarse)).astype(jnp.bfloat16)
    grad_w_coarse = gather_taps(padded_lift, grad_pre_coarse, coarse_extent, True)
    grad_act_lift = apply_taps(pad_last(grad_pre_coarse), flipped(w_coarse), coarse_extent, True)
    grad_pre_lift = (grad_act_lift * silu_grad(pre_lift)).astype(jnp.bfloat16)
    grad_w_lift = jnp.einsum('cxyz,xyzd->cd', pool_coarse.astype(jnp.float32), grad_pre_lift.astype(jnp.float32))
    grad_pool_coarse = jnp.einsum('xyzd,cd->cxyz', grad_pre_lift.astype(jnp.float32), w_lift.astype(jnp.float32))
    grad_pre_mid = ((grad_joined + upsample(grad_pool_coarse, 4) / 64.0) * silu_grad(pre_mid)).astype(jnp.bfloat16)
    grad_w_down = gather_taps(padded_pool, grad_pre_mid, mid_extent, False)
    grad_pool_mid = apply_taps(pad_first(grad_pre_mid), flipped(w_down), mid_extent, False)
    grad_pre_fine = ((grad_out + upsample(grad_pool_mid, 2) / 8.0) * silu_grad(pre_fine)).astype(jnp.bfloat16)
    grad_w_fine = gather_taps(padded_fine, grad_pre_fine, fine_extent, False)
    return (decoded, grad_w_fine, grad_w_down, grad_w_lift, grad_w_coarse, grad_w_proj, grad_w_up)
```

```python
import functools
import math

import jax
import jax.numpy as jnp
from jax import lax
from jax.experimental import pallas as pl
from jax.experimental.pallas import tpu as pltpu
from jax.sharding import PartitionSpec as P

BF = jnp.bfloat16
F32 = jnp.float32
MESH = pl.DeviceIdType.MESH
LANES = 128


def dot(left, right):
    return jnp.dot(left, right, preferred_element_type=F32)


def dot_nt(left, right):
    return lax.dot_general(left, right, (((1,), (1,)), ((), ())), preferred_element_type=F32)


def dot_tn(left, right):
    return lax.dot_general(left, right, (((0,), (0,)), ((), ())), preferred_element_type=F32)


def sigmoid(values):
    return 0.5 * jnp.tanh(0.5 * values) + 0.5


def slope(values, sig):
    return sig * (1.0 + values * (1.0 - sig))


def lane_of(rows):
    return lax.broadcasted_iota(jnp.int32, (rows, LANES), 1)


def turn(row, by):
    if isinstance(by, int):
        by = by % LANES
        return row if by == 0 else pltpu.roll(row, by, 1)
    return pltpu.roll(row, lax.rem(by + 4 * LANES, LANES), 1)


def store_taps(ref, at, row, rows):
    ref[at + (pl.ds(0, rows),)] = turn(row, 1).astype(BF)
    ref[at + (pl.ds(rows, rows),)] = row.astype(BF)
    ref[at + (pl.ds(2 * rows, rows),)] = turn(row, -1).astype(BF)


def around(ref, x, y):
    block = ref[pl.ds(x, 3), pl.ds(y, 3)]
    return block.reshape(9 * block.shape[2], LANES)


def conv_pair(weight, ref, x, y):
    both = jnp.concatenate([around(ref, x, y), around(ref, x, y + 1)], axis=1)
    out = dot(weight, both)
    return out[:, :LANES], out[:, LANES:]


def pool_matrix():
    row = lax.broadcasted_iota(jnp.int32, (8 * LANES, LANES), 0)
    col = lax.broadcasted_iota(jnp.int32, (8 * LANES, LANES), 1)
    hit = (row // 256 == col // 32) & (row % 64 // 2 == col % 32)
    return jnp.where(hit, 1.0, 0.0).astype(BF)


def grow_matrix():
    row = lax.broadcasted_iota(jnp.int32, (LANES, 4 * LANES), 0)
    col = lax.broadcasted_iota(jnp.int32, (LANES, 4 * LANES), 1)
    hit = (row // 32 == col // LANES) & (row % 32 == col % 64 // 2)
    return jnp.where(hit, 1.0, 0.0).astype(BF)


def coarse_sum_matrix(tiles):
    row = lax.broadcasted_iota(jnp.int32, (8, tiles * LANES), 0)
    col = lax.broadcasted_iota(jnp.int32, (8, tiles * LANES), 1) % LANES
    return jnp.where((col < 32) & (col // 4 == row), 1.0, 0.0).astype(BF)


def coarse_grow_matrix(cells, gz):
    row = lax.broadcasted_iota(jnp.int32, (cells, LANES), 0)
    col = lax.broadcasted_iota(jnp.int32, (cells, LANES), 1)
    cell = jnp.where(col < 64, col, col - LANES)
    near = (cell >= -3) & (cell < 35)
    mid = cell + gz * 32
    hit = near & (mid >= 0) & (row == (mid + 4) // 4 - 1)
    return jnp.where(hit, 1.0, 0.0).astype(BF)


def pack_four(rows):
    lane = lane_of(rows[0].shape[0])
    total = None
    for q, row in enumerate(rows):
        part = turn(jnp.where(lane < 32, row, 0.0), 32 * q)
        total = part if total is None else total + part
    return total


def plane_rows(block):
    rows = jnp.swapaxes(block, 0, 1)
    return [jnp.concatenate([rows[2 * t], rows[2 * t + 1]], axis=1) for t in range(8)]


def arrange_kernel(vol_ref, v_ref, e_ref):
    lane = lane_of(16)

    def plane(x, edges):
        low, high = edges
        for t, tile in enumerate(plane_rows(vol_ref[:, x])):
            v_ref[x, t] = tile
            wide = tile.astype(F32)
            for b in range(2):
                at = x * 16 + 2 * t + b
                low = jnp.where(lane == at, turn(wide, at - 64 * b), low)
                high = jnp.where(lane == at, turn(wide, at - 64 * b - 63), high)
        return low, high

    zero = jnp.zeros((16, LANES), F32)
    low, high = lax.fori_loop(0, 8, plane, (zero, zero))
    e_ref[0] = low.astype(BF)
    e_ref[1] = high.astype(BF)


def halo_kernel(sizes, hx, ht, a_ref, e_ref, p_ref, er_ref, el_ref, send_sem, recv_sem):
    me = [lax.axis_index(name) for name in ("gx", "gy", "gz")]
    planes, tiles = a_ref.shape[:2]

    def there(at, step):
        if step == 0:
            return None
        return at[0] > 0 if step < 0 else at[0] < at[1] - 1

    def valid(steps):
        found = None
        for axis, step in enumerate(steps):
            test = there((me[axis], sizes[axis]), step)
            if test is not None:
                found = test if found is None else found & test
        return found

    def part(step, halo, count):
        if step == 0:
            return pl.ds(0, count), pl.ds(halo, count)
        if step > 0:
            return pl.ds(count - halo, halo), pl.ds(0, halo)
        return pl.ds(0, halo), pl.ds(count + halo, halo)

    steps_all = [
        (dx, dy, dz)
        for dz in (-1, 1, 0)
        for dx in (-1, 0, 1)
        for dy in (-1, 0, 1)
        if (dx, dy, dz) != (0, 0, 0)
    ]

    def copy_of(k, steps):
        dx, dy, dz = steps
        if dz == 0:
            fx, tx = part(dx, hx, planes)
            fy, ty = part(dy, ht, tiles)
            src, dst = a_ref.at[fx, fy], p_ref.at[tx, ty]
        elif dz > 0:
            src, dst = e_ref.at[1], el_ref.at[1 - dx, 1 - dy]
        else:
            src, dst = e_ref.at[0], er_ref.at[1 - dx, 1 - dy]
        return pltpu.make_async_remote_copy(
            src_ref=src,
            dst_ref=dst,
            send_sem=send_sem.at[k],
            recv_sem=recv_sem.at[k],
            device_id=(me[0] + dx, me[1] + dy, me[2] + dz),
            device_id_type=MESH,
        )

    barrier = pltpu.get_barrier_semaphore()
    total = 1
    for axis in range(3):
        low = jnp.where(me[axis] > 0, 1, 0)
        high = jnp.where(me[axis] < sizes[axis] - 1, 1, 0)
        total = total * (1 + low + high)
    for steps in steps_all:

        @pl.when(valid(steps))
        def _():
            pl.semaphore_signal(
                barrier,
                inc=1,
                device_id=tuple(me[axis] + steps[axis] for axis in range(3)),
                device_id_type=MESH,
            )

    pl.semaphore_wait(barrier, total - 1)

    for k, steps in enumerate(steps_all):

        @pl.when(valid(steps))
        def _():
            copy_of(k, steps).start()

    p_ref[pl.ds(hx, planes), pl.ds(ht, tiles)] = a_ref[...]
    for k, steps in enumerate(steps_all):
        back = tuple(-step for step in steps)
        dx, dy, dz = steps

        @pl.when(jnp.logical_not(valid(back)))
        def _():
            if dz == 0:
                _, tx = part(dx, hx, planes)
                _, ty = part(dy, ht, tiles)
                into = p_ref.at[tx, ty]
            elif dz > 0:
                into = el_ref.at[1 - dx, 1 - dy]
            else:
                into = er_ref.at[1 - dx, 1 - dy]
            into[...] = jnp.zeros(into.shape, into.dtype)

    for k, steps in enumerate(steps_all):
        back = tuple(-step for step in steps)

        @pl.when(valid(back))
        def _():
            copy_of(k, steps).wait_recv()

    for k, steps in enumerate(steps_all):

        @pl.when(valid(steps))
        def _():
            copy_of(k, steps).wait_send()


def plane_peers(nx, nz):
    return [(ox, oz) for ox in range(nx) for oz in range(nz) if (ox, oz) != (0, 0)]


def greet(peers):
    barrier = pltpu.get_barrier_semaphore()
    for peer in peers:
        pl.semaphore_signal(barrier, inc=1, device_id=peer, device_id_type=MESH)
    pl.semaphore_wait(barrier, len(peers))


def gather_kernel(sizes, g_ref, all_ref, stage, send_a, recv_a, send_b, recv_b):
    nx, ny, nz = sizes
    gx, gy, gz = [lax.axis_index(name) for name in ("gx", "gy", "gz")]
    plane = plane_peers(nx, nz)
    greet(
        [(lax.rem(gx + ox, nx), gy, lax.rem(gz + oz, nz)) for ox, oz in plane]
        + [(gx, lax.rem(gy + oy, ny), gz) for oy in range(1, ny)]
    )

    def first(k, x, z, peer):
        return pltpu.make_async_remote_copy(
            src_ref=g_ref,
            dst_ref=stage.at[x, pl.ds(pl.multiple_of(z * 8, 8), 8)],
            send_sem=send_a.at[k],
            recv_sem=recv_a.at[k],
            device_id=peer,
            device_id_type=MESH,
        )

    def second(oy, y):
        return pltpu.make_async_remote_copy(
            src_ref=all_ref.at[gy],
            dst_ref=all_ref.at[y],
            send_sem=send_b.at[oy],
            recv_sem=recv_b.at[oy],
            device_id=(gx, lax.rem(gy + oy, ny), gz),
            device_id_type=MESH,
        )

    for k, (ox, oz) in enumerate(plane):
        first(k, gx, gz, (lax.rem(gx + ox, nx), gy, lax.rem(gz + oz, nz))).start()
    stage[gx, pl.ds(pl.multiple_of(gz * 8, 8), 8)] = g_ref[...]
    for k, (ox, oz) in enumerate(plane):
        peer = (lax.rem(gx + ox, nx), gy, lax.rem(gz + oz, nz))
        first(k, lax.rem(gx + nx - ox, nx), lax.rem(gz + nz - oz, nz), peer).wait_recv()
    all_ref[gy] = stage[...].astype(BF)
    for oy in range(1, ny):
        second(oy, gy).start()
    for k, (ox, oz) in enumerate(plane):
        first(k, gx, gz, (lax.rem(gx + ox, nx), gy, lax.rem(gz + oz, nz))).wait_send()
    for oy in range(1, ny):
        second(oy, lax.rem(gy + ny - oy, ny)).wait_recv()
    for oy in range(1, ny):
        second(oy, gy).wait_send()


def reduce_kernel(sizes, pay_ref, out_ref, ra, rb, send_a, recv_a, send_b, recv_b, send_c, recv_c):
    nx, ny, nz = sizes
    gx, gy, gz = [lax.axis_index(name) for name in ("gx", "gy", "gz")]
    mine = gx * nz + gz
    plane = plane_peers(nx, nz)
    greet(
        [(lax.rem(gx + ox, nx), gy, lax.rem(gz + oz, nz)) for ox, oz in plane]
        + [(gx, lax.rem(gy + oy, ny), gz) for oy in range(1, ny)]
    )

    def ahead(ox, oz):
        return lax.rem(gx + ox, nx), lax.rem(gz + oz, nz)

    def behind(ox, oz):
        return lax.rem(gx + nx - ox, nx), lax.rem(gz + nz - oz, nz)

    def scatter(k, ox, oz, slot):
        x, z = ahead(ox, oz)
        return pltpu.make_async_remote_copy(
            src_ref=pay_ref.at[x * nz + z],
            dst_ref=ra.at[slot],
            send_sem=send_a.at[k],
            recv_sem=recv_a.at[k],
            device_id=(x, gy, z),
            device_id_type=MESH,
        )

    def across(oy, slot):
        return pltpu.make_async_remote_copy(
            src_ref=rb.at[gy],
            dst_ref=rb.at[slot],
            send_sem=send_b.at[oy],
            recv_sem=recv_b.at[oy],
            device_id=(gx, lax.rem(gy + oy, ny), gz),
            device_id_type=MESH,
        )

    def spread(k, ox, oz, slot):
        x, z = ahead(ox, oz)
        return pltpu.make_async_remote_copy(
            src_ref=out_ref.at[mine],
            dst_ref=out_ref.at[slot],
            send_sem=send_c.at[k],
            recv_sem=recv_c.at[k],
            device_id=(x, gy, z),
            device_id_type=MESH,
        )

    for k, (ox, oz) in enumerate(plane):
        scatter(k, ox, oz, mine).start()
    ra[mine] = pay_ref[mine]
    for k, (ox, oz) in enumerate(plane):
        x, z = behind(ox, oz)
        scatter(k, ox, oz, x * nz + z).wait_recv()
    rb[gy] = jnp.sum(ra[...], axis=0)
    for oy in range(1, ny):
        across(oy, gy).start()
    for k, (ox, oz) in enumerate(plane):
        scatter(k, ox, oz, mine).wait_send()
    for oy in range(1, ny):
        across(oy, lax.rem(gy + ny - oy, ny)).wait_recv()
    out_ref[mine] = jnp.sum(rb[...], axis=0)
    for k, (ox, oz) in enumerate(plane):
        spread(k, ox, oz, mine).start()
    for oy in range(1, ny):
        across(oy, gy).wait_send()
    for k, (ox, oz) in enumerate(plane):
        x, z = behind(ox, oz)
        spread(k, ox, oz, x * nz + z).wait_recv()
    for k, (ox, oz) in enumerate(plane):
        spread(k, ox, oz, mine).wait_send()


def fine_kernel(
    p_ref, er_ref, el_ref, cot_ref, wf_ref, pre_ref, act_ref, mg_ref, e_ref, v3_ref, ct_ref, sums
):
    lane = lane_of(16)

    def rows(x, _):
        dx, sx = (x + 7) // 8, lax.rem(x + 7, 8)
        for y in range(18):
            dy, sy = (y + 15) // 16, (y + 15) % 16
            base = turn(p_ref[x, (y + 1) // 2].astype(F32), 64 * ((y + 1) % 2))
            at = sx * 16 + sy
            right = turn(er_ref[dx, dy].astype(F32), 64 - at)
            left = turn(el_ref[dx, dy].astype(F32), 127 - at)
            edge = jnp.where(lane == 64, right, jnp.where(lane == 127, left, 0.0))
            store_taps(v3_ref, (x, y), jnp.where(lane < 64, base, edge), 16)
        return 0

    lax.fori_loop(0, 10, rows, 0)
    sums[...] = pool_matrix()
    weight = wf_ref[...]

    def conv(x, _):
        for t, tile in enumerate(plane_rows(cot_ref[:, x])):
            ct_ref[x, t] = tile
        for t in range(8):
            one, two = conv_pair(weight, v3_ref, x, 2 * t)
            pre = jnp.where(lane < 64, one, turn(two, 64))
            pre_ref[x, t] = pre
            act_ref[x, t] = (pre * sigmoid(pre)).astype(BF)
        return 0

    lax.fori_loop(0, 8, conv, 0)

    lane = lane_of(32)

    def pools(x, edges):
        low, high = edges
        for half in range(2):
            parts = []
            for ref, factor in ((act_ref, 0.125), (ct_ref, 1.0)):
                cells = jnp.concatenate(
                    [ref[2 * x + a, 4 * half + q] for q in range(4) for a in range(2)], axis=1
                )
                parts.append((dot(cells, sums[...]) * factor).astype(BF))
            tile = jnp.concatenate(parts, axis=0)
            mg_ref[x, half] = tile
            wide = tile.astype(F32)
            for q in range(4):
                at = (x * 8 + half * 4 + q) * 4
                here = (lane >= at) & (lane < at + 4)
                low = jnp.where(here, turn(wide, at - 32 * q), low)
                high = jnp.where(here, turn(wide, at - 32 * q - 28), high)
        return low, high

    zero = jnp.zeros((32, LANES), F32)
    low, high = lax.fori_loop(0, 4, pools, (zero, zero))
    e_ref[0] = low.astype(BF)
    e_ref[1] = high.astype(BF)


def mid_kernel(
    sizes, p_ref, er_ref, el_ref, wd_ref, am_ref, dsm_ref, pm3n_ref, pgr_ref, pc_ref, pm3, pgf, dsf
):
    gx, gy, gz = [lax.axis_index(name) for name in ("gx", "gy", "gz")]
    nx, ny, nz = sizes
    lane = lane_of(32)

    def rows(x, _):
        dx, sx = x // 4, lax.rem(x, 4)
        for y in range(16):
            dy, sy = (y + 4) // 8, (y + 4) % 8
            base = turn(p_ref[x, y // 4].astype(F32), -32 * (y % 4))
            at = (sx * 8 + sy) * 4
            right = turn(er_ref[dx, dy].astype(F32), 32 - at)
            left = turn(el_ref[dx, dy].astype(F32), 124 - at)
            edge = jnp.where(lane < 36, right, jnp.where(lane >= 124, left, 0.0))
            row = jnp.where(lane < 32, base, edge)
            store_taps(pm3, (x, y), row[:16], 16)
            pgf[x, y] = row[16:].astype(BF)
        return 0

    lax.fori_loop(0, 12, rows, 0)
    weight = wd_ref[...]
    cell = jnp.where(lane < 64, lane, lane - LANES)
    mid = cell + gz * 32
    inside = (cell >= -3) & (cell < 35) & (mid >= 0) & (mid < 32 * nz)

    def conv(x, _):
        at_x = gx * 4 + x - 3
        for y in range(0, 14, 2):
            for b, pre in enumerate(conv_pair(weight, pm3, x, y)):
                at_y = gy * 8 + y + b - 3
                there = (at_x >= 0) & (at_x < 4 * nx) & (at_y >= 0) & (at_y < 8 * ny)
                keep = inside & there
                sig = sigmoid(pre)
                am_ref[x, y + b] = jnp.where(keep, pre * sig, 0.0).astype(BF)
                dsf[x, y + b] = jnp.where(keep, slope(pre, sig), 0.0).astype(BF)
        return 0

    lax.fori_loop(0, 10, conv, 0)
    dsm_ref[...] = dsf[2:8, 2:12]
    pm3n_ref[...] = pm3[3:9, 3:13]
    pgr_ref[...] = pgf[2:10, 2:14]
    halves = [
        jnp.concatenate([am_ref[3 + a, 3 + 4 * h + b] for a in range(4) for b in range(4)], axis=1)
        for h in range(2)
    ]
    cells = jnp.concatenate(halves + [jnp.zeros((64, 16 * LANES), BF)], axis=0)
    pooled = dot_nt(coarse_sum_matrix(16), cells) * (1.0 / 64.0)
    pc_ref[...] = pooled.astype(BF).astype(F32)


def place_weight(ref, weight):
    for y2 in range(2):
        ref[y2] = jnp.zeros((LANES, 256), BF)
        ref[y2, pl.ds(32 * y2, 32)] = weight


def store_coarse_taps(ref, at, cells):
    count = cells.shape[0]
    row = lax.broadcasted_iota(jnp.int32, cells.shape, 0)
    before = jnp.where(row > 0, pltpu.roll(cells, 1, 0), 0.0)
    after = jnp.where(row < count - 1, pltpu.roll(cells, count - 1, 0), 0.0)
    ref[at + (slice(None), pl.ds(0, 256))] = before.astype(BF)
    ref[at + (slice(None), pl.ds(256, 256))] = cells.astype(BF)
    ref[at + (slice(None), pl.ds(512, 256))] = after.astype(BF)


def zero_rim(ref, rim):
    planes, rows = ref.shape[:2]

    def clear(x, _):
        for y in list(range(rim)) + list(range(rows - rim, rows)):
            ref[x, y] = jnp.zeros(ref.shape[2:], ref.dtype)
        return 0

    lax.fori_loop(0, planes, clear, 0)

    def clear_plane(y, _):
        for x in list(range(rim)) + list(range(planes - rim, planes)):
            ref[x, y] = jnp.zeros(ref.shape[2:], ref.dtype)
        return 0

    lax.fori_loop(0, rows, clear_plane, 0)


def clamp(at, count):
    return jnp.minimum(jnp.maximum(at, 0), count - 1)


def near_cells(sizes):
    nx, ny, _ = sizes
    gx, gy = lax.axis_index("gx"), lax.axis_index("gy")
    found = []
    for dx in range(3):
        for dy in range(4):
            x, y = gx - 1 + dx, gy + (dy + 1) // 2 - 1
            there = (x >= 0) & (x < nx) & (y >= 0) & (y < ny)
            keep = jnp.where(there, 1.0, 0.0)
            found.append((dx, dy, clamp(x, nx), clamp(y, ny), (dy + 1) % 2, keep))
    return found


def up_kernel(
    sizes,
    scale,
    pcg_ref,
    am_ref,
    act_ref,
    pgr_ref,
    wl_ref,
    wc_ref,
    wp_ref,
    wu_ref,
    wut_ref,
    dec_ref,
    gj_ref,
    gwu_ref,
    gc_ref,
    dsc_ref,
    actc_ref,
    alc_ref,
    wide_lift,
    al3,
    acc,
    cos,
    j3,
    gu3,
    su,
    plane,
):
    nx, ny, nz = sizes
    gz = lax.axis_index("gz")
    cells = 8 * nz
    place_weight(wide_lift, wl_ref[...])
    zero_rim(al3, 1)

    def lift(y, _):
        for x in range(nx):
            for y2 in range(2):
                pre = dot(pcg_ref[y, x], wide_lift[y2])
                act = (pre * sigmoid(pre)).astype(BF)
                alc_ref[x, y, y2] = act
                store_coarse_taps(al3, (x + 1, 2 * y + y2 + 1), act.astype(F32))
        return 0

    lax.fori_loop(0, ny, lift, 0)

    def coarse(x, _):
        for i in range(3):
            for j in range(3):
                block = al3[x + i, pl.ds(j, 2 * ny)].reshape(2 * ny * cells, 768)
                part = dot(block, wc_ref[3 * i + j])
                if i + j == 0:
                    acc[...] = part
                else:
                    acc[...] += part
        pre = acc[...]
        sig = sigmoid(pre)
        shape = (ny, 2, cells, 256)
        actc_ref[x] = (pre * sig).astype(BF).reshape(shape)
        dsc_ref[x] = slope(pre, sig).astype(BF).reshape(shape)
        return 0

    lax.fori_loop(0, nx, coarse, 0)

    spread = coarse_grow_matrix(cells, gz)
    for dx, dy, x, y, y2, keep in near_cells(sizes):
        out = dot_nt(wp_ref[...], actc_ref[x, y, y2]).astype(BF)
        cos[dx, dy] = dot(out, spread) * keep

    def join(x, _):
        for y in range(14):
            row = am_ref[x, y].astype(F32) + cos[(x + 1) // 4, (y + 1) // 4]
            store_taps(j3, (x, y), row.astype(BF).astype(F32), 32)
        return 0

    lax.fori_loop(0, 10, join, 0)

    lane = lane_of(16)
    near = (lane < 34) | (lane >= 126)
    weight = wu_ref[...]

    def up(x, _):
        for y in range(0, 12, 2):
            for b, pre in enumerate(conv_pair(weight, j3, x, y)):
                sig = sigmoid(pre)
                su[x, y + b] = (pre * sig).astype(BF)
                pooled = pgr_ref[x, y + b].astype(F32) * scale
                grad = jnp.where(near, pooled * slope(pre, sig), 0.0)
                store_taps(gu3, (x, y + b), grad.astype(BF).astype(F32), 16)
        return 0

    lax.fori_loop(0, 8, up, 0)

    weight_t = wut_ref[...]

    def back(x, _):
        for y in range(0, 10, 2):
            for b, grad in enumerate(conv_pair(weight_t, gu3, x, y)):
                gj_ref[x, y + b] = grad
        return 0

    lax.fori_loop(0, 6, back, 0)

    sums = coarse_sum_matrix(1)
    halves = []
    for h in range(2):
        total = None
        for a in range(4):
            for b in range(4):
                row = gj_ref[1 + a, 1 + 4 * h + b]
                total = row if total is None else total + row
        halves.append(total)
    total = jnp.concatenate(halves + [jnp.zeros((64, LANES), F32)], axis=0)
    head = total.astype(BF)
    tail = (total - head.astype(F32)).astype(BF)
    gc_ref[...] = (dot_nt(sums, head) + dot_nt(sums, tail)).astype(BF).astype(F32)

    gwu_ref[...] = jnp.zeros(gwu_ref.shape, F32)

    def taps(x, _):
        grads, cells_near = [], []
        for y in range(8):
            grads.append(jnp.where(lane < 32, gu3[x + 2, y + 2, pl.ds(16, 16)].astype(F32), 0.0))
            cells_near.append(around(j3, x + 2, y + 2))
        grad = jnp.concatenate(grads, axis=1).astype(BF)
        gwu_ref[:, pl.ds(0, 864)] += dot_nt(grad, jnp.concatenate(cells_near, axis=1))
        return 0

    lax.fori_loop(0, 4, taps, 0)

    grow = grow_matrix()

    def decode(x, _):
        for a in range(2):
            for half in range(2):
                rows = [su[x + 2, 4 * half + q + 2].astype(F32) for q in range(4)]
                grown = dot(pack_four(rows).astype(BF), grow)
                for q in range(4):
                    t = 4 * half + q
                    tile = act_ref[2 * x + a, t].astype(F32) + grown[:, q * LANES : (q + 1) * LANES]
                    plane[2 * t] = tile.astype(BF)
                    plane[2 * t + 1] = turn(tile, 64).astype(BF)
            dec_ref[:, 2 * x + a] = jnp.swapaxes(plane[...], 0, 1)[:, :, :64]
        return 0

    lax.fori_loop(0, 4, decode, 0)


def back_kernel(
    sizes,
    scale,
    gcg_ref,
    pcg_ref,
    dsc_ref,
    actc_ref,
    gj_ref,
    dsm_ref,
    pm3n_ref,
    ct_ref,
    pre_ref,
    v3_ref,
    gwu_ref,
    wl_ref,
    wc_ref,
    wp_ref,
    wdt_ref,
    pay_ref,
    gpc_ref,
    gwp_ref,
    wide_lift,
    wide_proj,
    gp3,
    acc,
    gps,
    gm3,
    gpm,
    gf,
    accf,
    accd,
    sums,
):
    nx, ny, nz = sizes
    gx, gy, gz = [lax.axis_index(name) for name in ("gx", "gy", "gz")]
    cells = 8 * nz
    place_weight(wide_lift, wl_ref[...])
    place_weight(wide_proj, wp_ref[...])
    zero_rim(gp3, 2)

    def coarse(y, _):
        for x in range(nx):
            for y2 in range(2):
                grad = dot(gcg_ref[y, x], wide_proj[y2]) * dsc_ref[x, y, y2].astype(F32)
                grad = grad.astype(BF)
                gpc_ref[x, y, y2] = grad
                store_coarse_taps(gp3, (x + 2, 2 * y + y2 + 2), grad.astype(F32))
        return 0

    lax.fori_loop(0, ny, coarse, 0)

    sums[...] = jnp.zeros(sums.shape, F32)

    def proj_grad(x, _):
        for y2 in range(2):
            grads = gcg_ref[:, x].reshape(ny * cells, LANES)
            sums[y2] += dot_tn(grads, actc_ref[x, :, y2].reshape(ny * cells, 256))
        return 0

    lax.fori_loop(0, nx, proj_grad, 0)
    gwp_ref[...] = sums[0, :32] + sums[1, 32:64]

    acc[...] = jnp.zeros(acc.shape, F32)

    def coarse_back(i, _):
        for j in range(3):
            block = gp3[pl.ds(gx + i, 3), pl.ds(2 * gy + j, 4)].reshape(12 * cells, 768)
            for k in range(3):
                weight = wc_ref[8 - 3 * i - j, pl.ds(256 * (2 - k), 256)]
                acc[...] += dot_nt(block[:, 256 * k : 256 * (k + 1)], weight)
        return 0

    lax.fori_loop(0, 3, coarse_back, 0)

    spread = coarse_grow_matrix(cells, gz)
    own = lax.broadcasted_iota(jnp.int32, (cells, 256), 0) // 8 == gz
    for at, (dx, dy, x, y, y2, keep) in enumerate(near_cells(sizes)):
        pre = dot(pcg_ref[y, x], wide_lift[y2])
        grad = (acc[pl.ds(at * cells, cells)] * slope(pre, sigmoid(pre))).astype(BF)
        out = dot_nt(wl_ref[...], grad).astype(BF)
        gps[dx, dy] = dot(out, spread) * (keep * (1.0 / 64.0))
        if dx == 1 and dy in (1, 2):
            masked = jnp.where(own, grad.astype(F32), 0.0).astype(BF)
            sums[y2] = dot_tn(pcg_ref[y, x], masked)

    def join(x, _):
        for y in range(10):
            row = gj_ref[x, y] + gps[(x + 3) // 4, (y + 3) // 4]
            row = row * dsm_ref[x, y].astype(F32)
            store_taps(gm3, (x, y), row.astype(BF).astype(F32), 32)
        return 0

    lax.fori_loop(0, 6, join, 0)

    weight_t = wdt_ref[...]

    def back(x, _):
        rows = []
        for y in range(0, 8, 2):
            rows.extend(conv_pair(weight_t, gm3, x, y))
        for half in range(2):
            gpm[x, half] = pack_four(rows[4 * half : 4 * half + 4]).astype(BF)
        return 0

    lax.fori_loop(0, 4, back, 0)

    grow = grow_matrix()

    def fine(x, _):
        for half in range(2):
            grown = dot(gpm[x, half], grow) * 0.125
            for a in range(2):
                for q in range(4):
                    t = 4 * half + q
                    pre = pre_ref[2 * x + a, t]
                    grad = ct_ref[2 * x + a, t].astype(F32) * scale
                    grad = grad + grown[:, q * LANES : (q + 1) * LANES]
                    gf[2 * x + a, t] = (grad * slope(pre, sigmoid(pre))).astype(BF)
        return 0

    lax.fori_loop(0, 4, fine, 0)

    accd[...] = jnp.zeros(accd.shape, F32)
    lane = lane_of(32)

    def taps_down(x, _):
        grads, cells_near = [], []
        for y in range(8):
            grads.append(jnp.where(lane < 32, gm3[x + 1, y + 1, pl.ds(32, 32)].astype(F32), 0.0))
            cells_near.append(around(pm3n_ref, x, y))
        grad = jnp.concatenate(grads, axis=1).astype(BF)
        accd[:, pl.ds(0, 432)] += dot_nt(grad, jnp.concatenate(cells_near, axis=1))
        return 0

    lax.fori_loop(0, 4, taps_down, 0)

    accf[...] = jnp.zeros(accf.shape, F32)
    lane16 = lane_of(16)

    def taps_fine(x, _):
        for half in range(2):
            grads, cells_near = [], []
            for t in range(4 * half, 4 * half + 4):
                tile = gf[x, t].astype(F32)
                for b in range(2):
                    grads.append(jnp.where(lane16 < 64, turn(tile, 64 * b), 0.0))
                    cells_near.append(around(v3_ref, x, 2 * t + b))
            grad = jnp.concatenate(grads, axis=1).astype(BF)
            accf[:, pl.ds(0, 432)] += dot_nt(grad, jnp.concatenate(cells_near, axis=1))
        return 0

    lax.fori_loop(0, 8, taps_fine, 0)

    for b in range(4):
        pay_ref[pl.ds(16 * b, 16)] = accf[:, b * LANES : (b + 1) * LANES]
    for b in range(7):
        pay_ref[pl.ds(64 + 16 * b, 16)] = gwu_ref[:, b * LANES : (b + 1) * LANES]
    for b in range(4):
        pay_ref[pl.ds(176 + 32 * b, 32)] = accd[:, b * LANES : (b + 1) * LANES]
    lifts = sums[0, :32] + sums[1, 32:64]
    for b in range(2):
        pay_ref[pl.ds(304 + 32 * b, 32)] = lifts[:, b * LANES : (b + 1) * LANES]
    pay_ref[pl.ds(368, 16)] = jnp.zeros((16, LANES), F32)


def last_kernel(
    sizes,
    gpc_ref,
    alc_ref,
    red_ref,
    gwp_ref,
    wc_out,
    wf_out,
    wd_out,
    wl_out,
    wp_out,
    wu_out,
    cells_t,
    gs,
):
    nx, ny, nz = sizes
    cells = 8 * nz
    count = nx * ny * 2 * cells
    step = pl.program_id(0)

    @pl.when(step == 0)
    def _():
        def columns(start, blocks, rows):
            return jnp.concatenate(
                [red_ref[pl.ds(start + rows * b, rows)] for b in range(blocks)], axis=1
            )

        wf_out[...] = columns(0, 4, 16)[:, :432].T.reshape(27, 16, 16)
        wu_out[...] = columns(64, 7, 16)[:, :864].T.reshape(27, 32, 16)
        wd_out[...] = columns(176, 4, 32)[:, :432].T.reshape(27, 16, 32)
        wl_out[...] = columns(304, 2, 32)
        wp_out[...] = gwp_ref[...].T
        cells_t[...] = alc_ref[...].reshape(count, 256).T
        for k in range(3):
            zero_rim(gs.at[k], 1)

        def shift(y, _):
            row = lax.broadcasted_iota(jnp.int32, (cells, 256), 0)
            for x in range(nx):
                for y2 in range(2):
                    at = (x + 1, 2 * y + y2 + 1)
                    grad = gpc_ref[x, y, y2].astype(F32)
                    after = jnp.where(row < cells - 1, pltpu.roll(grad, cells - 1, 0), 0.0)
                    before = jnp.where(row > 0, pltpu.roll(grad, 1, 0), 0.0)
                    gs[(0,) + at] = after.astype(BF)
                    gs[(1,) + at] = grad.astype(BF)
                    gs[(2,) + at] = before.astype(BF)
            return 0

        lax.fori_loop(0, ny, shift, 0)

    i, j, k = step // 9, lax.rem(step // 3, 3), lax.rem(step, 3)
    block = gs[k, pl.ds(2 - i, nx), pl.ds(2 - j, 2 * ny)].reshape(count, 256)
    wc_out[0] = dot(cells_t[...], block)


VMEM = pl.BlockSpec(memory_space=pltpu.VMEM)


def call(kernel, outs, args, scratch=(), collective=None):
    params = dict(vmem_limit_bytes=56 * 1024 * 1024)
    if collective is not None:
        params.update(collective_id=collective, has_side_effects=True)
    return pl.pallas_call(
        kernel,
        out_shape=[jax.ShapeDtypeStruct(shape, kind) for shape, kind in outs],
        in_specs=[VMEM] * len(args),
        out_specs=[VMEM] * len(outs),
        scratch_shapes=list(scratch),
        compiler_params=pltpu.CompilerParams(**params),
    )(*args)


def dma(count):
    return pltpu.SemaphoreType.DMA((count,))


def exchange(sizes, cells, edges, hx, ht, collective):
    planes, tiles, chans, _ = cells.shape
    return call(
        functools.partial(halo_kernel, sizes, hx, ht),
        [
            ((planes + 2 * hx, tiles + 2 * ht, chans, LANES), BF),
            ((3, 3, chans, LANES), BF),
            ((3, 3, chans, LANES), BF),
        ],
        [cells, edges],
        [dma(26), dma(26)],
        collective,
    )


def gather(sizes, cells, collective):
    nx, ny, nz = sizes
    return call(
        functools.partial(gather_kernel, sizes),
        [((ny, nx, 8 * nz, LANES), BF)],
        [cells],
        [pltpu.VMEM((nx, 8 * nz, LANES), F32), dma(nx * nz), dma(nx * nz), dma(ny), dma(ny)],
        collective,
    )[0]


def reduce_all(sizes, pay, collective):
    nx, ny, nz = sizes
    parts = nx * nz
    rows = pay.shape[0] // parts
    out = call(
        functools.partial(reduce_kernel, sizes),
        [((parts, rows, LANES), F32)],
        [pay.reshape(parts, rows, LANES)],
        [
            pltpu.VMEM((parts, rows, LANES), F32),
            pltpu.VMEM((ny, rows, LANES), F32),
            dma(parts),
            dma(parts),
            dma(ny),
            dma(ny),
            dma(parts),
            dma(parts),
        ],
        collective,
    )[0]
    return out.reshape(pay.shape)


def shards(sizes, volume, w_fine, w_down, w_lift, w_coarse, w_proj, w_up, cotangent):
    nx, ny, nz = sizes
    total = 8 * nx * 16 * ny * 64 * nz
    scale = 1.0 / math.sqrt(total)
    cells = 8 * nz
    wf = jnp.transpose(w_fine, (2, 0, 1)).reshape(16, 432)
    wd = jnp.transpose(w_down, (2, 0, 1)).reshape(32, 432)
    wu = jnp.transpose(w_up, (2, 0, 1)).reshape(16, 864)
    wdt = jnp.transpose(jnp.flip(w_down, 0), (1, 0, 2)).reshape(16, 864)
    wut = jnp.transpose(jnp.flip(w_up, 0), (1, 0, 2)).reshape(32, 432)
    wp = jnp.transpose(w_proj)
    wc = w_coarse.reshape(9, 768, 256)

    rows, edges = call(arrange_kernel, [((8, 8, 16, LANES), BF), ((2, 16, LANES), BF)], [volume])
    padded, right, left = exchange(sizes, rows, edges, 1, 1, 1)
    pre, act, mg, edges, v3, ct = call(
        fine_kernel,
        [
            ((8, 8, 16, LANES), F32),
            ((8, 8, 16, LANES), BF),
            ((4, 2, 32, LANES), BF),
            ((2, 32, LANES), BF),
            ((10, 18, 48, LANES), BF),
            ((8, 8, 16, LANES), BF),
        ],
        [padded, right, left, cotangent, wf],
        [pltpu.VMEM((8 * LANES, LANES), BF)],
    )
    padded, right, left = exchange(sizes, mg, edges, 4, 1, 2)
    am, dsm, pm3n, pgr, pc = call(
        functools.partial(mid_kernel, sizes),
        [
            ((10, 14, 32, LANES), BF),
            ((6, 10, 32, LANES), BF),
            ((6, 10, 48, LANES), BF),
            ((8, 12, 16, LANES), BF),
            ((8, LANES), F32),
        ],
        [padded, right, left, wd],
        [
            pltpu.VMEM((12, 16, 48, LANES), BF),
            pltpu.VMEM((12, 16, 16, LANES), BF),
            pltpu.VMEM((10, 14, 32, LANES), BF),
        ],
    )
    pcg = gather(sizes, pc, 3)
    grid = (nx, ny, 2, cells, 256)
    dec, gj, gwu, gc, dsc, actc, alc = call(
        functools.partial(up_kernel, sizes, scale),
        [
            ((16, 8, 16, 64), BF),
            ((6, 10, 32, LANES), F32),
            ((16, 896), F32),
            ((8, LANES), F32),
            (grid, BF),
            (grid, BF),
            (grid, BF),
        ],
        [pcg, am, act, pgr, w_lift, wc, wp, wu, wut],
        [
            pltpu.VMEM((2, LANES, 256), BF),
            pltpu.VMEM((nx + 2, 2 * ny + 2, cells, 768), BF),
            pltpu.VMEM((2 * ny * cells, 256), F32),
            pltpu.VMEM((3, 4, 32, LANES), F32),
            pltpu.VMEM((10, 14, 96, LANES), BF),
            pltpu.VMEM((8, 12, 48, LANES), BF),
            pltpu.VMEM((8, 12, 16, LANES), BF),
            pltpu.VMEM((16, 16, LANES), BF),
        ],
    )
    gcg = gather(sizes, gc, 4)
    pay, gpc, gwp = call(
        functools.partial(back_kernel, sizes, scale),
        [((384, LANES), F32), (grid, BF), ((32, 256), F32)],
        [gcg, pcg, dsc, actc, gj, dsm, pm3n, ct, pre, v3, gwu, w_lift, wc, wp, wdt],
        [
            pltpu.VMEM((2, LANES, 256), BF),
            pltpu.VMEM((2, LANES, 256), BF),
            pltpu.VMEM((nx + 4, 2 * ny + 4, cells, 768), BF),
            pltpu.VMEM((12 * cells, 256), F32),
            pltpu.VMEM((3, 4, 32, LANES), F32),
            pltpu.VMEM((6, 10, 96, LANES), BF),
            pltpu.VMEM((4, 2, 16, LANES), BF),
            pltpu.VMEM((8, 8, 16, LANES), BF),
            pltpu.VMEM((16, 512), F32),
            pltpu.VMEM((32, 512), F32),
            pltpu.VMEM((2, LANES, 256), F32),
        ],
    )
    red = reduce_all(sizes, pay, 5)
    shapes = [
        (27, 256, 256),
        (27, 16, 16),
        (27, 16, 32),
        (32, 256),
        (256, 32),
        (27, 32, 16),
    ]
    specs = [pl.BlockSpec((1, 256, 256), lambda t: (t, 0, 0))] + [
        pl.BlockSpec(shape, functools.partial(lambda n, t: (0,) * n, len(shape)))
        for shape in shapes[1:]
    ]
    ins = [gpc, alc, red, gwp]
    gwc, gwf, gwd, gwl, gwp, gwu = pl.pallas_call(
        functools.partial(last_kernel, sizes),
        grid=(27,),
        out_shape=[jax.ShapeDtypeStruct(shape, F32) for shape in shapes],
        in_specs=[
            pl.BlockSpec(arg.shape, functools.partial(lambda n, t: (0,) * n, arg.ndim)) for arg in ins
        ],
        out_specs=specs,
        scratch_shapes=[
            pltpu.VMEM((256, nx * ny * 2 * cells), BF),
            pltpu.VMEM((3, nx + 2, 2 * ny + 2, cells, 256), BF),
        ],
        compiler_params=pltpu.CompilerParams(
            vmem_limit_bytes=56 * 1024 * 1024, dimension_semantics=("arbitrary",)
        ),
    )(*ins)
    return dec, gwf, gwd, gwl, gwc, gwp, gwu


def solution(mesh):
    sizes = tuple(mesh.shape[name] for name in ("gx", "gy", "gz"))
    block = P(None, "gx", "gy", "gz")
    return jax.shard_map(
        functools.partial(shards, sizes),
        mesh=mesh,
        in_specs=(block, P(), P(), P(), P(), P(), P(), block),
        out_specs=(block, P(), P(), P(), P(), P(), P()),
        check_vma=False,
    )
```

```python
import functools
import math

import jax
import jax.numpy as jnp
from jax import lax
from jax.experimental import pallas as pl
from jax.experimental.pallas import tpu as pltpu
from jax.sharding import PartitionSpec as P

BF = jnp.bfloat16
F32 = jnp.float32
MESH = pl.DeviceIdType.MESH
LANES = 128


def dot(left, right):
    return jnp.dot(left, right, preferred_element_type=F32)


def dot_nt(left, right):
    return lax.dot_general(left, right, (((1,), (1,)), ((), ())), preferred_element_type=F32)


def dot_tn(left, right):
    return lax.dot_general(left, right, (((0,), (0,)), ((), ())), preferred_element_type=F32)


def sigmoid(values):
    return 0.5 * jnp.tanh(0.5 * values) + 0.5


def slope(values, sig):
    return sig * (1.0 + values * (1.0 - sig))


def lane_of(rows):
    return lax.broadcasted_iota(jnp.int32, (rows, LANES), 1)


def turn(tile, by):
    if isinstance(by, int):
        by = by % LANES
        return tile if by == 0 else pltpu.roll(tile, by, 1)
    return pltpu.roll(tile, lax.rem(by + 4 * LANES, LANES), 1)


def tap_rows(pair):
    return jnp.concatenate([turn(pair, 1), pair, turn(pair, -1)], axis=0)


def between(lower, upper):
    lane = lane_of(lower.shape[0])
    return jnp.where(lane < 64, turn(lower, 64), turn(upper, 64))


def store_taps(ref, x, pairs):
    stacks = [tap_rows(pair) for pair in pairs]
    for n, stack in enumerate(stacks):
        ref[x, 2 * n] = stack.astype(BF)
        if n + 1 < len(stacks):
            ref[x, 2 * n + 1] = between(stack, stacks[n + 1]).astype(BF)


def three(ref, x, y):
    block = ref[x, pl.ds(y, 3)]
    return block.reshape(3 * block.shape[1], LANES)


def conv(weight, ref, planes, starts):
    outs = weight.shape[0] // 3
    parts = []
    for x in range(planes + 2):
        tiles = [three(ref, x, y) for y in starts]
        block = tiles[0] if len(tiles) == 1 else jnp.concatenate(tiles, axis=1)
        parts.append(dot(weight, block))
        if x >= 2:
            yield (
                x - 2,
                parts[x - 2][:outs] + parts[x - 1][outs : 2 * outs] + parts[x][2 * outs :],
            )


def pool_matrix():
    row = lax.broadcasted_iota(jnp.int32, (8 * LANES, LANES), 0)
    col = lax.broadcasted_iota(jnp.int32, (8 * LANES, LANES), 1)
    hit = (row // 256 == col // 32) & (row % 64 // 2 == col % 32)
    return jnp.where(hit, 1.0, 0.0).astype(BF)


def pool_tile(ref, sums, x, half):
    cells = jnp.concatenate([ref[2 * x + a, 4 * half + q] for q in range(4) for a in range(2)], axis=1)
    return dot(cells, sums)


def grow_matrix():
    row = lax.broadcasted_iota(jnp.int32, (LANES, 2 * LANES), 0)
    col = lax.broadcasted_iota(jnp.int32, (LANES, 2 * LANES), 1)
    hit = (row // 64 == col // LANES) & (row % 64 - 8 == col % 64 // 2)
    return jnp.where(hit, 1.0, 0.0).astype(BF)


def coarse_sum_matrix(tiles):
    row = lax.broadcasted_iota(jnp.int32, (8, tiles * LANES), 0)
    cell = lax.broadcasted_iota(jnp.int32, (8, tiles * LANES), 1) % 64 - 8
    return (cell >= 0) & (cell < 32) & ((cell + 4) // 4 == row + 1)


def coarse_grow_matrix(cells, gz):
    row = lax.broadcasted_iota(jnp.int32, (cells, LANES), 0)
    cell = lax.broadcasted_iota(jnp.int32, (cells, LANES), 1) % 64 - 8
    mid = cell + gz * 32
    hit = (cell >= -3) & (cell < 35) & (mid >= 0) & (row == (mid + 4) // 4 - 1)
    return jnp.where(hit, 1.0, 0.0).astype(BF)


def plane_rows(block):
    rows = jnp.swapaxes(block, 0, 1)
    return [jnp.concatenate([rows[2 * t], rows[2 * t + 1]], axis=1) for t in range(8)]


def place_weight(ref, weight):
    for y2 in range(2):
        ref[y2] = jnp.zeros((LANES, 256), BF)
        ref[y2, pl.ds(32 * y2, 32)] = weight


def store_coarse_taps(ref, at, cells):
    count = cells.shape[0]
    row = lax.broadcasted_iota(jnp.int32, cells.shape, 0)
    before = jnp.where(row > 0, pltpu.roll(cells, 1, 0), 0.0)
    after = jnp.where(row < count - 1, pltpu.roll(cells, count - 1, 0), 0.0)
    ref[at + (slice(None), pl.ds(0, 256))] = before.astype(BF)
    ref[at + (slice(None), pl.ds(256, 256))] = cells.astype(BF)
    ref[at + (slice(None), pl.ds(512, 256))] = after.astype(BF)


def zero_rim(ref, rim):
    planes, rows = ref.shape[:2]

    def clear(x, _):
        for y in list(range(rim)) + list(range(rows - rim, rows)):
            ref[x, y] = jnp.zeros(ref.shape[2:], ref.dtype)
        return 0

    lax.fori_loop(0, planes, clear, 0)

    def clear_plane(y, _):
        for x in list(range(rim)) + list(range(planes - rim, planes)):
            ref[x, y] = jnp.zeros(ref.shape[2:], ref.dtype)
        return 0

    lax.fori_loop(0, rows, clear_plane, 0)


def clamp(at, count):
    return jnp.minimum(jnp.maximum(at, 0), count - 1)


def near_cells(sizes):
    nx, ny, _ = sizes
    gx, gy = lax.axis_index("gx"), lax.axis_index("gy")
    found = []
    for dx in range(3):
        for dy in range(4):
            x, y = gx - 1 + dx, gy + (dy + 1) // 2 - 1
            there = (x >= 0) & (x < nx) & (y >= 0) & (y < ny)
            keep = jnp.where(there, 1.0, 0.0)
            found.append((dx, dy, clamp(x, nx), clamp(y, ny), (dy + 1) % 2, keep))
    return found


def nothing():
    pass


def halo_round(sizes, hx, ht, refs, work, meanwhile):
    a_ref, e_ref, p_ref, er_ref, el_ref, send_sem, recv_sem = refs
    me = [lax.axis_index(name) for name in ("gx", "gy", "gz")]
    planes, tiles = a_ref.shape[:2]

    def there(at, step):
        if step == 0:
            return None
        return at[0] > 0 if step < 0 else at[0] < at[1] - 1

    def valid(steps):
        found = None
        for axis, step in enumerate(steps):
            test = there((me[axis], sizes[axis]), step)
            if test is not None:
                found = test if found is None else found & test
        return found

    def part(step, halo, count):
        if step == 0:
            return pl.ds(0, count), pl.ds(halo, count)
        if step > 0:
            return pl.ds(count - halo, halo), pl.ds(0, halo)
        return pl.ds(0, halo), pl.ds(count + halo, halo)

    steps_all = [
        (dx, dy, dz)
        for dz in (-1, 1, 0)
        for dx in (-1, 0, 1)
        for dy in (-1, 0, 1)
        if (dx, dy, dz) != (0, 0, 0)
    ]

    def copy_of(k, steps):
        dx, dy, dz = steps
        if dz == 0:
            fx, tx = part(dx, hx, planes)
            fy, ty = part(dy, ht, tiles)
            src, dst = a_ref.at[fx, fy], p_ref.at[tx, ty]
        elif dz > 0:
            src, dst = e_ref.at[1], el_ref.at[1 - dx, 1 - dy]
        else:
            src, dst = e_ref.at[0], er_ref.at[1 - dx, 1 - dy]
        return pltpu.make_async_remote_copy(
            src_ref=src,
            dst_ref=dst,
            send_sem=send_sem.at[k],
            recv_sem=recv_sem.at[k],
            device_id=(me[0] + dx, me[1] + dy, me[2] + dz),
            device_id_type=MESH,
        )

    barrier = pltpu.get_barrier_semaphore()
    total = 1
    for axis in range(3):
        low = jnp.where(me[axis] > 0, 1, 0)
        high = jnp.where(me[axis] < sizes[axis] - 1, 1, 0)
        total = total * (1 + low + high)
    for steps in steps_all:

        @pl.when(valid(steps))
        def _():
            pl.semaphore_signal(
                barrier,
                inc=1,
                device_id=tuple(me[axis] + steps[axis] for axis in range(3)),
                device_id_type=MESH,
            )

    work()
    pl.semaphore_wait(barrier, total - 1)

    for k, steps in enumerate(steps_all):

        @pl.when(valid(steps))
        def _():
            copy_of(k, steps).start()

    p_ref[pl.ds(hx, planes), pl.ds(ht, tiles)] = a_ref[...]
    for k, steps in enumerate(steps_all):
        back = tuple(-step for step in steps)
        dx, dy, dz = steps

        @pl.when(jnp.logical_not(valid(back)))
        def _():
            if dz == 0:
                _, tx = part(dx, hx, planes)
                _, ty = part(dy, ht, tiles)
                into = p_ref.at[tx, ty]
            elif dz > 0:
                into = el_ref.at[1 - dx, 1 - dy]
            else:
                into = er_ref.at[1 - dx, 1 - dy]
            into[...] = jnp.zeros(into.shape, into.dtype)

    meanwhile()
    for k, steps in enumerate(steps_all):
        back = tuple(-step for step in steps)

        @pl.when(valid(back))
        def _():
            copy_of(k, steps).wait_recv()

    for k, steps in enumerate(steps_all):

        @pl.when(valid(steps))
        def _():
            copy_of(k, steps).wait_send()


def plane_peers(nx, nz):
    return [(ox, oz) for ox in range(nx) for oz in range(nz) if (ox, oz) != (0, 0)]


def greet(peers, work):
    barrier = pltpu.get_barrier_semaphore()
    for peer in peers:
        pl.semaphore_signal(barrier, inc=1, device_id=peer, device_id_type=MESH)
    work()
    pl.semaphore_wait(barrier, len(peers))


def gather_round(sizes, refs, work, first_wait, second_wait):
    g_ref, all_ref, stage, send_a, recv_a, send_b, recv_b = refs
    nx, ny, nz = sizes
    gx, gy, gz = [lax.axis_index(name) for name in ("gx", "gy", "gz")]
    plane = plane_peers(nx, nz)
    greet(
        [(lax.rem(gx + ox, nx), gy, lax.rem(gz + oz, nz)) for ox, oz in plane]
        + [(gx, lax.rem(gy + oy, ny), gz) for oy in range(1, ny)],
        work,
    )

    def first(k, x, z, peer):
        return pltpu.make_async_remote_copy(
            src_ref=g_ref,
            dst_ref=stage.at[x, pl.ds(pl.multiple_of(z * 8, 8), 8)],
            send_sem=send_a.at[k],
            recv_sem=recv_a.at[k],
            device_id=peer,
            device_id_type=MESH,
        )

    def second(oy, y):
        return pltpu.make_async_remote_copy(
            src_ref=all_ref.at[gy],
            dst_ref=all_ref.at[y],
            send_sem=send_b.at[oy],
            recv_sem=recv_b.at[oy],
            device_id=(gx, lax.rem(gy + oy, ny), gz),
            device_id_type=MESH,
        )

    for k, (ox, oz) in enumerate(plane):
        first(k, gx, gz, (lax.rem(gx + ox, nx), gy, lax.rem(gz + oz, nz))).start()
    stage[gx, pl.ds(pl.multiple_of(gz * 8, 8), 8)] = g_ref[...]
    first_wait()
    for k, (ox, oz) in enumerate(plane):
        peer = (lax.rem(gx + ox, nx), gy, lax.rem(gz + oz, nz))
        first(k, lax.rem(gx + nx - ox, nx), lax.rem(gz + nz - oz, nz), peer).wait_recv()
    all_ref[gy] = stage[...].astype(BF)
    for oy in range(1, ny):
        second(oy, gy).start()
    second_wait()
    for k, (ox, oz) in enumerate(plane):
        first(k, gx, gz, (lax.rem(gx + ox, nx), gy, lax.rem(gz + oz, nz))).wait_send()
    for oy in range(1, ny):
        second(oy, lax.rem(gy + ny - oy, ny)).wait_recv()
    for oy in range(1, ny):
        second(oy, gy).wait_send()


def reduce_round(sizes, refs, work, waits):
    pay_ref, out_ref, ra, rb, send_a, recv_a, send_b, recv_b, send_c, recv_c = refs
    nx, ny, nz = sizes
    gx, gy, gz = [lax.axis_index(name) for name in ("gx", "gy", "gz")]
    mine = gx * nz + gz
    plane = plane_peers(nx, nz)
    greet(
        [(lax.rem(gx + ox, nx), gy, lax.rem(gz + oz, nz)) for ox, oz in plane]
        + [(gx, lax.rem(gy + oy, ny), gz) for oy in range(1, ny)],
        work,
    )

    def ahead(ox, oz):
        return lax.rem(gx + ox, nx), lax.rem(gz + oz, nz)

    def behind(ox, oz):
        return lax.rem(gx + nx - ox, nx), lax.rem(gz + nz - oz, nz)

    def scatter(k, ox, oz, slot):
        x, z = ahead(ox, oz)
        return pltpu.make_async_remote_copy(
            src_ref=pay_ref.at[x * nz + z],
            dst_ref=ra.at[slot],
            send_sem=send_a.at[k],
            recv_sem=recv_a.at[k],
            device_id=(x, gy, z),
            device_id_type=MESH,
        )

    def across(oy, slot):
        return pltpu.make_async_remote_copy(
            src_ref=rb.at[gy],
            dst_ref=rb.at[slot],
            send_sem=send_b.at[oy],
            recv_sem=recv_b.at[oy],
            device_id=(gx, lax.rem(gy + oy, ny), gz),
            device_id_type=MESH,
        )

    def spread(k, ox, oz, slot):
        x, z = ahead(ox, oz)
        return pltpu.make_async_remote_copy(
            src_ref=out_ref.at[mine],
            dst_ref=out_ref.at[slot],
            send_sem=send_c.at[k],
            recv_sem=recv_c.at[k],
            device_id=(x, gy, z),
            device_id_type=MESH,
        )

    for k, (ox, oz) in enumerate(plane):
        scatter(k, ox, oz, mine).start()
    ra[mine] = pay_ref[mine]
    waits[0]()
    for k, (ox, oz) in enumerate(plane):
        x, z = behind(ox, oz)
        scatter(k, ox, oz, x * nz + z).wait_recv()
    rb[gy] = jnp.sum(ra[...], axis=0)
    for oy in range(1, ny):
        across(oy, gy).start()
    waits[1]()
    for k, (ox, oz) in enumerate(plane):
        scatter(k, ox, oz, mine).wait_send()
    for oy in range(1, ny):
        across(oy, lax.rem(gy + ny - oy, ny)).wait_recv()
    out_ref[mine] = jnp.sum(rb[...], axis=0)
    for k, (ox, oz) in enumerate(plane):
        spread(k, ox, oz, mine).start()
    waits[2]()
    for oy in range(1, ny):
        across(oy, gy).wait_send()
    for k, (ox, oz) in enumerate(plane):
        x, z = behind(ox, oz)
        spread(k, ox, oz, x * nz + z).wait_recv()
    for k, (ox, oz) in enumerate(plane):
        spread(k, ox, oz, mine).wait_send()


def fold(ref, weight):
    ins, outs = weight.shape[1:]
    for i in range(3):
        block = weight[9 * i : 9 * i + 9].astype(F32).reshape(9 * ins, outs)
        ref[pl.ds(i * outs, outs)] = block.T.astype(BF)


def fold_back(ref, weight):
    outs, ins = weight.shape[1:]
    for i in range(3):
        parts = [weight[26 - 9 * i - jk].astype(F32).T for jk in range(9)]
        ref[pl.ds(i * outs, outs)] = jnp.concatenate(parts, axis=0).T.astype(BF)


def arrange_kernel(
    sizes,
    vol_ref,
    cot_ref,
    wf_ref,
    wd_ref,
    wu_ref,
    wp_ref,
    p_ref,
    er_ref,
    el_ref,
    ct_ref,
    pg_ref,
    wf_out,
    wd_out,
    wu_out,
    wdt_out,
    wut_out,
    wp_out,
    v_ref,
    e_ref,
    send,
    recv,
):
    def work():
        spot = lane_of(16) % 64

        def plane(x, edges):
            low, high = edges
            for t, tile in enumerate(plane_rows(vol_ref[:, x])):
                v_ref[x, t] = tile
                wide = tile.astype(F32)
                at = t * 8 + x
                low = jnp.where(spot == at, turn(wide, at), low)
                high = jnp.where(spot == at, turn(wide, at - 63), high)
            return low, high

        zero = jnp.zeros((16, LANES), F32)
        low, high = lax.fori_loop(0, 8, plane, (zero, zero))
        e_ref[0] = low.astype(BF)
        e_ref[1] = high.astype(BF)

    def meanwhile():
        def plane(x, _):
            for t, tile in enumerate(plane_rows(cot_ref[:, x])):
                ct_ref[x, t] = tile
            return 0

        lax.fori_loop(0, 8, plane, 0)
        sums = pool_matrix()

        for x in range(4):
            for half in range(2):
                pg_ref[x, half] = pool_tile(ct_ref, sums, x, half).astype(BF)

        fold(wf_out, wf_ref[...])
        fold(wd_out, wd_ref[...])
        fold(wu_out, wu_ref[...])
        fold_back(wdt_out, wd_ref[...])
        fold_back(wut_out, wu_ref[...])
        wp_out[...] = wp_ref[...].astype(F32).T.astype(BF)

    halo_round(sizes, 1, 1, (v_ref, e_ref, p_ref, er_ref, el_ref, send, recv), work, meanwhile)


def fine_kernel(
    sizes,
    p_ref,
    er_ref,
    el_ref,
    pg_ref,
    wf_ref,
    pre_ref,
    act_ref,
    v3_ref,
    p2_ref,
    er2_ref,
    el2_ref,
    mg_ref,
    e_ref,
    send,
    recv,
):
    def work():
        spot = lane_of(16) % 64

        def rows(x, _):
            dx, sx = (x + 7) // 8, lax.rem(x + 7, 8)
            stacks = []
            for t in range(10):
                dy, sy = (t + 7) // 8, (t + 7) % 8
                at = sy * 8 + sx
                tile = p_ref[x, t].astype(F32)
                left = turn(el_ref[dx, dy].astype(F32), -at)
                right = turn(er_ref[dx, dy].astype(F32), 63 - at)
                before = jnp.where(spot == 0, left, turn(tile, 1))
                after = jnp.where(spot == 63, right, turn(tile, -1))
                stacks.append(jnp.concatenate([before, tile, after], axis=0))
            for t in range(9):
                if t > 0:
                    v3_ref[x, 2 * t - 1] = stacks[t].astype(BF)
                v3_ref[x, 2 * t] = between(stacks[t], stacks[t + 1]).astype(BF)
            return 0

        lax.fori_loop(0, 10, rows, 0)
        weight = wf_ref[...]

        def convs(g, _):
            for x, pre in conv(weight, v3_ref, 8, (4 * g, 4 * g + 2)):
                act = (pre * sigmoid(pre)).astype(BF)
                for b in range(2):
                    pre_ref[x, 2 * g + b] = pre[:, b * LANES : (b + 1) * LANES]
                    act_ref[x, 2 * g + b] = act[:, b * LANES : (b + 1) * LANES]
            return 0

        lax.fori_loop(0, 4, convs, 0)

        sums = pool_matrix()
        lane = lane_of(32)
        low = jnp.zeros((32, LANES), F32)
        high = low
        for x in range(4):
            for half in range(2):
                pooled = (pool_tile(act_ref, sums, x, half) * 0.125).astype(BF)
                tile = jnp.concatenate([pooled, pg_ref[x, half]], axis=0)
                mg_ref[x, half] = tile
                wide = tile.astype(F32)
                for q in range(4):
                    at = (q % 2) * 64 + (x * 4 + 2 * half + q // 2) * 4
                    here = (lane >= at) & (lane < at + 4)
                    low = jnp.where(here, turn(wide, at - 32 * q), low)
                    high = jnp.where(here, turn(wide, at - 32 * q - 28), high)
        e_ref[0] = low.astype(BF)
        e_ref[1] = high.astype(BF)

    halo_round(sizes, 4, 1, (mg_ref, e_ref, p2_ref, er2_ref, el2_ref, send, recv), work, nothing)


def mid_kernel(
    sizes,
    p_ref,
    er_ref,
    el_ref,
    wd_ref,
    am_ref,
    dsm_ref,
    pm3n_ref,
    pgr_ref,
    pcg_ref,
    pm3,
    pgf,
    dsf,
    pc,
    stage,
    send_a,
    recv_a,
    send_b,
    recv_b,
):
    gx, gy, gz = [lax.axis_index(name) for name in ("gx", "gy", "gz")]
    nx, ny, nz = sizes

    def work():
        lane = lane_of(32)
        spot = lane % 64

        def rows(x, _):
            dx, sx = x // 4, lax.rem(x, 4)
            pairs = []
            for a in range(8):
                dy, sy = (a + 2) // 4, (a + 2) % 4
                tile = p_ref[x, a // 2].astype(F32)
                q = 2 * (a % 2)
                base = jnp.where(lane < 64, turn(tile, 8 - 32 * q), turn(tile, 40 - 32 * q))
                at = (sx * 4 + sy) * 4
                right = turn(er_ref[dx, dy].astype(F32), 40 - at)
                left = turn(el_ref[dx, dy].astype(F32), 4 - at)
                row = jnp.where(spot < 44, right, 0.0)
                row = jnp.where(spot < 40, base, row)
                row = jnp.where(spot < 8, left, row)
                row = jnp.where(spot < 4, 0.0, row)
                pgf[x, a] = row[16:].astype(BF)
                pairs.append(row[:16])
            store_taps(pm3, x, pairs)
            pm3[x, 15] = jnp.zeros((48, LANES), BF)
            pm3[x, 16] = jnp.zeros((48, LANES), BF)
            return 0

        lax.fori_loop(0, 12, rows, 0)
        weight = wd_ref[...]
        cell = spot - 8
        mid = cell + gz * 32
        inside = (cell >= -3) & (cell < 35) & (mid >= 0) & (mid < 32 * nz)
        second = lane // 64

        def convs(g, _):
            for x, both in conv(weight, pm3, 10, (4 * g, 4 * g + 2)):
                at_x = gx * 4 + x - 3
                for b in range(2):
                    pre = both[:, b * LANES : (b + 1) * LANES]
                    at_y = gy * 8 + 4 * g + 2 * b - 3 + second
                    keep = inside & (at_y >= 0) & (at_y < 8 * ny)
                    keep = keep & (at_x >= 0) & (at_x < 4 * nx)
                    sig = sigmoid(pre)
                    am_ref[x, 2 * g + b] = jnp.where(keep, pre * sig, 0.0).astype(BF)
                    dsf[x, 2 * g + b] = jnp.where(keep, slope(pre, sig), 0.0).astype(BF)
            return 0

        lax.fori_loop(0, 4, convs, 0)
        halves = [
            jnp.concatenate([am_ref[3 + a, 1 + 2 * h + m] for a in range(4) for m in range(3)], axis=1)
            for h in range(2)
        ]
        cells = jnp.concatenate(halves + [jnp.zeros((64, 12 * LANES), BF)], axis=0)
        col = lax.broadcasted_iota(jnp.int32, (8, 12 * LANES), 1)
        third, upper = col // LANES % 3, col // 64 % 2
        hit = coarse_sum_matrix(12) & ((third == 1) | ((third == 0) == (upper == 1)))
        pooled = dot_nt(jnp.where(hit, 1.0, 0.0).astype(BF), cells) * (1.0 / 64.0)
        pc[...] = pooled.astype(BF).astype(F32)

    def first_wait():
        dsm_ref[...] = dsf[2:8, 1:6]
        pm3n_ref[...] = pm3[3:9, 3:12]
        pgr_ref[...] = pgf[2:10, 1:7]

    gather_round(
        sizes, (pc, pcg_ref, stage, send_a, recv_a, send_b, recv_b), work, first_wait, nothing
    )


def up_kernel(
    sizes,
    scale,
    pcg_ref,
    am_ref,
    act_ref,
    pgr_ref,
    wl_ref,
    wc_ref,
    wp_ref,
    wu_ref,
    wut_ref,
    dec_ref,
    gj_ref,
    gwu_ref,
    gcg_ref,
    dsc_ref,
    actc_ref,
    alc_ref,
    wide_lift,
    al3,
    acc,
    cos,
    j3,
    guo,
    gu3,
    su,
    plane,
    gc,
    stage,
    send_a,
    recv_a,
    send_b,
    recv_b,
):
    nx, ny, nz = sizes
    gy, gz = lax.axis_index("gy"), lax.axis_index("gz")
    cells = 8 * nz

    def lift(o, _):
        y = lax.rem(gy + o + 4 * ny - 2, ny)
        for x in range(nx):
            for y2 in range(2):
                pre = dot(pcg_ref[y, x], wide_lift[y2])
                act = (pre * sigmoid(pre)).astype(BF)
                alc_ref[x, y, y2] = act
                store_coarse_taps(al3, (x + 1, 2 * y + y2 + 1), act.astype(F32))
        return 0

    def coarse(o, _):
        y = lax.rem(gy + o + ny - 1, ny)
        for i in range(3):
            for j in range(3):
                block = al3[pl.ds(i, nx), pl.ds(2 * y + j, 2)].reshape(nx * 2 * cells, 768)
                part = dot(block, wc_ref[3 * i + j])
                if i + j == 0:
                    acc[...] = part
                else:
                    acc[...] += part
        pre = acc[...]
        sig = sigmoid(pre)
        act = (pre * sig).astype(BF).reshape(nx, 2, cells, 256)
        grad = slope(pre, sig).astype(BF).reshape(nx, 2, cells, 256)
        for x in range(nx):
            actc_ref[x, y] = act[x]
            dsc_ref[x, y] = grad[x]
        return 0

    def work():
        place_weight(wide_lift, wl_ref[...])
        zero_rim(al3, 1)
        lax.fori_loop(0, 5, lift, 0)
        lax.fori_loop(0, 3, coarse, 0)

        spread = coarse_grow_matrix(cells, gz)
        for dx, dy, x, y, y2, keep in near_cells(sizes):
            out = dot_nt(wp_ref[...], actc_ref[x, y, y2]).astype(BF)
            cos[dx, dy] = dot(out, spread) * keep

        first = lane_of(32) < 64

        def join(x, _):
            pairs = []
            for m in range(7):
                add = jnp.where(
                    first, cos[(x + 1) // 4, (2 * m + 1) // 4], cos[(x + 1) // 4, (2 * m + 2) // 4]
                )
                row = am_ref[x, m].astype(F32) + add
                pairs.append(row.astype(BF).astype(F32))
            store_taps(j3, x, pairs)
            return 0

        lax.fori_loop(0, 10, join, 0)

        cell = lane_of(16) % 64 - 8
        near = (cell >= -2) & (cell < 34)
        weight = wu_ref[...]

        def up(g, _):
            for x, both in conv(weight, j3, 8, (4 * g, 4 * g + 2)):
                for b in range(2):
                    pre = both[:, b * LANES : (b + 1) * LANES]
                    sig = sigmoid(pre)
                    su[x, 2 * g + b] = (pre * sig).astype(BF)
                    pooled = pgr_ref[x, 2 * g + b].astype(F32) * scale
                    guo[x, 2 * g + b] = jnp.where(near, pooled * slope(pre, sig), 0.0).astype(BF)
            return 0

        lax.fori_loop(0, 3, up, 0)

        def stack(x, _):
            store_taps(gu3, x, [guo[x, m].astype(F32) for m in range(6)])
            return 0

        lax.fori_loop(0, 8, stack, 0)

        weight_t = wut_ref[...]
        for starts in ((0, 2), (4, 6), (8,)):
            for x, both in conv(weight_t, gu3, 6, starts):
                for b, y in enumerate(starts):
                    gj_ref[x, y // 2] = both[:, b * LANES : (b + 1) * LANES]

        totals = []
        for h in range(2):
            total = None
            for a in range(4):
                lower, middle, upper = [gj_ref[1 + a, 2 * h + m] for m in range(3)]
                row = middle + jnp.where(first, upper, lower)
                total = row if total is None else total + row
            totals.append(total)
        total = jnp.concatenate(totals + [jnp.zeros((64, LANES), F32)], axis=0)
        head = total.astype(BF)
        tail = (total - head.astype(F32)).astype(BF)
        sums = jnp.where(coarse_sum_matrix(1), 1.0, 0.0).astype(BF)
        gc[...] = (dot_nt(sums, head) + dot_nt(sums, tail)).astype(BF).astype(F32)

    def first_wait():
        cell = lane_of(16) % 64 - 8
        own = (cell >= 0) & (cell < 32)
        gwu_ref[...] = jnp.zeros(gwu_ref.shape, F32)
        grads = [
            jnp.concatenate(
                [jnp.where(own, guo[x + 2, m + 1].astype(F32), 0.0) for m in range(4)], axis=1
            ).astype(BF)
            for x in range(4)
        ]
        none = jnp.zeros((16, 4 * LANES), BF)
        for x in range(6):
            left = [grads[x - i] if 0 <= x - i < 4 else none for i in range(3)]
            right = [three(j3, x + 2, 2 * m + 2) for m in range(4)]
            gwu_ref[:, pl.ds(0, 288)] += dot_nt(
                jnp.concatenate(left, axis=0), jnp.concatenate(right, axis=1)
            )

        grow = grow_matrix()

        def decode(x, _):
            rows = jnp.concatenate([su[x + 2, m + 1] for m in range(4)], axis=0)
            grown = dot(rows, grow)
            for a in range(2):
                for t in range(8):
                    add = grown[16 * (t // 2) : 16 * (t // 2) + 16, (t % 2) * LANES :][:, :LANES]
                    tile = act_ref[2 * x + a, t].astype(F32) + add
                    plane[2 * t] = tile.astype(BF)
                    plane[2 * t + 1] = turn(tile, 64).astype(BF)
                dec_ref[:, 2 * x + a] = jnp.swapaxes(plane[...], 0, 1)[:, :, :64]
            return 0

        lax.fori_loop(0, 4, decode, 0)

    def second_wait():
        lax.fori_loop(5, max(ny, 5), lift, 0)
        lax.fori_loop(3, max(ny, 3), coarse, 0)

    gather_round(
        sizes, (gc, gcg_ref, stage, send_a, recv_a, send_b, recv_b), work, first_wait, second_wait
    )


def back_kernel(
    sizes,
    scale,
    gcg_ref,
    pcg_ref,
    dsc_ref,
    actc_ref,
    alc_ref,
    gj_ref,
    dsm_ref,
    pm3n_ref,
    ct_ref,
    pre_ref,
    v3_ref,
    gwu_ref,
    wl_ref,
    wc_ref,
    wp_ref,
    wdt_ref,
    red_ref,
    gwc_ref,
    gwp_ref,
    wide_lift,
    wide_proj,
    gp3,
    acc,
    gps,
    gm3,
    gpm,
    gf,
    accf,
    accd,
    sums,
    cells_t,
    pay,
    ra,
    rb,
    send_a,
    recv_a,
    send_b,
    recv_b,
    send_c,
    recv_c,
):
    nx, ny, nz = sizes
    gx, gy, gz = [lax.axis_index(name) for name in ("gx", "gy", "gz")]
    cells = 8 * nz
    count = nx * ny * 2 * cells

    def coarse(o, _):
        y = lax.rem(gy + o + ny - 1, ny)
        for x in range(nx):
            for y2 in range(2):
                grad = dot(gcg_ref[y, x], wide_proj[y2]) * dsc_ref[x, y, y2].astype(F32)
                grad = grad.astype(BF).astype(F32)
                store_coarse_taps(gp3, (x + 2, 2 * y + y2 + 2), grad)
        return 0

    def work():
        place_weight(wide_lift, wl_ref[...])
        place_weight(wide_proj, wp_ref[...])
        zero_rim(gp3, 2)
        lax.fori_loop(0, 3, coarse, 0)
        acc[...] = jnp.zeros(acc.shape, F32)

        def coarse_back(i, _):
            for j in range(3):
                block = gp3[pl.ds(gx + i, 3), pl.ds(2 * gy + j, 4)].reshape(12 * cells, 768)
                for k in range(3):
                    weight = wc_ref[8 - 3 * i - j, pl.ds(256 * (2 - k), 256)]
                    acc[...] += dot_nt(block[:, 256 * k : 256 * (k + 1)], weight)
            return 0

        lax.fori_loop(0, 3, coarse_back, 0)

        spread = coarse_grow_matrix(cells, gz)
        own = lax.broadcasted_iota(jnp.int32, (cells, 256), 0) // 8 == gz
        for at, (dx, dy, x, y, y2, keep) in enumerate(near_cells(sizes)):
            pre = dot(pcg_ref[y, x], wide_lift[y2])
            grad = (acc[pl.ds(at * cells, cells)] * slope(pre, sigmoid(pre))).astype(BF)
            out = dot_nt(wl_ref[...], grad).astype(BF)
            gps[dx, dy] = dot(out, spread) * (keep * (1.0 / 64.0))
            if dx == 1 and dy in (1, 2):
                masked = jnp.where(own, grad.astype(F32), 0.0).astype(BF)
                sums[y2] = dot_tn(pcg_ref[y, x], masked)
        lifts = sums[0, :32] + sums[1, 32:64]
        for b in range(2):
            pay_rows(432 + 32 * b, lifts[:, b * LANES : (b + 1) * LANES])

        first = lane_of(32) < 64

        def join(x, _):
            pairs = []
            for n in range(5):
                add = jnp.where(
                    first,
                    gps[(x + 3) // 4, (2 * n + 3) // 4],
                    gps[(x + 3) // 4, (2 * n + 4) // 4],
                )
                row = (gj_ref[x, n] + add) * dsm_ref[x, n].astype(F32)
                pairs.append(row.astype(BF).astype(F32))
            store_taps(gm3, x, pairs)
            return 0

        lax.fori_loop(0, 6, join, 0)

        weight_t = wdt_ref[...]
        for starts in ((0, 2), (4, 6)):
            for x, both in conv(weight_t, gm3, 4, starts):
                for b, y in enumerate(starts):
                    tile = both[:, b * LANES : (b + 1) * LANES].astype(BF)
                    gpm[x, pl.ds(8 * y, 16)] = tile

        grow = grow_matrix()
        for x in (0, 1, 10, 11):
            gf[x] = jnp.zeros(gf.shape[1:], BF)

        def fine(x, _):
            grown = dot(gpm[x], grow) * 0.125
            for a in range(2):
                for t in range(8):
                    add = grown[16 * (t // 2) : 16 * (t // 2) + 16, (t % 2) * LANES :][:, :LANES]
                    pre = pre_ref[2 * x + a, t]
                    grad = ct_ref[2 * x + a, t].astype(F32) * scale + add
                    grad = (grad * slope(pre, sigmoid(pre))).astype(BF)
                    gf[2 * x + a + 2, :, pl.ds(t * LANES, LANES)] = grad
            return 0

        lax.fori_loop(0, 4, fine, 0)

        accd[...] = jnp.zeros(accd.shape, F32)
        spot = lane_of(32) % 64
        inner = (spot >= 8) & (spot < 40)
        grads = [
            jnp.concatenate(
                [
                    jnp.where(inner, gm3[x + 1, 2 * m + 1, pl.ds(32, 32)].astype(F32), 0.0)
                    for m in range(4)
                ],
                axis=1,
            ).astype(BF)
            for x in range(4)
        ]
        none = jnp.zeros((32, 4 * LANES), BF)
        for x in range(6):
            left = [grads[x - i] if 0 <= x - i < 4 else none for i in range(3)]
            right = [three(pm3n_ref, x, 2 * m) for m in range(4)]
            accd[:, pl.ds(0, 144)] += dot_nt(
                jnp.concatenate(left, axis=0), jnp.concatenate(right, axis=1)
            )

        accf[...] = jnp.zeros(accf.shape, F32)

        def taps_fine(x, _):
            left = jnp.concatenate([gf[x + 2 - i] for i in range(3)], axis=0)
            right = jnp.concatenate([three(v3_ref, x, 2 * t) for t in range(8)], axis=1)
            accf[:, pl.ds(0, 144)] += dot_nt(left, right)
            return 0

        lax.fori_loop(0, 10, taps_fine, 0)

        for b in range(2):
            pay_rows(48 * b, accf[:, b * LANES : (b + 1) * LANES])
        for b in range(3):
            pay_rows(96 + 48 * b, gwu_ref[:, b * LANES : (b + 1) * LANES])
        for b in range(2):
            pay_rows(240 + 96 * b, accd[:, b * LANES : (b + 1) * LANES])
        pay_rows(496, jnp.zeros((16, LANES), F32))

    def pay_rows(start, block):
        per = pay.shape[1]
        done = 0
        while done < block.shape[0]:
            part, at = divmod(start + done, per)
            size = min(per - at, block.shape[0] - done)
            pay[part, pl.ds(at, size)] = block[done : done + size]
            done += size

    def coarse_taps(t, _):
        i, j = t // 3, lax.rem(t, 3)
        block = gp3[pl.ds(3 - i, nx), pl.ds(3 - j, 2 * ny)].reshape(count, 768)
        out = dot(cells_t[...], block)
        for k in range(3):
            gwc_ref[3 * t + k] = out[:, 256 * (2 - k) : 256 * (3 - k)].astype(BF)
        return 0

    def wait_a():
        lax.fori_loop(3, max(ny, 3), coarse, 0)
        cells_t[...] = alc_ref[...].reshape(count, 256).T
        lax.fori_loop(0, 2, coarse_taps, 0)

    def wait_b():
        lax.fori_loop(2, 5, coarse_taps, 0)

    def wait_c():
        lax.fori_loop(5, 9, coarse_taps, 0)
        sums[...] = jnp.zeros(sums.shape, F32)

        def proj_grad(x, _):
            for y2 in range(2):
                grads = gcg_ref[:, x].reshape(ny * cells, LANES)
                sums[y2] += dot_tn(grads, actc_ref[x, :, y2].reshape(ny * cells, 256))
            return 0

        lax.fori_loop(0, nx, proj_grad, 0)
        gwp_ref[...] = sums[0, :32] + sums[1, 32:64]

    reduce_round(
        sizes,
        (pay, red_ref, ra, rb, send_a, recv_a, send_b, recv_b, send_c, recv_c),
        work,
        (wait_a, wait_b, wait_c),
    )


def last_kernel(gwc_ref, red_ref, gwp_ref, wc_out, wf_out, wd_out, wl_out, wp_out, wu_out):
    @pl.when(pl.program_id(0) == 0)
    def _():
        def columns(start, blocks, rows):
            return jnp.concatenate(
                [red_ref[pl.ds(start + rows * b, rows)] for b in range(blocks)], axis=1
            )

        for out, start, blocks in ((wf_out, 0, 2), (wu_out, 96, 3), (wd_out, 240, 2)):
            ins, outs = out.shape[1:]
            table = columns(start, blocks, 3 * outs)
            for i in range(3):
                part = table[i * outs : (i + 1) * outs, : 9 * ins]
                out[pl.ds(9 * i, 9)] = part.T.reshape(9, ins, outs)
        wl_out[...] = columns(432, 2, 32)
        wp_out[...] = gwp_ref[...].T

    wc_out[...] = gwc_ref[...].astype(F32)


VMEM = pl.BlockSpec(memory_space=pltpu.VMEM)


def call(kernel, outs, args, scratch, collective):
    return pl.pallas_call(
        kernel,
        out_shape=[jax.ShapeDtypeStruct(shape, kind) for shape, kind in outs],
        in_specs=[VMEM] * len(args),
        out_specs=[VMEM] * len(outs),
        scratch_shapes=scratch,
        compiler_params=pltpu.CompilerParams(
            vmem_limit_bytes=56 * 1024 * 1024, collective_id=collective, has_side_effects=True
        ),
    )(*args)


def dma(*counts):
    return [pltpu.SemaphoreType.DMA((count,)) for count in counts]


def bf(*shape):
    return pltpu.VMEM(shape, BF)


def f32(*shape):
    return pltpu.VMEM(shape, F32)


def halo_shapes(planes, tiles, chans):
    return [
        ((planes, tiles, chans, LANES), BF),
        ((3, 3, chans, LANES), BF),
        ((3, 3, chans, LANES), BF),
    ]


def shards(sizes, volume, w_fine, w_down, w_lift, w_coarse, w_proj, w_up, cotangent):
    nx, ny, nz = sizes
    scale = 1.0 / math.sqrt(8 * nx * 16 * ny * 64 * nz)
    cells = 8 * nz
    wc = w_coarse.reshape(9, 768, 256)

    *halo, ct, pg, wf, wd, wu, wdt, wut, wp = call(
        functools.partial(arrange_kernel, sizes),
        halo_shapes(10, 10, 16)
        + [
            ((8, 8, 16, LANES), BF),
            ((4, 2, 16, LANES), BF),
            ((48, 144), BF),
            ((96, 144), BF),
            ((48, 288), BF),
            ((48, 288), BF),
            ((96, 144), BF),
            ((32, 256), BF),
        ],
        [volume, cotangent, w_fine, w_down, w_up, w_proj],
        [bf(8, 8, 16, LANES), bf(2, 16, LANES)] + dma(26, 26),
        1,
    )
    pre, act, v3, *halo = call(
        functools.partial(fine_kernel, sizes),
        [((8, 8, 16, LANES), F32), ((8, 8, 16, LANES), BF), ((10, 17, 48, LANES), BF)]
        + halo_shapes(12, 4, 32),
        [*halo, pg, wf],
        [bf(4, 2, 32, LANES), bf(2, 32, LANES)] + dma(26, 26),
        2,
    )
    gather_scratch = [f32(8, LANES), f32(nx, cells, LANES)] + dma(nx * nz, nx * nz, ny, ny)
    am, dsm, pm3n, pgr, pcg = call(
        functools.partial(mid_kernel, sizes),
        [
            ((10, 8, 32, LANES), BF),
            ((6, 5, 32, LANES), BF),
            ((6, 9, 48, LANES), BF),
            ((8, 6, 16, LANES), BF),
            ((ny, nx, cells, LANES), BF),
        ],
        [*halo, wd],
        [bf(12, 17, 48, LANES), bf(12, 8, 16, LANES), bf(10, 8, 32, LANES)] + gather_scratch,
        3,
    )
    grid = (nx, ny, 2, cells, 256)
    dec, gj, gwu, gcg, dsc, actc, alc = call(
        functools.partial(up_kernel, sizes, scale),
        [
            ((16, 8, 16, 64), BF),
            ((6, 5, 32, LANES), F32),
            ((48, 3 * LANES), F32),
            ((ny, nx, cells, LANES), BF),
            (grid, BF),
            (grid, BF),
            (grid, BF),
        ],
        [pcg, am, act, pgr, w_lift, wc, wp, wu, wut],
        [
            bf(2, LANES, 256),
            bf(nx + 2, 2 * ny + 2, cells, 768),
            f32(nx * 2 * cells, 256),
            f32(3, 4, 32, LANES),
            bf(10, 13, 96, LANES),
            bf(8, 6, 16, LANES),
            bf(8, 11, 48, LANES),
            bf(8, 6, 16, LANES),
            bf(16, 16, LANES),
        ]
        + gather_scratch,
        4,
    )
    parts = nx * nz
    rows = 512 // parts
    red, gwc, gwp = call(
        functools.partial(back_kernel, sizes, scale),
        [((parts, rows, LANES), F32), ((27, 256, 256), BF), ((32, 256), F32)],
        [gcg, pcg, dsc, actc, alc, gj, dsm, pm3n, ct, pre, v3, gwu, w_lift, wc, wp, wdt],
        [
            bf(2, LANES, 256),
            bf(2, LANES, 256),
            bf(nx + 4, 2 * ny + 4, cells, 768),
            f32(12 * cells, 256),
            f32(3, 4, 32, LANES),
            bf(6, 9, 96, LANES),
            bf(4, 64, LANES),
            bf(12, 16, 8 * LANES),
            f32(48, 2 * LANES),
            f32(96, 2 * LANES),
            f32(2, LANES, 256),
            bf(256, nx * ny * 2 * cells),
            f32(parts, rows, LANES),
            f32(parts, rows, LANES),
            f32(ny, rows, LANES),
        ]
        + dma(parts, parts, ny, ny, parts, parts),
        5,
    )
    shapes = [(27, 256, 256), (27, 16, 16), (27, 16, 32), (32, 256), (256, 32), (27, 32, 16)]

    def whole(shape):
        return pl.BlockSpec(shape, lambda t: (0,) * len(shape))

    block = pl.BlockSpec((3, 256, 256), lambda t: (t, 0, 0))
    gwc, gwf, gwd, gwl, gwp, gwu = pl.pallas_call(
        last_kernel,
        grid=(9,),
        out_shape=[jax.ShapeDtypeStruct(shape, F32) for shape in shapes],
        in_specs=[block, whole((512, LANES)), whole((32, 256))],
        out_specs=[block] + [whole(shape) for shape in shapes[1:]],
        compiler_params=pltpu.CompilerParams(dimension_semantics=("arbitrary",)),
    )(gwc, red.reshape(512, LANES), gwp)
    return dec, gwf, gwd, gwl, gwc, gwp, gwu


def solution(mesh):
    sizes = tuple(mesh.shape[name] for name in ("gx", "gy", "gz"))
    block = P(None, "gx", "gy", "gz")
    return jax.shard_map(
        functools.partial(shards, sizes),
        mesh=mesh,
        in_specs=(block, P(), P(), P(), P(), P(), P(), block),
        out_specs=(block, P(), P(), P(), P(), P(), P()),
        check_vma=False,
    )
```

```python
import functools
import math
import types

import jax
import jax.numpy as jnp
from jax import lax
from jax.experimental import pallas as pl
from jax.experimental.pallas import tpu as pltpu
from jax.sharding import PartitionSpec as P

BF = jnp.bfloat16
F32 = jnp.float32
MESH = pl.DeviceIdType.MESH
LANES = 128


def dot(left, right):
    return jnp.dot(left, right, preferred_element_type=F32)


def dot_nt(left, right):
    return lax.dot_general(left, right, (((1,), (1,)), ((), ())), preferred_element_type=F32)


def dot_tn(left, right):
    return lax.dot_general(left, right, (((0,), (0,)), ((), ())), preferred_element_type=F32)


def sigmoid(values):
    return 0.5 * jnp.tanh(0.5 * values) + 0.5


def slope(values, sig):
    return sig * (1.0 + values * (1.0 - sig))


def lane_of(rows):
    return lax.broadcasted_iota(jnp.int32, (rows, LANES), 1)


def turn(tile, by):
    if isinstance(by, int):
        by = by % LANES
        return tile if by == 0 else pltpu.roll(tile, by, 1)
    return pltpu.roll(tile, lax.rem(by + 4 * LANES, LANES), 1)


def tap_rows(pair):
    return jnp.concatenate([turn(pair, 1), pair, turn(pair, -1)], axis=0)


def between(lower, upper):
    lane = lane_of(lower.shape[0])
    return jnp.where(lane < 64, turn(lower, 64), turn(upper, 64))


def store_taps(ref, x, pairs):
    stacks = [tap_rows(pair) for pair in pairs]
    for n, stack in enumerate(stacks):
        ref[x, 2 * n] = stack.astype(BF)
        if n + 1 < len(stacks):
            ref[x, 2 * n + 1] = between(stack, stacks[n + 1]).astype(BF)


def three(ref, x, y):
    block = ref[x, pl.ds(y, 3)]
    return block.reshape(3 * block.shape[1], LANES)


def conv(weight, ref, planes, starts):
    outs = weight.shape[0] // 3
    parts = []
    for x in range(planes + 2):
        tiles = [three(ref, x, y) for y in starts]
        block = tiles[0] if len(tiles) == 1 else jnp.concatenate(tiles, axis=1)
        parts.append(dot(weight, block))
        if x >= 2:
            yield (
                x - 2,
                parts[x - 2][:outs] + parts[x - 1][outs : 2 * outs] + parts[x][2 * outs :],
            )


def pool_matrix():
    row = lax.broadcasted_iota(jnp.int32, (8 * LANES, LANES), 0)
    col = lax.broadcasted_iota(jnp.int32, (8 * LANES, LANES), 1)
    hit = (row // 256 == col // 32) & (row % 64 // 2 == col % 32)
    return jnp.where(hit, 1.0, 0.0).astype(BF)


def pool_tile(ref, sums, x, half):
    cells = jnp.concatenate([ref[2 * x + a, 4 * half + q] for q in range(4) for a in range(2)], axis=1)
    return dot(cells, sums)


def grow_matrix():
    row = lax.broadcasted_iota(jnp.int32, (LANES, 2 * LANES), 0)
    col = lax.broadcasted_iota(jnp.int32, (LANES, 2 * LANES), 1)
    hit = (row // 64 == col // LANES) & (row % 64 - 8 == col % 64 // 2)
    return jnp.where(hit, 1.0, 0.0).astype(BF)


def coarse_sum_matrix(tiles):
    row = lax.broadcasted_iota(jnp.int32, (8, tiles * LANES), 0)
    cell = lax.broadcasted_iota(jnp.int32, (8, tiles * LANES), 1) % 64 - 8
    return (cell >= 0) & (cell < 32) & ((cell + 4) // 4 == row + 1)


def coarse_grow_matrix(cells, gz):
    row = lax.broadcasted_iota(jnp.int32, (cells, LANES), 0)
    cell = lax.broadcasted_iota(jnp.int32, (cells, LANES), 1) % 64 - 8
    mid = cell + gz * 32
    hit = (cell >= -3) & (cell < 35) & (mid >= 0) & (row == (mid + 4) // 4 - 1)
    return jnp.where(hit, 1.0, 0.0).astype(BF)


def plane_rows(block):
    rows = jnp.swapaxes(block, 0, 1)
    return [jnp.concatenate([rows[2 * t], rows[2 * t + 1]], axis=1) for t in range(8)]


def place_weight(ref, weight):
    for y2 in range(2):
        ref[y2] = jnp.zeros((LANES, 256), BF)
        ref[y2, pl.ds(32 * y2, 32)] = weight


def store_coarse_taps(ref, at, cells):
    count = cells.shape[0]
    row = lax.broadcasted_iota(jnp.int32, cells.shape, 0)
    before = jnp.where(row > 0, pltpu.roll(cells, 1, 0), 0.0)
    after = jnp.where(row < count - 1, pltpu.roll(cells, count - 1, 0), 0.0)
    ref[at + (slice(None), pl.ds(0, 256))] = before.astype(BF)
    ref[at + (slice(None), pl.ds(256, 256))] = cells.astype(BF)
    ref[at + (slice(None), pl.ds(512, 256))] = after.astype(BF)


def zero_rim(ref, rim):
    planes, rows = ref.shape[:2]

    def clear(x, _):
        for y in list(range(rim)) + list(range(rows - rim, rows)):
            ref[x, y] = jnp.zeros(ref.shape[2:], ref.dtype)
        return 0

    lax.fori_loop(0, planes, clear, 0)

    def clear_plane(y, _):
        for x in list(range(rim)) + list(range(planes - rim, planes)):
            ref[x, y] = jnp.zeros(ref.shape[2:], ref.dtype)
        return 0

    lax.fori_loop(0, rows, clear_plane, 0)


def clamp(at, count):
    return jnp.minimum(jnp.maximum(at, 0), count - 1)


def near_cells(sizes):
    nx, ny, _ = sizes
    gx, gy = lax.axis_index("gx"), lax.axis_index("gy")
    found = []
    for dx in range(3):
        for dy in range(4):
            x, y = gx - 1 + dx, gy + (dy + 1) // 2 - 1
            there = (x >= 0) & (x < nx) & (y >= 0) & (y < ny)
            keep = jnp.where(there, 1.0, 0.0)
            found.append((dx, dy, clamp(x, nx), clamp(y, ny), (dy + 1) % 2, keep))
    return found


def nothing():
    pass


NEIGHBOURS = [
    (dx, dy, dz)
    for dz in (-1, 1, 0)
    for dx in (-1, 0, 1)
    for dy in (-1, 0, 1)
    if (dx, dy, dz) != (0, 0, 0)
]


def position():
    return [lax.axis_index(name) for name in ("gx", "gy", "gz")]


def valid(sizes, steps):
    found = None
    for at, size, step in zip(position(), sizes, steps):
        if step != 0:
            test = at > 0 if step < 0 else at < size - 1
            found = test if found is None else found & test
    return found


def plane_peers(nx, nz):
    return [(ox, oz) for ox in range(nx) for oz in range(nz) if (ox, oz) != (0, 0)]


def greet(sizes, work):
    nx, ny, nz = sizes
    me = gx, gy, gz = position()
    barrier = pltpu.get_barrier_semaphore()
    peers = [(lax.rem(gx + ox, nx), gy, lax.rem(gz + oz, nz)) for ox, oz in plane_peers(nx, nz)]
    peers += [(gx, lax.rem(gy + oy, ny), gz) for oy in range(1, ny)]
    for peer in peers:
        pl.semaphore_signal(barrier, inc=1, device_id=peer, device_id_type=MESH)
    total = 1
    for axis in range(3):
        low = jnp.where(me[axis] > 0, 1, 0)
        high = jnp.where(me[axis] < sizes[axis] - 1, 1, 0)
        total = total * (1 + low + high)
    for steps in NEIGHBOURS:

        @pl.when(valid(sizes, steps))
        def _():
            pl.semaphore_signal(
                barrier,
                inc=1,
                device_id=tuple(me[axis] + steps[axis] for axis in range(3)),
                device_id_type=MESH,
            )

    work()
    pl.semaphore_wait(barrier, total - 1 + len(peers))


def halo_round(sizes, hx, ht, refs, meanwhile):
    a_ref, e_ref, p_ref, er_ref, el_ref, send_sem, recv_sem = refs
    me = [lax.axis_index(name) for name in ("gx", "gy", "gz")]
    planes, tiles = a_ref.shape[:2]

    def part(step, halo, count):
        if step == 0:
            return pl.ds(0, count), pl.ds(halo, count)
        if step > 0:
            return pl.ds(count - halo, halo), pl.ds(0, halo)
        return pl.ds(0, halo), pl.ds(count + halo, halo)

    def copy_of(k, steps):
        dx, dy, dz = steps
        if dz == 0:
            fx, tx = part(dx, hx, planes)
            fy, ty = part(dy, ht, tiles)
            src, dst = a_ref.at[fx, fy], p_ref.at[tx, ty]
        elif dz > 0:
            src, dst = e_ref.at[1], el_ref.at[1 - dx, 1 - dy]
        else:
            src, dst = e_ref.at[0], er_ref.at[1 - dx, 1 - dy]
        return pltpu.make_async_remote_copy(
            src_ref=src,
            dst_ref=dst,
            send_sem=send_sem.at[k],
            recv_sem=recv_sem.at[k],
            device_id=(me[0] + dx, me[1] + dy, me[2] + dz),
            device_id_type=MESH,
        )

    for k, steps in enumerate(NEIGHBOURS):

        @pl.when(valid(sizes, steps))
        def _():
            copy_of(k, steps).start()

    p_ref[pl.ds(hx, planes), pl.ds(ht, tiles)] = a_ref[...]
    for k, steps in enumerate(NEIGHBOURS):
        back = tuple(-step for step in steps)
        dx, dy, dz = steps

        @pl.when(jnp.logical_not(valid(sizes, back)))
        def _():
            if dz == 0:
                _, tx = part(dx, hx, planes)
                _, ty = part(dy, ht, tiles)
                into = p_ref.at[tx, ty]
            elif dz > 0:
                into = el_ref.at[1 - dx, 1 - dy]
            else:
                into = er_ref.at[1 - dx, 1 - dy]
            into[...] = jnp.zeros(into.shape, into.dtype)

    meanwhile()
    for k, steps in enumerate(NEIGHBOURS):
        back = tuple(-step for step in steps)

        @pl.when(valid(sizes, back))
        def _():
            copy_of(k, steps).wait_recv()

    for k, steps in enumerate(NEIGHBOURS):

        @pl.when(valid(sizes, steps))
        def _():
            copy_of(k, steps).wait_send()


def gather_round(sizes, refs, first_wait, second_wait):
    g_ref, all_ref, stage, send_a, recv_a, send_b, recv_b = refs
    nx, ny, nz = sizes
    gx, gy, gz = [lax.axis_index(name) for name in ("gx", "gy", "gz")]
    plane = plane_peers(nx, nz)

    def first(k, x, z, peer):
        return pltpu.make_async_remote_copy(
            src_ref=g_ref,
            dst_ref=stage.at[x, pl.ds(pl.multiple_of(z * 8, 8), 8)],
            send_sem=send_a.at[k],
            recv_sem=recv_a.at[k],
            device_id=peer,
            device_id_type=MESH,
        )

    def second(oy, y):
        return pltpu.make_async_remote_copy(
            src_ref=all_ref.at[gy],
            dst_ref=all_ref.at[y],
            send_sem=send_b.at[oy],
            recv_sem=recv_b.at[oy],
            device_id=(gx, lax.rem(gy + oy, ny), gz),
            device_id_type=MESH,
        )

    for k, (ox, oz) in enumerate(plane):
        first(k, gx, gz, (lax.rem(gx + ox, nx), gy, lax.rem(gz + oz, nz))).start()
    stage[gx, pl.ds(pl.multiple_of(gz * 8, 8), 8)] = g_ref[...]
    first_wait()
    for k, (ox, oz) in enumerate(plane):
        peer = (lax.rem(gx + ox, nx), gy, lax.rem(gz + oz, nz))
        first(k, lax.rem(gx + nx - ox, nx), lax.rem(gz + nz - oz, nz), peer).wait_recv()
    all_ref[gy] = stage[...].astype(BF)
    for oy in range(1, ny):
        second(oy, gy).start()
    second_wait()
    for k, (ox, oz) in enumerate(plane):
        first(k, gx, gz, (lax.rem(gx + ox, nx), gy, lax.rem(gz + oz, nz))).wait_send()
    for oy in range(1, ny):
        second(oy, lax.rem(gy + ny - oy, ny)).wait_recv()
    for oy in range(1, ny):
        second(oy, gy).wait_send()


def reduce_round(sizes, refs, waits):
    pay_ref, out_ref, ra, rb, send_a, recv_a, send_b, recv_b, send_c, recv_c = refs
    nx, ny, nz = sizes
    gx, gy, gz = [lax.axis_index(name) for name in ("gx", "gy", "gz")]
    mine = gx * nz + gz
    plane = plane_peers(nx, nz)

    def ahead(ox, oz):
        return lax.rem(gx + ox, nx), lax.rem(gz + oz, nz)

    def behind(ox, oz):
        return lax.rem(gx + nx - ox, nx), lax.rem(gz + nz - oz, nz)

    def scatter(k, ox, oz, slot):
        x, z = ahead(ox, oz)
        return pltpu.make_async_remote_copy(
            src_ref=pay_ref.at[x * nz + z],
            dst_ref=ra.at[slot],
            send_sem=send_a.at[k],
            recv_sem=recv_a.at[k],
            device_id=(x, gy, z),
            device_id_type=MESH,
        )

    def across(oy, slot):
        return pltpu.make_async_remote_copy(
            src_ref=rb.at[gy],
            dst_ref=rb.at[slot],
            send_sem=send_b.at[oy],
            recv_sem=recv_b.at[oy],
            device_id=(gx, lax.rem(gy + oy, ny), gz),
            device_id_type=MESH,
        )

    def spread(k, ox, oz, slot):
        x, z = ahead(ox, oz)
        return pltpu.make_async_remote_copy(
            src_ref=out_ref.at[mine],
            dst_ref=out_ref.at[slot],
            send_sem=send_c.at[k],
            recv_sem=recv_c.at[k],
            device_id=(x, gy, z),
            device_id_type=MESH,
        )

    for k, (ox, oz) in enumerate(plane):
        scatter(k, ox, oz, mine).start()
    ra[mine] = pay_ref[mine]
    waits[0]()
    for k, (ox, oz) in enumerate(plane):
        x, z = behind(ox, oz)
        scatter(k, ox, oz, x * nz + z).wait_recv()
    rb[gy] = jnp.sum(ra[...], axis=0)
    for oy in range(1, ny):
        across(oy, gy).start()
    waits[1]()
    for k, (ox, oz) in enumerate(plane):
        scatter(k, ox, oz, mine).wait_send()
    for oy in range(1, ny):
        across(oy, lax.rem(gy + ny - oy, ny)).wait_recv()
    out_ref[mine] = jnp.sum(rb[...], axis=0)
    for k, (ox, oz) in enumerate(plane):
        spread(k, ox, oz, mine).start()
    waits[2]()
    for oy in range(1, ny):
        across(oy, gy).wait_send()
    for k, (ox, oz) in enumerate(plane):
        x, z = behind(ox, oz)
        spread(k, ox, oz, x * nz + z).wait_recv()
    for k, (ox, oz) in enumerate(plane):
        spread(k, ox, oz, mine).wait_send()


def fold(ref, i, tiles):
    block = jnp.concatenate(tiles, axis=0)
    outs = block.shape[1]
    ref[pl.ds(i * outs, outs)] = block.T.astype(BF)


def prepare_weights(r):
    for c in range(16):
        r.wrows[pl.ds(c, 27, stride=16)] = r.wf_in[c].astype(F32).T
    for i in range(3):
        r.wf[pl.ds(16 * i, 16)] = r.wrows[pl.ds(144 * i, 144)].T.astype(BF)
        down = [r.wd_in[9 * i + jk].astype(F32) for jk in range(9)]
        up = [r.wu_in[9 * i + jk].astype(F32).T for jk in range(9)]
        down_back = [r.wd_in[26 - 9 * i - jk].astype(F32).T for jk in range(9)]
        up_back = [r.wu_in[26 - 9 * i - jk].astype(F32) for jk in range(9)]
        fold(r.wd, i, down)
        fold(r.wu, i, up)
        fold(r.wdt, i, down_back)
        fold(r.wut, i, up_back)


def arrange_volume(r):
    spot = lane_of(16) % 64

    def plane(x, edges):
        low, high = edges
        for t, tile in enumerate(plane_rows(r.vol[:, x])):
            r.v[x, t] = tile
            wide = tile.astype(F32)
            at = t * 8 + x
            low = jnp.where(spot == at, turn(wide, at), low)
            high = jnp.where(spot == at, turn(wide, at - 63), high)
        return low, high

    zero = jnp.zeros((16, LANES), F32)
    low, high = lax.fori_loop(0, 8, plane, (zero, zero))
    r.ve[0] = low.astype(BF)
    r.ve[1] = high.astype(BF)


def arrange_cotangent(r):
    def plane(x, _):
        for t, tile in enumerate(plane_rows(r.cot[:, x])):
            r.ct[x, t] = tile
        return 0

    lax.fori_loop(0, 8, plane, 0)
    sums = pool_matrix()
    r.sums[...] = sums
    for x in range(4):
        for half in range(2):
            r.pg[x, half] = pool_tile(r.ct, sums, x, half).astype(BF)


def fine_forward(r):
    spot = lane_of(16) % 64

    def rows(x, _):
        dx, sx = (x + 7) // 8, lax.rem(x + 7, 8)
        stacks = []
        for t in range(10):
            dy, sy = (t + 7) // 8, (t + 7) % 8
            at = sy * 8 + sx
            tile = r.vp[x, t].astype(F32)
            left = turn(r.vel[dx, dy].astype(F32), -at)
            right = turn(r.ver[dx, dy].astype(F32), 63 - at)
            before = jnp.where(spot == 0, left, turn(tile, 1))
            after = jnp.where(spot == 63, right, turn(tile, -1))
            stacks.append(jnp.concatenate([before, tile, after], axis=0))
        for t in range(9):
            if t > 0:
                r.v3[x, 2 * t - 1] = stacks[t].astype(BF)
            r.v3[x, 2 * t] = between(stacks[t], stacks[t + 1]).astype(BF)
        return 0

    lax.fori_loop(0, 10, rows, 0)
    weight = r.wf[...]

    def convs(g, _):
        for x, pre in conv(weight, r.v3, 8, (4 * g, 4 * g + 2)):
            act = (pre * sigmoid(pre)).astype(BF)
            for b in range(2):
                r.pre[x, 2 * g + b] = pre[:, b * LANES : (b + 1) * LANES]
                r.act[x, 2 * g + b] = act[:, b * LANES : (b + 1) * LANES]
        return 0

    lax.fori_loop(0, 4, convs, 0)

    sums = r.sums[...]
    lane = lane_of(32)
    low = jnp.zeros((32, LANES), F32)
    high = low
    for x in range(4):
        for half in range(2):
            pooled = (pool_tile(r.act, sums, x, half) * 0.125).astype(BF)
            tile = jnp.concatenate([pooled, r.pg[x, half]], axis=0)
            r.m[x, half] = tile
            wide = tile.astype(F32)
            for q in range(4):
                at = (q % 2) * 64 + (x * 4 + 2 * half + q // 2) * 4
                here = (lane >= at) & (lane < at + 4)
                low = jnp.where(here, turn(wide, at - 32 * q), low)
                high = jnp.where(here, turn(wide, at - 32 * q - 28), high)
    r.me[0] = low.astype(BF)
    r.me[1] = high.astype(BF)


def mid_forward(r, sizes):
    nx, ny, nz = sizes
    gx, gy, gz = position()
    lane = lane_of(32)
    spot = lane % 64

    def rows(x, _):
        dx, sx = x // 4, lax.rem(x, 4)
        pairs = []
        for a in range(8):
            dy, sy = (a + 2) // 4, (a + 2) % 4
            tile = r.mp[x, a // 2].astype(F32)
            q = 2 * (a % 2)
            base = jnp.where(lane < 64, turn(tile, 8 - 32 * q), turn(tile, 40 - 32 * q))
            at = (sx * 4 + sy) * 4
            right = turn(r.mer[dx, dy].astype(F32), 40 - at)
            left = turn(r.mel[dx, dy].astype(F32), 4 - at)
            row = jnp.where(spot < 44, right, 0.0)
            row = jnp.where(spot < 40, base, row)
            row = jnp.where(spot < 8, left, row)
            row = jnp.where(spot < 4, 0.0, row)
            r.pgp[x, a] = row[16:].astype(BF)
            pairs.append(row[:16])
        store_taps(r.pm3, x, pairs)
        r.pm3[x, 15] = jnp.zeros((48, LANES), BF)
        r.pm3[x, 16] = jnp.zeros((48, LANES), BF)
        return 0

    lax.fori_loop(0, 12, rows, 0)
    weight = r.wd[...]
    cell = spot - 8
    mid = cell + gz * 32
    inside = (cell >= -3) & (cell < 35) & (mid >= 0) & (mid < 32 * nz)
    second = lane // 64

    def convs(g, _):
        for x, both in conv(weight, r.pm3, 10, (4 * g, 4 * g + 2)):
            at_x = gx * 4 + x - 3
            for b in range(2):
                pre = both[:, b * LANES : (b + 1) * LANES]
                at_y = gy * 8 + 4 * g + 2 * b - 3 + second
                keep = inside & (at_y >= 0) & (at_y < 8 * ny)
                keep = keep & (at_x >= 0) & (at_x < 4 * nx)
                sig = sigmoid(pre)
                r.am[x, 2 * g + b] = jnp.where(keep, pre * sig, 0.0).astype(BF)
                r.dsm[x, 2 * g + b] = jnp.where(keep, slope(pre, sig), 0.0).astype(BF)
        return 0

    lax.fori_loop(0, 4, convs, 0)
    halves = [
        jnp.concatenate([r.am[3 + a, 1 + 2 * h + m] for a in range(4) for m in range(3)], axis=1)
        for h in range(2)
    ]
    cells = jnp.concatenate(halves + [jnp.zeros((64, 12 * LANES), BF)], axis=0)
    col = lax.broadcasted_iota(jnp.int32, (8, 12 * LANES), 1)
    third, upper = col // LANES % 3, col // 64 % 2
    hit = coarse_sum_matrix(12) & ((third == 1) | ((third == 0) == (upper == 1)))
    pooled = dot_nt(jnp.where(hit, 1.0, 0.0).astype(BF), cells) * (1.0 / 64.0)
    r.pc[...] = pooled.astype(BF).astype(F32)


def near_rows(sizes, count):
    ny = sizes[1]
    have = min(count, ny)
    start = lax.axis_index("gy") - count // 2
    return jnp.minimum(jnp.maximum(start, 0), ny - have), have


def lift_row(r, sizes, y):
    for x in range(sizes[0]):
        for y2 in range(2):
            pre = dot(r.pcg[y, x], r.wide_lift[y2])
            act = (pre * sigmoid(pre)).astype(BF)
            r.alc[x, y, y2] = act
            store_coarse_taps(r.al3, (x + 1, 2 * y + y2 + 1), act.astype(F32))


def coarse_forward(r, sizes, y, have):
    nx, cells = sizes[0], 8 * sizes[2]
    rows = nx * 2 * have * cells
    for i in range(3):
        for j in range(3):
            block = r.al3[pl.ds(i, nx), pl.ds(2 * y + j, 2 * have)].reshape(rows, 768)
            part = dot(block, r.wc[3 * i + j])
            if i + j == 0:
                r.acc[pl.ds(0, rows)] = part
            else:
                r.acc[pl.ds(0, rows)] += part
    per = 2 * have * cells
    for x in range(nx):
        pre = r.acc[pl.ds(x * per, per)]
        sig = sigmoid(pre)
        r.actc[x, pl.ds(y, have)] = (pre * sig).astype(BF).reshape(have, 2, cells, 256)
        r.dsc[x, pl.ds(y, have)] = slope(pre, sig).astype(BF).reshape(have, 2, cells, 256)


def up_forward(r, sizes, scale):
    cells = 8 * sizes[2]
    gz = lax.axis_index("gz")
    start, have = near_rows(sizes, 5)

    def lift(o, _):
        lift_row(r, sizes, start + o)
        return 0

    lax.fori_loop(0, have, lift, 0)
    coarse_forward(r, sizes, *near_rows(sizes, 3))

    spread = coarse_grow_matrix(cells, gz)
    for dx, dy, x, y, y2, keep in near_cells(sizes):
        out = dot_nt(r.wp[...], r.actc[x, y, y2]).astype(BF)
        r.cos[dx, dy] = dot(out, spread) * keep

    first = lane_of(32) < 64

    def join(x, _):
        pairs = []
        for m in range(7):
            lower = r.cos[(x + 1) // 4, (2 * m + 1) // 4]
            upper = r.cos[(x + 1) // 4, (2 * m + 2) // 4]
            row = r.am[x, m].astype(F32) + jnp.where(first, lower, upper)
            pairs.append(row.astype(BF).astype(F32))
        store_taps(r.j3, x, pairs)
        return 0

    lax.fori_loop(0, 10, join, 0)

    cell = lane_of(16) % 64 - 8
    near = (cell >= -2) & (cell < 34)
    weight = r.wu[...]

    def up(g, _):
        for x, both in conv(weight, r.j3, 8, (4 * g, 4 * g + 2)):
            for b in range(2):
                pre = both[:, b * LANES : (b + 1) * LANES]
                sig = sigmoid(pre)
                r.su[x, 2 * g + b] = (pre * sig).astype(BF)
                pooled = r.pgp[x + 2, 2 * g + b + 1].astype(F32) * scale
                grad = jnp.where(near, pooled * slope(pre, sig), 0.0)
                r.guo[x, 2 * g + b] = grad.astype(BF)
        return 0

    lax.fori_loop(0, 3, up, 0)

    def stack(x, _):
        store_taps(r.gu3, x, [r.guo[x, m].astype(F32) for m in range(6)])
        return 0

    lax.fori_loop(0, 8, stack, 0)

    weight_t = r.wut[...]
    for starts in ((0, 2), (4, 6), (8,)):
        for x, both in conv(weight_t, r.gu3, 6, starts):
            for b, y in enumerate(starts):
                r.gj[x, y // 2] = both[:, b * LANES : (b + 1) * LANES]

    totals = []
    for h in range(2):
        total = None
        for a in range(4):
            lower, middle, upper = [r.gj[1 + a, 2 * h + m] for m in range(3)]
            row = middle + jnp.where(first, upper, lower)
            total = row if total is None else total + row
        totals.append(total)
    total = jnp.concatenate(totals + [jnp.zeros((64, LANES), F32)], axis=0)
    head = total.astype(BF)
    tail = (total - head.astype(F32)).astype(BF)
    sums = jnp.where(coarse_sum_matrix(1), 1.0, 0.0).astype(BF)
    r.gc[...] = (dot_nt(sums, head) + dot_nt(sums, tail)).astype(BF).astype(F32)


def up_taps(r):
    cell = lane_of(16) % 64 - 8
    own = (cell >= 0) & (cell < 32)
    r.accu[...] = jnp.zeros(r.accu.shape, F32)
    grads = [
        jnp.concatenate(
            [jnp.where(own, r.guo[x + 2, m + 1].astype(F32), 0.0) for m in range(4)], axis=1
        ).astype(BF)
        for x in range(4)
    ]
    none = jnp.zeros((16, 4 * LANES), BF)
    for x in range(6):
        left = [grads[x - i] if 0 <= x - i < 4 else none for i in range(3)]
        right = [three(r.j3, x + 2, 2 * m + 2) for m in range(4)]
        r.accu[:, pl.ds(0, 288)] += dot_nt(
            jnp.concatenate(left, axis=0), jnp.concatenate(right, axis=1)
        )


def decode(r):
    grow = grow_matrix()

    def plane(x, _):
        rows = jnp.concatenate([r.su[x + 2, m + 1] for m in range(4)], axis=0)
        grown = dot(rows, grow)
        for a in range(2):
            for t in range(8):
                add = grown[16 * (t // 2) : 16 * (t // 2) + 16, (t % 2) * LANES :][:, :LANES]
                tile = r.act[2 * x + a, t].astype(F32) + add
                r.plane[2 * t] = tile.astype(BF)
                r.plane[2 * t + 1] = turn(tile, 64).astype(BF)
            r.dec[:, 2 * x + a] = jnp.swapaxes(r.plane[...], 0, 1)[:, :, :64]
        return 0

    lax.fori_loop(0, 4, plane, 0)


def coarse_grad_row(r, sizes, y):
    for x in range(sizes[0]):
        for y2 in range(2):
            grad = dot(r.gcg[y, x], r.wide_proj[y2]) * r.dsc[x, y, y2].astype(F32)
            grad = grad.astype(BF).astype(F32)
            store_coarse_taps(r.gp3, (x + 2, 2 * y + y2 + 2), grad)


def pay_rows(r, start, block):
    per = r.pay.shape[1]
    done = 0
    while done < block.shape[0]:
        part, at = divmod(start + done, per)
        size = min(per - at, block.shape[0] - done)
        r.pay[part, pl.ds(at, size)] = block[done : done + size]
        done += size


def backward(r, sizes, scale):
    cells = 8 * sizes[2]
    gx, gy, gz = position()
    start, have = near_rows(sizes, 3)

    def coarse(o, _):
        coarse_grad_row(r, sizes, start + o)
        return 0

    lax.fori_loop(0, have, coarse, 0)
    rows = 12 * cells
    for i in range(3):
        for j in range(3):
            block = r.gp3[pl.ds(gx + i, 3), pl.ds(2 * gy + j, 4)].reshape(rows, 768)
            part = dot(block, r.wct[3 * i + j])
            if i + j == 0:
                r.acc[pl.ds(0, rows)] = part
            else:
                r.acc[pl.ds(0, rows)] += part

    spread = coarse_grow_matrix(cells, gz)
    own = lax.broadcasted_iota(jnp.int32, (cells, 256), 0) // 8 == gz
    for at, (dx, dy, x, y, y2, keep) in enumerate(near_cells(sizes)):
        pre = dot(r.pcg[y, x], r.wide_lift[y2])
        grad = (r.acc[pl.ds(at * cells, cells)] * slope(pre, sigmoid(pre))).astype(BF)
        out = dot_nt(r.wl[...], grad).astype(BF)
        r.cos[dx, dy] = dot(out, spread) * (keep * (1.0 / 64.0))
        if dx == 1 and dy in (1, 2):
            masked = jnp.where(own, grad.astype(F32), 0.0).astype(BF)
            r.pairs[y2] = dot_tn(r.pcg[y, x], masked)
    lifts = r.pairs[0, :32] + r.pairs[1, 32:64]
    for b in range(2):
        pay_rows(r, 432 + 32 * b, lifts[:, b * LANES : (b + 1) * LANES])

    first = lane_of(32) < 64

    def join(x, _):
        pairs = []
        for n in range(5):
            lower = r.cos[(x + 3) // 4, (2 * n + 3) // 4]
            upper = r.cos[(x + 3) // 4, (2 * n + 4) // 4]
            row = r.gj[x, n] + jnp.where(first, lower, upper)
            row = row * r.dsm[x + 2, n + 1].astype(F32)
            pairs.append(row.astype(BF).astype(F32))
        store_taps(r.gm3, x, pairs)
        return 0

    lax.fori_loop(0, 6, join, 0)

    weight_t = r.wdt[...]
    for starts in ((0, 2), (4, 6)):
        for x, both in conv(weight_t, r.gm3, 4, starts):
            for b, y in enumerate(starts):
                r.gpm[x, pl.ds(8 * y, 16)] = both[:, b * LANES : (b + 1) * LANES].astype(BF)

    grow = grow_matrix()
    for x in (0, 1, 10, 11):
        r.gf[x] = jnp.zeros(r.gf.shape[1:], BF)

    def fine(x, _):
        grown = dot(r.gpm[x], grow) * 0.125
        for a in range(2):
            for t in range(8):
                add = grown[16 * (t // 2) : 16 * (t // 2) + 16, (t % 2) * LANES :][:, :LANES]
                pre = r.pre[2 * x + a, t]
                grad = r.ct[2 * x + a, t].astype(F32) * scale + add
                grad = (grad * slope(pre, sigmoid(pre))).astype(BF)
                r.gf[2 * x + a + 2, :, pl.ds(t * LANES, LANES)] = grad
        return 0

    lax.fori_loop(0, 4, fine, 0)

    r.accd[...] = jnp.zeros(r.accd.shape, F32)
    spot = lane_of(32) % 64
    inner = (spot >= 8) & (spot < 40)
    grads = [
        jnp.concatenate(
            [
                jnp.where(inner, r.gm3[x + 1, 2 * m + 1, pl.ds(32, 32)].astype(F32), 0.0)
                for m in range(4)
            ],
            axis=1,
        ).astype(BF)
        for x in range(4)
    ]
    none = jnp.zeros((32, 4 * LANES), BF)
    for x in range(6):
        left = [grads[x - i] if 0 <= x - i < 4 else none for i in range(3)]
        right = [three(r.pm3, x + 3, 2 * m + 3) for m in range(4)]
        r.accd[:, pl.ds(0, 144)] += dot_nt(
            jnp.concatenate(left, axis=0), jnp.concatenate(right, axis=1)
        )

    r.accf[...] = jnp.zeros(r.accf.shape, F32)

    def taps_fine(x, _):
        left = jnp.concatenate([r.gf[x + 2 - i] for i in range(3)], axis=0)
        right = jnp.concatenate([three(r.v3, x, 2 * t) for t in range(8)], axis=1)
        r.accf[:, pl.ds(0, 144)] += dot_nt(left, right)
        return 0

    lax.fori_loop(0, 10, taps_fine, 0)

    for b in range(2):
        pay_rows(r, 48 * b, r.accf[:, b * LANES : (b + 1) * LANES])
    for b in range(3):
        pay_rows(r, 96 + 48 * b, r.accu[:, b * LANES : (b + 1) * LANES])
    for b in range(2):
        pay_rows(r, 240 + 96 * b, r.accd[:, b * LANES : (b + 1) * LANES])
    pay_rows(r, 496, jnp.zeros((16, LANES), F32))


def coarse_taps(r, sizes, first, last):
    nx, ny, nz = sizes
    count = nx * ny * 16 * nz

    def taps(t, _):
        i, j = t // 3, lax.rem(t, 3)
        block = r.gp3[pl.ds(3 - i, nx), pl.ds(3 - j, 2 * ny)].reshape(count, 768)
        out = dot(r.cells_t[...], block)
        for k in range(3):
            r.gwc[3 * t + k] = out[:, 256 * (2 - k) : 256 * (3 - k)].astype(BF)
        return 0

    lax.fori_loop(first, last, taps, 0)


def proj_grad(r, sizes):
    nx, ny, nz = sizes
    cells = 8 * nz
    r.pairs[...] = jnp.zeros(r.pairs.shape, F32)

    def plane(x, _):
        for y2 in range(2):
            grads = r.gcg[:, x].reshape(ny * cells, LANES)
            r.pairs[y2] += dot_tn(grads, r.actc[x, :, y2].reshape(ny * cells, 256))
        return 0

    lax.fori_loop(0, nx, plane, 0)
    r.gwp[...] = r.pairs[0, :32] + r.pairs[1, 32:64]


def step_kernel(sizes, scale, names, *refs):
    nx, ny, nz = sizes
    count = nx * ny * 16 * nz
    r = types.SimpleNamespace(**dict(zip(names, refs, strict=True)))
    fetch = pltpu.make_async_copy(r.wc_in, r.wc, r.fetched)
    fetch.start()
    greet(sizes, lambda: arrange_volume(r))

    def first_wait():
        prepare_weights(r)
        arrange_cotangent(r)
        place_weight(r.wide_lift, r.wl[...])
        place_weight(r.wide_proj, r.wp[...])

    halo_round(sizes, 1, 1, (r.v, r.ve, r.vp, r.ver, r.vel, r.vsend, r.vrecv), first_wait)
    fine_forward(r)

    def second_wait():
        zero_rim(r.al3, 1)
        zero_rim(r.gp3, 2)
        fetch.wait()

        def turn_weights(t, _):
            for k in range(3):
                block = r.wc[8 - t, pl.ds(256 * (2 - k), 256)]
                r.wct[t, pl.ds(256 * k, 256)] = block.T
            return 0

        lax.fori_loop(0, 9, turn_weights, 0)

    halo_round(sizes, 4, 1, (r.m, r.me, r.mp, r.mer, r.mel, r.msend, r.mrecv), second_wait)
    mid_forward(r, sizes)
    sems = (r.ga_send, r.ga_recv, r.gb_send, r.gb_recv)
    gather_round(sizes, (r.pc, r.pcg, r.pstage) + sems, nothing, nothing)
    up_forward(r, sizes, scale)

    def third_wait():
        up_taps(r)
        decode(r)

    def fourth_wait():
        start, have = near_rows(sizes, 5)

        def lift(o, _):
            lift_row(r, sizes, lax.rem(start + o, ny))
            return 0

        lax.fori_loop(have, ny, lift, 0)
        start_c, have_c = near_rows(sizes, 3)

        def coarse(o, _):
            coarse_forward(r, sizes, lax.rem(start_c + o, ny), 1)
            return 0

        lax.fori_loop(have_c, ny, coarse, 0)

    sems = (r.ha_send, r.ha_recv, r.hb_send, r.hb_recv)
    gather_round(sizes, (r.gc, r.gcg, r.gstage) + sems, third_wait, fourth_wait)
    backward(r, sizes, scale)

    def store(part, first, last):
        taps = pl.ds(3 * first, 3 * (last - first))
        return pltpu.make_async_copy(r.gwc.at[taps], r.gwc_out.at[taps], r.stored.at[part])

    ends = (0, 2, 5, 9)

    def taps_wait(part):
        def wait():
            if part == 0:
                start, have = near_rows(sizes, 3)

                def coarse(o, _):
                    coarse_grad_row(r, sizes, lax.rem(start + o, ny))
                    return 0

                lax.fori_loop(have, ny, coarse, 0)
                r.cells_t[...] = r.alc[...].reshape(count, 256).T
            coarse_taps(r, sizes, ends[part], ends[part + 1])
            store(part, ends[part], ends[part + 1]).start()
            if part == 2:
                proj_grad(r, sizes)

        return wait

    sems = (r.ra_send, r.ra_recv, r.rb_send, r.rb_recv, r.rc_send, r.rc_recv)
    reduce_round(sizes, (r.pay, r.red, r.ra, r.rb) + sems, [taps_wait(part) for part in range(3)])
    for part in range(3):
        store(part, ends[part], ends[part + 1]).wait()


def last_kernel(gwc_ref, red_ref, gwp_ref, wc_out, wf_out, wd_out, wl_out, wp_out, wu_out, rows):
    step = pl.program_id(0)

    def columns(start, blocks, count):
        return jnp.concatenate(
            [red_ref[pl.ds(start + count * b, count)] for b in range(blocks)], axis=1
        )

    @pl.when(step == 0)
    def _():
        table = columns(0, 2, 48)
        for i in range(3):
            rows[pl.ds(144 * i, 144)] = table[16 * i : 16 * i + 16, :144].T
        for c in range(16):
            wf_out[c] = rows[pl.ds(c, 27, stride=16)].T

    @pl.when(step == 1)
    def _():
        table = columns(96, 3, 48)
        for i in range(3):
            for jk in range(9):
                tile = table[16 * i : 16 * i + 16, 32 * jk : 32 * jk + 32]
                wu_out[9 * i + jk] = tile

    @pl.when(step == 2)
    def _():
        table = columns(240, 2, 96)
        for i in range(3):
            part = table[32 * i : 32 * i + 32, :144]
            wd_out[pl.ds(9 * i, 9)] = part.T.reshape(9, 16, 32)

    @pl.when(step == 3)
    def _():
        wl_out[...] = columns(432, 2, 32)
        wp_out[...] = gwp_ref[...]

    wc_out[...] = gwc_ref[...].astype(F32)


VMEM = pl.BlockSpec(memory_space=pltpu.VMEM)
HBM = pl.BlockSpec(memory_space=pl.ANY)


def shards(sizes, volume, w_fine, w_down, w_lift, w_coarse, w_proj, w_up, cotangent):
    nx, ny, nz = sizes
    scale = 1.0 / math.sqrt(8 * nx * 16 * ny * 64 * nz)
    cells = 8 * nz
    parts = nx * nz
    per = 512 // parts
    grid = (nx, ny, 2, cells, 256)
    gathered = (ny, nx, cells, LANES)
    ins = {
        "vol": volume,
        "cot": cotangent,
        "wf_in": jnp.transpose(w_fine, (1, 2, 0)),
        "wd_in": w_down,
        "wu_in": jnp.transpose(w_up, (0, 2, 1)),
        "wl": w_lift,
        "wp": jnp.transpose(w_proj),
        "wc_in": w_coarse.reshape(9, 768, 256),
    }
    outs = {
        "dec": ((16, 8, 16, 64), BF),
        "red": ((parts, per, LANES), F32),
        "gwp": ((32, 256), F32),
        "gwc_out": ((27, 256, 256), BF),
    }
    narrow = {
        "v": (8, 8, 16, LANES),
        "ve": (2, 16, LANES),
        "vp": (10, 10, 16, LANES),
        "ver": (3, 3, 16, LANES),
        "vel": (3, 3, 16, LANES),
        "ct": (8, 8, 16, LANES),
        "sums": (8 * LANES, LANES),
        "pg": (4, 2, 16, LANES),
        "wf": (48, 144),
        "wd": (96, 144),
        "wu": (48, 288),
        "wdt": (48, 288),
        "wut": (96, 144),
        "v3": (10, 17, 48, LANES),
        "act": (8, 8, 16, LANES),
        "m": (4, 2, 32, LANES),
        "me": (2, 32, LANES),
        "mp": (12, 4, 32, LANES),
        "mer": (3, 3, 32, LANES),
        "mel": (3, 3, 32, LANES),
        "pm3": (12, 17, 48, LANES),
        "pgp": (12, 8, 16, LANES),
        "am": (10, 8, 32, LANES),
        "dsm": (10, 8, 32, LANES),
        "pcg": gathered,
        "gcg": gathered,
        "wc": (9, 768, 256),
        "wct": (9, 768, 256),
        "wide_lift": (2, LANES, 256),
        "wide_proj": (2, LANES, 256),
        "al3": (nx + 2, 2 * ny + 2, cells, 768),
        "gp3": (nx + 4, 2 * ny + 4, cells, 768),
        "alc": grid,
        "actc": grid,
        "dsc": grid,
        "j3": (10, 13, 96, LANES),
        "guo": (8, 6, 16, LANES),
        "gu3": (8, 11, 48, LANES),
        "su": (8, 6, 16, LANES),
        "plane": (16, 16, LANES),
        "gm3": (6, 9, 96, LANES),
        "gpm": (4, 64, LANES),
        "gf": (12, 16, 8 * LANES),
        "cells_t": (256, nx * ny * 2 * cells),
        "gwc": (27, 256, 256),
    }
    wide = {
        "wrows": (432, 16),
        "pre": (8, 8, 16, LANES),
        "pc": (8, LANES),
        "pstage": (nx, cells, LANES),
        "acc": (max(nx * 2 * min(3, ny), 12) * cells, 256),
        "cos": (3, 4, 32, LANES),
        "gj": (6, 5, 32, LANES),
        "gc": (8, LANES),
        "gstage": (nx, cells, LANES),
        "accu": (48, 3 * LANES),
        "accf": (48, 2 * LANES),
        "accd": (96, 2 * LANES),
        "pairs": (2, LANES, 256),
        "pay": (parts, per, LANES),
        "ra": (parts, per, LANES),
        "rb": (ny, per, LANES),
    }
    sems = {
        "vsend": 26,
        "vrecv": 26,
        "msend": 26,
        "mrecv": 26,
        "ga_send": parts,
        "ga_recv": parts,
        "gb_send": ny,
        "gb_recv": ny,
        "ha_send": parts,
        "ha_recv": parts,
        "hb_send": ny,
        "hb_recv": ny,
        "ra_send": parts,
        "ra_recv": parts,
        "rb_send": ny,
        "rb_recv": ny,
        "rc_send": parts,
        "rc_recv": parts,
        "stored": 3,
    }
    names = list(ins) + list(outs) + list(narrow) + list(wide) + list(sems) + ["fetched"]
    dec, red, gwp, gwc = pl.pallas_call(
        functools.partial(step_kernel, sizes, scale, names),
        out_shape=[jax.ShapeDtypeStruct(shape, kind) for shape, kind in outs.values()],
        in_specs=[VMEM] * (len(ins) - 1) + [HBM],
        out_specs=[VMEM] * (len(outs) - 1) + [HBM],
        scratch_shapes=[pltpu.VMEM(shape, BF) for shape in narrow.values()]
        + [pltpu.VMEM(shape, F32) for shape in wide.values()]
        + [pltpu.SemaphoreType.DMA((size,)) for size in sems.values()]
        + [pltpu.SemaphoreType.DMA],
        compiler_params=pltpu.CompilerParams(
            vmem_limit_bytes=62 * 1024 * 1024, collective_id=1, has_side_effects=True
        ),
    )(*ins.values())
    shapes = [(27, 256, 256), (16, 16, 27), (27, 16, 32), (32, 256), (32, 256), (27, 16, 32)]

    def whole(shape):
        return pl.BlockSpec(shape, lambda t: (0,) * len(shape))

    block = pl.BlockSpec((3, 256, 256), lambda t: (t, 0, 0))
    gwc, gwf, gwd, gwl, gwp, gwu = pl.pallas_call(
        last_kernel,
        grid=(9,),
        out_shape=[jax.ShapeDtypeStruct(shape, F32) for shape in shapes],
        in_specs=[block, whole((512, LANES)), whole((32, 256))],
        out_specs=[block] + [whole(shape) for shape in shapes[1:]],
        scratch_shapes=[pltpu.VMEM((432, 16), F32)],
        compiler_params=pltpu.CompilerParams(dimension_semantics=("arbitrary",)),
    )(gwc, red.reshape(512, LANES), gwp)
    gwf = jnp.transpose(gwf, (2, 0, 1))
    gwu = jnp.transpose(gwu, (0, 2, 1))
    return dec, gwf, gwd, gwl, gwc, jnp.transpose(gwp), gwu


def solution(mesh):
    sizes = tuple(mesh.shape[name] for name in ("gx", "gy", "gz"))
    block = P(None, "gx", "gy", "gz")
    return jax.shard_map(
        functools.partial(shards, sizes),
        mesh=mesh,
        in_specs=(block, P(), P(), P(), P(), P(), P(), block),
        out_specs=(block, P(), P(), P(), P(), P(), P()),
        check_vma=False,
    )
```

```python
import functools
import math
import types

import jax
import jax.numpy as jnp
from jax import lax
from jax.experimental import pallas as pl
from jax.experimental.pallas import tpu as pltpu
from jax.sharding import PartitionSpec as P

BF = jnp.bfloat16
F32 = jnp.float32
MESH = pl.DeviceIdType.MESH
LANES = 128


def dot(left, right):
    return jnp.dot(left, right, preferred_element_type=F32)


def dot_nt(left, right):
    return lax.dot_general(left, right, (((1,), (1,)), ((), ())), preferred_element_type=F32)


def dot_tn(left, right):
    return lax.dot_general(left, right, (((0,), (0,)), ((), ())), preferred_element_type=F32)


def sigmoid(values):
    return 0.5 * jnp.tanh(0.5 * values) + 0.5


def slope(values, sig):
    return sig * (1.0 + values * (1.0 - sig))


def lane_of(rows):
    return lax.broadcasted_iota(jnp.int32, (rows, LANES), 1)


def turn(tile, by):
    if isinstance(by, int):
        by = by % LANES
        return tile if by == 0 else pltpu.roll(tile, by, 1)
    return pltpu.roll(tile, lax.rem(by + 4 * LANES, LANES), 1)


def tap_rows(pair):
    return jnp.concatenate([turn(pair, 1), pair, turn(pair, -1)], axis=0)


def between(lower, upper):
    lane = lane_of(lower.shape[0])
    return jnp.where(lane < 64, turn(lower, 64), turn(upper, 64))


def store_taps(ref, x, pairs):
    stacks = [tap_rows(pair) for pair in pairs]
    for n, stack in enumerate(stacks):
        ref[x, 2 * n] = stack.astype(BF)
        if n + 1 < len(stacks):
            ref[x, 2 * n + 1] = between(stack, stacks[n + 1]).astype(BF)


def three(ref, x, y):
    block = ref[x, pl.ds(y, 3)]
    return block.reshape(3 * block.shape[1], LANES)


def conv(weight, ref, planes, starts):
    outs = weight.shape[0] // 3
    parts = []
    for x in range(planes + 2):
        tiles = [three(ref, x, y) for y in starts]
        block = tiles[0] if len(tiles) == 1 else jnp.concatenate(tiles, axis=1)
        parts.append(dot(weight, block))
        if x >= 2:
            yield (
                x - 2,
                parts[x - 2][:outs] + parts[x - 1][outs : 2 * outs] + parts[x][2 * outs :],
            )


def pool_matrix():
    row = lax.broadcasted_iota(jnp.int32, (8 * LANES, LANES), 0)
    col = lax.broadcasted_iota(jnp.int32, (8 * LANES, LANES), 1)
    hit = (row // 256 == col // 32) & (row % 64 // 2 == col % 32)
    return jnp.where(hit, 1.0, 0.0).astype(BF)


def pool_tiles(ref, sums):
    cells = [
        jnp.concatenate([ref[2 * x + a, 4 * half + q] for q in range(4) for a in range(2)], axis=1)
        for x in range(4)
        for half in range(2)
    ]
    return dot(jnp.concatenate(cells, axis=0), sums)


def grow_matrix():
    row = lax.broadcasted_iota(jnp.int32, (LANES, 2 * LANES), 0)
    col = lax.broadcasted_iota(jnp.int32, (LANES, 2 * LANES), 1)
    hit = (row // 64 == col // LANES) & (row % 64 - 8 == col % 64 // 2)
    return jnp.where(hit, 1.0, 0.0).astype(BF)


def coarse_sum_matrix(tiles):
    row = lax.broadcasted_iota(jnp.int32, (8, tiles * LANES), 0)
    cell = lax.broadcasted_iota(jnp.int32, (8, tiles * LANES), 1) % 64 - 8
    return (cell >= 0) & (cell < 32) & ((cell + 4) // 4 == row + 1)


def coarse_grow_matrix(cells, gz):
    row = lax.broadcasted_iota(jnp.int32, (cells, LANES), 0)
    cell = lax.broadcasted_iota(jnp.int32, (cells, LANES), 1) % 64 - 8
    mid = cell + gz * 32
    hit = (cell >= -3) & (cell < 35) & (mid >= 0) & (row == (mid + 4) // 4 - 1)
    return jnp.where(hit, 1.0, 0.0).astype(BF)


def plane_rows(block):
    rows = jnp.swapaxes(block, 0, 1)
    return [jnp.concatenate([rows[2 * t], rows[2 * t + 1]], axis=1) for t in range(8)]


def place_weight(ref, weight):
    for y2 in range(2):
        ref[y2] = jnp.zeros((LANES, 256), BF)
        ref[y2, pl.ds(32 * y2, 32)] = weight


def store_coarse_taps(ref, at, cells):
    count = cells.shape[0]
    row = lax.broadcasted_iota(jnp.int32, cells.shape, 0)
    before = jnp.where(row > 0, pltpu.roll(cells, 1, 0), 0.0)
    after = jnp.where(row < count - 1, pltpu.roll(cells, count - 1, 0), 0.0)
    ref[at + (slice(None), pl.ds(0, 256))] = before.astype(BF)
    ref[at + (slice(None), pl.ds(256, 256))] = cells.astype(BF)
    ref[at + (slice(None), pl.ds(512, 256))] = after.astype(BF)


def zero_rim(ref, rim):
    planes, rows = ref.shape[:2]

    def clear(x, _):
        for y in list(range(rim)) + list(range(rows - rim, rows)):
            ref[x, y] = jnp.zeros(ref.shape[2:], ref.dtype)
        return 0

    lax.fori_loop(0, planes, clear, 0)

    def clear_plane(y, _):
        for x in list(range(rim)) + list(range(planes - rim, planes)):
            ref[x, y] = jnp.zeros(ref.shape[2:], ref.dtype)
        return 0

    lax.fori_loop(0, rows, clear_plane, 0)


def clamp(at, count):
    return jnp.minimum(jnp.maximum(at, 0), count - 1)


def near_cells(sizes):
    nx, ny, _ = sizes
    gx, gy = lax.axis_index("gx"), lax.axis_index("gy")
    found = []
    for dx in range(3):
        for dy in range(4):
            x, y = gx - 1 + dx, gy + (dy + 1) // 2 - 1
            there = (x >= 0) & (x < nx) & (y >= 0) & (y < ny)
            keep = jnp.where(there, 1.0, 0.0)
            found.append((dx, dy, clamp(x, nx), clamp(y, ny), (dy + 1) % 2, keep))
    return found


def nothing():
    pass


NEIGHBOURS = [
    (dx, dy, dz)
    for dz in (-1, 1, 0)
    for dx in (-1, 0, 1)
    for dy in (-1, 0, 1)
    if (dx, dy, dz) != (0, 0, 0)
]


def position():
    return [lax.axis_index(name) for name in ("gx", "gy", "gz")]


def valid(sizes, steps):
    found = None
    for at, size, step in zip(position(), sizes, steps):
        if step != 0:
            test = at > 0 if step < 0 else at < size - 1
            found = test if found is None else found & test
    return found


def plane_peers(nx, nz):
    return [(ox, oz) for ox in range(nx) for oz in range(nz) if (ox, oz) != (0, 0)]


def greet(sizes, work):
    nx, ny, nz = sizes
    me = gx, gy, gz = position()
    barrier = pltpu.get_barrier_semaphore()
    peers = [(lax.rem(gx + ox, nx), gy, lax.rem(gz + oz, nz)) for ox, oz in plane_peers(nx, nz)]
    peers += [(gx, lax.rem(gy + oy, ny), gz) for oy in range(1, ny)]
    for peer in peers:
        pl.semaphore_signal(barrier, inc=1, device_id=peer, device_id_type=MESH)
    total = 1
    for axis in range(3):
        low = jnp.where(me[axis] > 0, 1, 0)
        high = jnp.where(me[axis] < sizes[axis] - 1, 1, 0)
        total = total * (1 + low + high)
    for steps in NEIGHBOURS:

        @pl.when(valid(sizes, steps))
        def _():
            pl.semaphore_signal(
                barrier,
                inc=1,
                device_id=tuple(me[axis] + steps[axis] for axis in range(3)),
                device_id_type=MESH,
            )

    work()
    pl.semaphore_wait(barrier, total - 1 + len(peers))


def halo_round(sizes, hx, ht, refs, meanwhile):
    a_ref, e_ref, p_ref, er_ref, el_ref, send_sem, recv_sem = refs
    me = [lax.axis_index(name) for name in ("gx", "gy", "gz")]
    planes, tiles = a_ref.shape[:2]

    def part(step, halo, count):
        if step == 0:
            return pl.ds(0, count), pl.ds(halo, count)
        if step > 0:
            return pl.ds(count - halo, halo), pl.ds(0, halo)
        return pl.ds(0, halo), pl.ds(count + halo, halo)

    def copy_of(k, steps):
        dx, dy, dz = steps
        if dz == 0:
            fx, tx = part(dx, hx, planes)
            fy, ty = part(dy, ht, tiles)
            src, dst = a_ref.at[fx, fy], p_ref.at[tx, ty]
        elif dz > 0:
            src, dst = e_ref.at[1], el_ref.at[1 - dx, 1 - dy]
        else:
            src, dst = e_ref.at[0], er_ref.at[1 - dx, 1 - dy]
        return pltpu.make_async_remote_copy(
            src_ref=src,
            dst_ref=dst,
            send_sem=send_sem.at[k],
            recv_sem=recv_sem.at[k],
            device_id=(me[0] + dx, me[1] + dy, me[2] + dz),
            device_id_type=MESH,
        )

    for k, steps in enumerate(NEIGHBOURS):

        @pl.when(valid(sizes, steps))
        def _():
            copy_of(k, steps).start()

    p_ref[pl.ds(hx, planes), pl.ds(ht, tiles)] = a_ref[...]
    for k, steps in enumerate(NEIGHBOURS):
        back = tuple(-step for step in steps)
        dx, dy, dz = steps

        @pl.when(jnp.logical_not(valid(sizes, back)))
        def _():
            if dz == 0:
                _, tx = part(dx, hx, planes)
                _, ty = part(dy, ht, tiles)
                into = p_ref.at[tx, ty]
            elif dz > 0:
                into = el_ref.at[1 - dx, 1 - dy]
            else:
                into = er_ref.at[1 - dx, 1 - dy]
            into[...] = jnp.zeros(into.shape, into.dtype)

    meanwhile()
    for k, steps in enumerate(NEIGHBOURS):
        back = tuple(-step for step in steps)

        @pl.when(valid(sizes, back))
        def _():
            copy_of(k, steps).wait_recv()

    for k, steps in enumerate(NEIGHBOURS):

        @pl.when(valid(sizes, steps))
        def _():
            copy_of(k, steps).wait_send()


def gather_round(sizes, refs, first_wait, second_wait):
    g_ref, all_ref, stage, send_a, recv_a, send_b, recv_b = refs
    nx, ny, nz = sizes
    gx, gy, gz = [lax.axis_index(name) for name in ("gx", "gy", "gz")]
    plane = plane_peers(nx, nz)

    def first(k, x, z, peer):
        return pltpu.make_async_remote_copy(
            src_ref=g_ref,
            dst_ref=stage.at[x, pl.ds(pl.multiple_of(z * 8, 8), 8)],
            send_sem=send_a.at[k],
            recv_sem=recv_a.at[k],
            device_id=peer,
            device_id_type=MESH,
        )

    def second(oy, y):
        return pltpu.make_async_remote_copy(
            src_ref=all_ref.at[gy],
            dst_ref=all_ref.at[y],
            send_sem=send_b.at[oy],
            recv_sem=recv_b.at[oy],
            device_id=(gx, lax.rem(gy + oy, ny), gz),
            device_id_type=MESH,
        )

    for k, (ox, oz) in enumerate(plane):
        first(k, gx, gz, (lax.rem(gx + ox, nx), gy, lax.rem(gz + oz, nz))).start()
    stage[gx, pl.ds(pl.multiple_of(gz * 8, 8), 8)] = g_ref[...]
    first_wait()
    for k, (ox, oz) in enumerate(plane):
        peer = (lax.rem(gx + ox, nx), gy, lax.rem(gz + oz, nz))
        first(k, lax.rem(gx + nx - ox, nx), lax.rem(gz + nz - oz, nz), peer).wait_recv()
    all_ref[gy] = stage[...].astype(BF)
    for oy in range(1, ny):
        second(oy, gy).start()
    second_wait()
    for k, (ox, oz) in enumerate(plane):
        first(k, gx, gz, (lax.rem(gx + ox, nx), gy, lax.rem(gz + oz, nz))).wait_send()
    for oy in range(1, ny):
        second(oy, lax.rem(gy + ny - oy, ny)).wait_recv()
    for oy in range(1, ny):
        second(oy, gy).wait_send()


def reduce_round(sizes, refs, waits):
    pay_ref, out_ref, ra, rb, send_a, recv_a, send_b, recv_b, send_c, recv_c = refs
    nx, ny, nz = sizes
    gx, gy, gz = [lax.axis_index(name) for name in ("gx", "gy", "gz")]
    mine = gx * nz + gz
    plane = plane_peers(nx, nz)

    def ahead(ox, oz):
        return lax.rem(gx + ox, nx), lax.rem(gz + oz, nz)

    def behind(ox, oz):
        return lax.rem(gx + nx - ox, nx), lax.rem(gz + nz - oz, nz)

    def scatter(k, ox, oz, slot):
        x, z = ahead(ox, oz)
        return pltpu.make_async_remote_copy(
            src_ref=pay_ref.at[x * nz + z],
            dst_ref=ra.at[slot],
            send_sem=send_a.at[k],
            recv_sem=recv_a.at[k],
            device_id=(x, gy, z),
            device_id_type=MESH,
        )

    def across(oy, slot):
        return pltpu.make_async_remote_copy(
            src_ref=rb.at[gy],
            dst_ref=rb.at[slot],
            send_sem=send_b.at[oy],
            recv_sem=recv_b.at[oy],
            device_id=(gx, lax.rem(gy + oy, ny), gz),
            device_id_type=MESH,
        )

    def spread(k, ox, oz, slot):
        x, z = ahead(ox, oz)
        return pltpu.make_async_remote_copy(
            src_ref=out_ref.at[mine],
            dst_ref=out_ref.at[slot],
            send_sem=send_c.at[k],
            recv_sem=recv_c.at[k],
            device_id=(x, gy, z),
            device_id_type=MESH,
        )

    for k, (ox, oz) in enumerate(plane):
        scatter(k, ox, oz, mine).start()
    ra[mine] = pay_ref[mine]
    waits[0]()
    for k, (ox, oz) in enumerate(plane):
        x, z = behind(ox, oz)
        scatter(k, ox, oz, x * nz + z).wait_recv()
    rb[gy] = jnp.sum(ra[...], axis=0)
    for oy in range(1, ny):
        across(oy, gy).start()
    waits[1]()
    for k, (ox, oz) in enumerate(plane):
        scatter(k, ox, oz, mine).wait_send()
    for oy in range(1, ny):
        across(oy, lax.rem(gy + ny - oy, ny)).wait_recv()
    out_ref[mine] = jnp.sum(rb[...], axis=0)
    for k, (ox, oz) in enumerate(plane):
        spread(k, ox, oz, mine).start()
    waits[2]()
    for oy in range(1, ny):
        across(oy, gy).wait_send()
    for k, (ox, oz) in enumerate(plane):
        x, z = behind(ox, oz)
        spread(k, ox, oz, x * nz + z).wait_recv()
    for k, (ox, oz) in enumerate(plane):
        spread(k, ox, oz, mine).wait_send()


def fold(ref, i, tiles):
    block = jnp.concatenate(tiles, axis=0)
    outs = block.shape[1]
    ref[pl.ds(i * outs, outs)] = block.T.astype(BF)


def prepare_weights(r):
    for c in range(16):
        r.wrows[pl.ds(c, 27, stride=16)] = r.wf_in[c].astype(F32).T
    for i in range(3):
        r.wf[pl.ds(16 * i, 16)] = r.wrows[pl.ds(144 * i, 144)].T.astype(BF)
        down = [r.wd_in[9 * i + jk].astype(F32) for jk in range(9)]
        up = [r.wu_in[9 * i + jk].astype(F32).T for jk in range(9)]
        down_back = [r.wd_in[26 - 9 * i - jk].astype(F32).T for jk in range(9)]
        up_back = [r.wu_in[26 - 9 * i - jk].astype(F32) for jk in range(9)]
        fold(r.wd, i, down)
        fold(r.wu, i, up)
        fold(r.wdt, i, down_back)
        fold(r.wut, i, up_back)


def arrange_volume(r):
    spot = lane_of(16) % 64

    def plane(x, edges):
        low, high = edges
        for t, tile in enumerate(plane_rows(r.vol[:, x])):
            r.v[x, t] = tile
            wide = tile.astype(F32)
            at = t * 8 + x
            low = jnp.where(spot == at, turn(wide, at), low)
            high = jnp.where(spot == at, turn(wide, at - 63), high)
        return low, high

    zero = jnp.zeros((16, LANES), F32)
    low, high = lax.fori_loop(0, 8, plane, (zero, zero))
    r.ve[0] = low.astype(BF)
    r.ve[1] = high.astype(BF)


def arrange_cotangent(r):
    def plane(x, _):
        for t, tile in enumerate(plane_rows(r.cot[:, x])):
            r.ct[x, t] = tile
        return 0

    lax.fori_loop(0, 8, plane, 0)
    sums = pool_matrix()
    r.sums[...] = sums
    r.pg[...] = pool_tiles(r.ct, sums).astype(BF).reshape(4, 2, 16, LANES)


def fine_forward(r):
    spot = lane_of(16) % 64

    def rows(x, _):
        dx, sx = (x + 7) // 8, lax.rem(x + 7, 8)
        stacks = []
        for t in range(10):
            dy, sy = (t + 7) // 8, (t + 7) % 8
            at = sy * 8 + sx
            tile = r.vp[x, t].astype(F32)
            left = turn(r.vel[dx, dy].astype(F32), -at)
            right = turn(r.ver[dx, dy].astype(F32), 63 - at)
            before = jnp.where(spot == 0, left, turn(tile, 1))
            after = jnp.where(spot == 63, right, turn(tile, -1))
            stacks.append(jnp.concatenate([before, tile, after], axis=0))
        for t in range(9):
            if t > 0:
                r.v3[x, 2 * t - 1] = stacks[t].astype(BF)
            r.v3[x, 2 * t] = between(stacks[t], stacks[t + 1]).astype(BF)
        return 0

    lax.fori_loop(0, 10, rows, 0)
    weight = r.wf[...]

    def convs(g, _):
        for x, pre in conv(weight, r.v3, 8, (4 * g, 4 * g + 2)):
            act = (pre * sigmoid(pre)).astype(BF)
            for b in range(2):
                r.pre[x, 2 * g + b] = pre[:, b * LANES : (b + 1) * LANES]
                r.act[x, 2 * g + b] = act[:, b * LANES : (b + 1) * LANES]
        return 0

    lax.fori_loop(0, 4, convs, 0)

    sums = r.sums[...]
    lane = lane_of(32)
    low = jnp.zeros((32, LANES), F32)
    high = low
    pooled = (pool_tiles(r.act, sums) * 0.125).astype(BF).reshape(4, 2, 16, LANES)
    for x in range(4):
        for half in range(2):
            tile = jnp.concatenate([pooled[x, half], r.pg[x, half]], axis=0)
            r.m[x, half] = tile
            wide = tile.astype(F32)
            for q in range(4):
                at = (q % 2) * 64 + (x * 4 + 2 * half + q // 2) * 4
                here = (lane >= at) & (lane < at + 4)
                low = jnp.where(here, turn(wide, at - 32 * q), low)
                high = jnp.where(here, turn(wide, at - 32 * q - 28), high)
    r.me[0] = low.astype(BF)
    r.me[1] = high.astype(BF)


def mid_forward(r, sizes):
    nx, ny, nz = sizes
    gx, gy, gz = position()
    lane = lane_of(32)
    spot = lane % 64

    def rows(x, _):
        dx, sx = x // 4, lax.rem(x, 4)
        pairs = []
        for a in range(8):
            dy, sy = (a + 2) // 4, (a + 2) % 4
            tile = r.mp[x, a // 2].astype(F32)
            q = 2 * (a % 2)
            base = jnp.where(lane < 64, turn(tile, 8 - 32 * q), turn(tile, 40 - 32 * q))
            at = (sx * 4 + sy) * 4
            right = turn(r.mer[dx, dy].astype(F32), 40 - at)
            left = turn(r.mel[dx, dy].astype(F32), 4 - at)
            row = jnp.where(spot < 44, right, 0.0)
            row = jnp.where(spot < 40, base, row)
            row = jnp.where(spot < 8, left, row)
            row = jnp.where(spot < 4, 0.0, row)
            r.pgp[x, a] = row[16:].astype(BF)
            pairs.append(row[:16])
        store_taps(r.pm3, x, pairs)
        r.pm3[x, 15] = jnp.zeros((48, LANES), BF)
        r.pm3[x, 16] = jnp.zeros((48, LANES), BF)
        return 0

    lax.fori_loop(0, 12, rows, 0)
    weight = r.wd[...]
    cell = spot - 8
    mid = cell + gz * 32
    inside = (cell >= -3) & (cell < 35) & (mid >= 0) & (mid < 32 * nz)
    second = lane // 64

    def convs(g, _):
        for x, both in conv(weight, r.pm3, 10, (4 * g, 4 * g + 2)):
            at_x = gx * 4 + x - 3
            for b in range(2):
                pre = both[:, b * LANES : (b + 1) * LANES]
                at_y = gy * 8 + 4 * g + 2 * b - 3 + second
                keep = inside & (at_y >= 0) & (at_y < 8 * ny)
                keep = keep & (at_x >= 0) & (at_x < 4 * nx)
                sig = sigmoid(pre)
                r.am[x, 2 * g + b] = jnp.where(keep, pre * sig, 0.0).astype(BF)
                r.dsm[x, 2 * g + b] = jnp.where(keep, slope(pre, sig), 0.0).astype(BF)
        return 0

    lax.fori_loop(0, 4, convs, 0)
    halves = [
        jnp.concatenate([r.am[3 + a, 1 + 2 * h + m] for a in range(4) for m in range(3)], axis=1)
        for h in range(2)
    ]
    cells = jnp.concatenate(halves + [jnp.zeros((64, 12 * LANES), BF)], axis=0)
    col = lax.broadcasted_iota(jnp.int32, (8, 12 * LANES), 1)
    third, upper = col // LANES % 3, col // 64 % 2
    hit = coarse_sum_matrix(12) & ((third == 1) | ((third == 0) == (upper == 1)))
    pooled = dot_nt(jnp.where(hit, 1.0, 0.0).astype(BF), cells) * (1.0 / 64.0)
    r.pc[...] = pooled.astype(BF).astype(F32)


def near_rows(sizes, count):
    ny = sizes[1]
    have = min(count, ny)
    start = lax.axis_index("gy") - count // 2
    return jnp.minimum(jnp.maximum(start, 0), ny - have), have


def lift_row(r, sizes, y):
    for x in range(sizes[0]):
        for y2 in range(2):
            pre = dot(r.pcg[y, x], r.wide_lift[y2])
            act = (pre * sigmoid(pre)).astype(BF)
            r.alc[x, y, y2] = act
            store_coarse_taps(r.al3, (x + 1, 2 * y + y2 + 1), act.astype(F32))


def coarse_forward(r, sizes, y, have):
    nx, cells = sizes[0], 8 * sizes[2]
    rows = nx * 2 * have * cells
    for i in range(3):
        for j in range(3):
            block = r.al3[pl.ds(i, nx), pl.ds(2 * y + j, 2 * have)].reshape(rows, 768)
            part = dot(block, r.wc[3 * i + j])
            if i + j == 0:
                r.acc[pl.ds(0, rows)] = part
            else:
                r.acc[pl.ds(0, rows)] += part
    per = 2 * have * cells
    for x in range(nx):
        pre = r.acc[pl.ds(x * per, per)]
        sig = sigmoid(pre)
        r.actc[x, pl.ds(y, have)] = (pre * sig).astype(BF).reshape(have, 2, cells, 256)
        r.dsc[x, pl.ds(y, have)] = slope(pre, sig).astype(BF).reshape(have, 2, cells, 256)


def up_forward(r, sizes, scale):
    cells = 8 * sizes[2]
    gz = lax.axis_index("gz")
    start, have = near_rows(sizes, 5)

    def lift(o, _):
        lift_row(r, sizes, start + o)
        return 0

    lax.fori_loop(0, have, lift, 0)
    coarse_forward(r, sizes, *near_rows(sizes, 3))

    spread = coarse_grow_matrix(cells, gz)
    for dx, dy, x, y, y2, keep in near_cells(sizes):
        out = dot_nt(r.wp[...], r.actc[x, y, y2]).astype(BF)
        r.cos[dx, dy] = dot(out, spread) * keep

    first = lane_of(32) < 64

    def join(x, _):
        pairs = []
        for m in range(7):
            lower = r.cos[(x + 1) // 4, (2 * m + 1) // 4]
            upper = r.cos[(x + 1) // 4, (2 * m + 2) // 4]
            row = r.am[x, m].astype(F32) + jnp.where(first, lower, upper)
            pairs.append(row.astype(BF).astype(F32))
        store_taps(r.j3, x, pairs)
        return 0

    lax.fori_loop(0, 10, join, 0)

    cell = lane_of(16) % 64 - 8
    near = (cell >= -2) & (cell < 34)
    weight = r.wu[...]

    def up(g, _):
        for x, both in conv(weight, r.j3, 8, (4 * g, 4 * g + 2)):
            for b in range(2):
                pre = both[:, b * LANES : (b + 1) * LANES]
                sig = sigmoid(pre)
                r.su[x, 2 * g + b] = (pre * sig).astype(BF)
                pooled = r.pgp[x + 2, 2 * g + b + 1].astype(F32) * scale
                grad = jnp.where(near, pooled * slope(pre, sig), 0.0)
                r.guo[x, 2 * g + b] = grad.astype(BF)
        return 0

    lax.fori_loop(0, 3, up, 0)

    def stack(x, _):
        store_taps(r.gu3, x, [r.guo[x, m].astype(F32) for m in range(6)])
        return 0

    lax.fori_loop(0, 8, stack, 0)

    weight_t = r.wut[...]
    for starts in ((0, 2), (4, 6), (8,)):
        for x, both in conv(weight_t, r.gu3, 6, starts):
            for b, y in enumerate(starts):
                r.gj[x, y // 2] = both[:, b * LANES : (b + 1) * LANES]

    totals = []
    for h in range(2):
        total = None
        for a in range(4):
            lower, middle, upper = [r.gj[1 + a, 2 * h + m] for m in range(3)]
            row = middle + jnp.where(first, upper, lower)
            total = row if total is None else total + row
        totals.append(total)
    total = jnp.concatenate(totals + [jnp.zeros((64, LANES), F32)], axis=0)
    head = total.astype(BF)
    tail = (total - head.astype(F32)).astype(BF)
    sums = jnp.where(coarse_sum_matrix(1), 1.0, 0.0).astype(BF)
    r.gc[...] = (dot_nt(sums, head) + dot_nt(sums, tail)).astype(BF).astype(F32)


def up_taps(r):
    cell = lane_of(16) % 64 - 8
    own = (cell >= 0) & (cell < 32)
    r.accu[...] = jnp.zeros(r.accu.shape, F32)
    grads = [
        jnp.concatenate(
            [jnp.where(own, r.guo[x + 2, m + 1].astype(F32), 0.0) for m in range(4)], axis=1
        ).astype(BF)
        for x in range(4)
    ]
    none = jnp.zeros((16, 4 * LANES), BF)
    for x in range(6):
        left = [grads[x - i] if 0 <= x - i < 4 else none for i in range(3)]
        right = [three(r.j3, x + 2, 2 * m + 2) for m in range(4)]
        r.accu[:, pl.ds(0, 288)] += dot_nt(
            jnp.concatenate(left, axis=0), jnp.concatenate(right, axis=1)
        )


def decode(r):
    grow = grow_matrix()

    def plane(x, _):
        rows = jnp.concatenate([r.su[x + 2, m + 1] for m in range(4)], axis=0)
        grown = dot(rows, grow)
        for a in range(2):
            for t in range(8):
                add = grown[16 * (t // 2) : 16 * (t // 2) + 16, (t % 2) * LANES :][:, :LANES]
                tile = r.act[2 * x + a, t].astype(F32) + add
                r.plane[2 * t] = tile.astype(BF)
                r.plane[2 * t + 1] = turn(tile, 64).astype(BF)
            r.dec[:, 2 * x + a] = jnp.swapaxes(r.plane[...], 0, 1)[:, :, :64]
        return 0

    lax.fori_loop(0, 4, plane, 0)


def coarse_grad_row(r, sizes, y):
    for x in range(sizes[0]):
        for y2 in range(2):
            grad = dot(r.gcg[y, x], r.wide_proj[y2]) * r.dsc[x, y, y2].astype(F32)
            grad = grad.astype(BF).astype(F32)
            store_coarse_taps(r.gp3, (x + 2, 2 * y + y2 + 2), grad)


def pay_rows(r, start, block):
    per = r.pay.shape[1]
    done = 0
    while done < block.shape[0]:
        part, at = divmod(start + done, per)
        size = min(per - at, block.shape[0] - done)
        r.pay[part, pl.ds(at, size)] = block[done : done + size]
        done += size


def backward(r, sizes, scale):
    cells = 8 * sizes[2]
    gx, gy, gz = position()
    start, have = near_rows(sizes, 3)

    def coarse(o, _):
        coarse_grad_row(r, sizes, start + o)
        return 0

    lax.fori_loop(0, have, coarse, 0)
    rows = 12 * cells
    for i in range(3):
        for j in range(3):
            block = r.gp3[pl.ds(gx + i, 3), pl.ds(2 * gy + j, 4)].reshape(rows, 768)
            part = dot(block, r.wct[3 * i + j])
            if i + j == 0:
                r.acc[pl.ds(0, rows)] = part
            else:
                r.acc[pl.ds(0, rows)] += part

    spread = coarse_grow_matrix(cells, gz)
    own = lax.broadcasted_iota(jnp.int32, (cells, 256), 0) // 8 == gz
    for at, (dx, dy, x, y, y2, keep) in enumerate(near_cells(sizes)):
        pre = dot(r.pcg[y, x], r.wide_lift[y2])
        grad = (r.acc[pl.ds(at * cells, cells)] * slope(pre, sigmoid(pre))).astype(BF)
        out = dot_nt(r.wl[...], grad).astype(BF)
        r.cos[dx, dy] = dot(out, spread) * (keep * (1.0 / 64.0))
        if dx == 1 and dy in (1, 2):
            masked = jnp.where(own, grad.astype(F32), 0.0).astype(BF)
            r.pairs[y2] = dot_tn(r.pcg[y, x], masked)
    lifts = r.pairs[0, :32] + r.pairs[1, 32:64]
    for b in range(2):
        pay_rows(r, 432 + 32 * b, lifts[:, b * LANES : (b + 1) * LANES])

    first = lane_of(32) < 64

    def join(x, _):
        pairs = []
        for n in range(5):
            lower = r.cos[(x + 3) // 4, (2 * n + 3) // 4]
            upper = r.cos[(x + 3) // 4, (2 * n + 4) // 4]
            row = r.gj[x, n] + jnp.where(first, lower, upper)
            row = row * r.dsm[x + 2, n + 1].astype(F32)
            pairs.append(row.astype(BF).astype(F32))
        store_taps(r.gm3, x, pairs)
        return 0

    lax.fori_loop(0, 6, join, 0)

    weight_t = r.wdt[...]
    for starts in ((0, 2), (4, 6)):
        for x, both in conv(weight_t, r.gm3, 4, starts):
            for b, y in enumerate(starts):
                r.gpm[x, pl.ds(8 * y, 16)] = both[:, b * LANES : (b + 1) * LANES].astype(BF)

    grow = grow_matrix()
    for x in (0, 1, 10, 11):
        r.gf[x] = jnp.zeros(r.gf.shape[1:], BF)

    def fine(x, _):
        grown = dot(r.gpm[x], grow) * 0.125
        for a in range(2):
            for t in range(8):
                add = grown[16 * (t // 2) : 16 * (t // 2) + 16, (t % 2) * LANES :][:, :LANES]
                pre = r.pre[2 * x + a, t]
                grad = r.ct[2 * x + a, t].astype(F32) * scale + add
                grad = (grad * slope(pre, sigmoid(pre))).astype(BF)
                r.gf[2 * x + a + 2, :, pl.ds(t * LANES, LANES)] = grad
        return 0

    lax.fori_loop(0, 4, fine, 0)

    r.accd[...] = jnp.zeros(r.accd.shape, F32)
    spot = lane_of(32) % 64
    inner = (spot >= 8) & (spot < 40)
    grads = [
        jnp.concatenate(
            [
                jnp.where(inner, r.gm3[x + 1, 2 * m + 1, pl.ds(32, 32)].astype(F32), 0.0)
                for m in range(4)
            ],
            axis=1,
        ).astype(BF)
        for x in range(4)
    ]
    none = jnp.zeros((32, 4 * LANES), BF)
    for x in range(6):
        left = [grads[x - i] if 0 <= x - i < 4 else none for i in range(3)]
        right = [three(r.pm3, x + 3, 2 * m + 3) for m in range(4)]
        r.accd[:, pl.ds(0, 144)] += dot_nt(
            jnp.concatenate(left, axis=0), jnp.concatenate(right, axis=1)
        )

    r.accf[...] = jnp.zeros(r.accf.shape, F32)

    def taps_fine(n, _):
        planes = (2 * n, 2 * n + 1)
        left = [jnp.concatenate([r.gf[x + 2 - i] for x in planes], axis=1) for i in range(3)]
        right = [three(r.v3, x, 2 * t) for x in planes for t in range(8)]
        r.accf[:, pl.ds(0, 144)] += dot_nt(
            jnp.concatenate(left, axis=0), jnp.concatenate(right, axis=1)
        )
        return 0

    lax.fori_loop(0, 5, taps_fine, 0)

    for b in range(2):
        pay_rows(r, 48 * b, r.accf[:, b * LANES : (b + 1) * LANES])
    for b in range(3):
        pay_rows(r, 96 + 48 * b, r.accu[:, b * LANES : (b + 1) * LANES])
    for b in range(2):
        pay_rows(r, 240 + 96 * b, r.accd[:, b * LANES : (b + 1) * LANES])
    pay_rows(r, 496, jnp.zeros((16, LANES), F32))


def coarse_taps(r, sizes, t):
    nx, ny, nz = sizes
    count = nx * ny * 16 * nz
    i, j = t // 3, lax.rem(t, 3)
    block = r.gp3[pl.ds(3 - i, nx), pl.ds(3 - j, 2 * ny)].reshape(count, 768)
    out = dot(r.cells_t[...], block)
    for k in range(3):
        r.gwc[3 * t + k] = out[:, 256 * (2 - k) : 256 * (3 - k)].astype(BF)


def proj_grad(r, sizes):
    nx, ny, nz = sizes
    cells = 8 * nz
    r.pairs[...] = jnp.zeros(r.pairs.shape, F32)

    def plane(x, _):
        for y2 in range(2):
            grads = r.gcg[:, x].reshape(ny * cells, LANES)
            r.pairs[y2] += dot_tn(grads, r.actc[x, :, y2].reshape(ny * cells, 256))
        return 0

    lax.fori_loop(0, nx, plane, 0)
    r.gwp[...] = r.pairs[0, :32] + r.pairs[1, 32:64]


def step_kernel(sizes, scale, names, *refs):
    nx, ny, nz = sizes
    count = nx * ny * 16 * nz
    r = types.SimpleNamespace(**dict(zip(names, refs, strict=True)))
    gx, gy, gz = position()
    pair = nz % 2 == 0
    mine = lax.rem(gz, 2) if pair else 0
    other = (gx, gy, gz + 1 - 2 * mine) if pair else None

    fetch = [
        pltpu.make_async_copy(source, target, r.fetched.at[n])
        for n, (source, target) in enumerate(
            ((r.vol_in, r.vol), (r.cot_in, r.cot), (r.wc_in, r.wc))
        )
    ]
    for copy in fetch:
        copy.start()

    def arrange():
        fetch[0].wait()
        arrange_volume(r)

    greet(sizes, arrange)

    def first_wait():
        prepare_weights(r)
        fetch[1].wait()
        arrange_cotangent(r)
        place_weight(r.wide_lift, r.wl[...])
        place_weight(r.wide_proj, r.wp[...])

    halo_round(sizes, 1, 1, (r.v, r.ve, r.vp, r.ver, r.vel, r.vsend, r.vrecv), first_wait)
    fine_forward(r)

    def second_wait():
        zero_rim(r.al3, 1)
        zero_rim(r.gp3, 2)
        fetch[2].wait()

        def turn_weights(t, _):
            for k in range(3):
                block = r.wc[8 - t, pl.ds(256 * (2 - k), 256)]
                r.wct[t, pl.ds(256 * k, 256)] = block.T
            return 0

        lax.fori_loop(0, 9, turn_weights, 0)

    halo_round(sizes, 4, 1, (r.m, r.me, r.mp, r.mer, r.mel, r.msend, r.mrecv), second_wait)
    mid_forward(r, sizes)
    sems = (r.ga_send, r.ga_recv, r.gb_send, r.gb_recv)
    gather_round(sizes, (r.pc, r.pcg, r.pstage) + sems, nothing, nothing)
    up_forward(r, sizes, scale)

    decoded = pltpu.make_async_copy(r.dec, r.dec_out, r.fetched.at[3])

    def third_wait():
        up_taps(r)
        decode(r)
        decoded.start()

    far_start, far_first = near_rows(sizes, 3)

    def far_row(n, whose):
        step = 2 if pair else 1
        return lax.rem(far_start + far_first + step * n + whose, ny)

    def far_count(whose):
        return (ny - far_first + 1 - whose) // 2 if pair else ny - far_first

    def far_copies(n, whose):
        y = far_row(n, whose)
        return [
            pltpu.make_async_remote_copy(
                src_ref=ref.at[:, pl.ds(y, 1)],
                dst_ref=ref.at[:, pl.ds(y, 1)],
                send_sem=r.far_send.at[part, n],
                recv_sem=r.far_recv.at[part, n],
                device_id=other,
                device_id_type=MESH,
            )
            for part, ref in enumerate((r.actc, r.dsc))
        ]

    def fourth_wait():
        start, have = near_rows(sizes, 5)

        def lift(o, _):
            lift_row(r, sizes, lax.rem(start + o, ny))
            return 0

        lax.fori_loop(have, ny, lift, 0)

        def coarse(n, _):
            coarse_forward(r, sizes, far_row(n, mine), 1)
            if pair:
                for copy in far_copies(n, mine):
                    copy.start()
            return 0

        lax.fori_loop(0, far_count(mine), coarse, 0)

    sems = (r.ha_send, r.ha_recv, r.hb_send, r.hb_recv)
    gather_round(sizes, (r.gc, r.gcg, r.gstage) + sems, third_wait, fourth_wait)
    backward(r, sizes, scale)

    half = 5 if pair else 9

    def taps_count(whose):
        return half - whose

    def keep_taps(n):
        taps = pl.ds(3 * (n + half * mine), 3)
        return pltpu.make_async_copy(r.gwc.at[taps], r.gwc_out.at[taps], r.kept.at[n])

    def send_taps(n, whose):
        taps = pl.ds(3 * (n + half * whose), 3)
        return pltpu.make_async_remote_copy(
            src_ref=r.gwc.at[taps],
            dst_ref=r.gwc_out.at[taps],
            send_sem=r.tap_send.at[n],
            recv_sem=r.tap_recv.at[n],
            device_id=other,
            device_id_type=MESH,
        )

    def do_taps(first, last):
        def taps(n, _):
            coarse_taps(r, sizes, n + half * mine)
            keep_taps(n).start()
            if pair:
                send_taps(n, mine).start()
            return 0

        lax.fori_loop(first, last, taps, 0)

    def wait_a():
        if pair:

            def arrived(n, _):
                for copy in far_copies(n, 1 - mine):
                    copy.wait_recv()
                return 0

            lax.fori_loop(0, far_count(1 - mine), arrived, 0)
        start, have = near_rows(sizes, 3)

        def coarse(o, _):
            coarse_grad_row(r, sizes, lax.rem(start + o, ny))
            return 0

        lax.fori_loop(have, ny, coarse, 0)
        r.cells_t[...] = r.alc[...].reshape(count, 256).T
        do_taps(0, 1)

    def wait_b():
        do_taps(1, 3)

    def wait_c():
        do_taps(3, taps_count(mine))
        proj_grad(r, sizes)

    sems = (r.ra_send, r.ra_recv, r.rb_send, r.rb_recv, r.rc_send, r.rc_recv)
    reduce_round(sizes, (r.pay, r.red, r.ra, r.rb) + sems, (wait_a, wait_b, wait_c))

    def finish(n, _):
        keep_taps(n).wait()
        if pair:
            send_taps(n, mine).wait_send()
        return 0

    lax.fori_loop(0, taps_count(mine), finish, 0)
    decoded.wait()
    if pair:

        def sent(n, _):
            for copy in far_copies(n, mine):
                copy.wait_send()
            return 0

        def landed(n, _):
            send_taps(n, 1 - mine).wait_recv()
            return 0

        lax.fori_loop(0, far_count(mine), sent, 0)
        lax.fori_loop(0, taps_count(1 - mine), landed, 0)


def last_kernel(
    gwc_in,
    red_ref,
    gwp_ref,
    wc_out,
    wf_out,
    wd_out,
    wl_out,
    wp_out,
    wu_out,
    rows,
    narrow,
    wide,
    load_sem,
    store_sem,
):
    blocks = [pl.ds(3 * n, 3) for n in range(9)]
    loads = [
        pltpu.make_async_copy(gwc_in.at[block], narrow.at[block], load_sem.at[n])
        for n, block in enumerate(blocks)
    ]
    stores = [
        pltpu.make_async_copy(wide.at[block], wc_out.at[block], store_sem.at[n])
        for n, block in enumerate(blocks)
    ]
    for load in loads:
        load.start()
    for n, block in enumerate(blocks):
        loads[n].wait()
        wide[block] = narrow[block].astype(F32)
        stores[n].start()

    def columns(start, blocks, count):
        return jnp.concatenate(
            [red_ref[pl.ds(start + count * b, count)] for b in range(blocks)], axis=1
        )

    table = columns(0, 2, 48)
    for i in range(3):
        rows[pl.ds(144 * i, 144)] = table[16 * i : 16 * i + 16, :144].T
    for c in range(16):
        wf_out[c] = rows[pl.ds(c, 27, stride=16)].T
    table = columns(96, 3, 48)
    for i in range(3):
        for jk in range(9):
            wu_out[9 * i + jk] = table[16 * i : 16 * i + 16, 32 * jk : 32 * jk + 32]
    table = columns(240, 2, 96)
    for i in range(3):
        part = table[32 * i : 32 * i + 32, :144]
        wd_out[pl.ds(9 * i, 9)] = part.T.reshape(9, 16, 32)
    wl_out[...] = columns(432, 2, 32)
    wp_out[...] = gwp_ref[...]
    for store in stores:
        store.wait()


VMEM = pl.BlockSpec(memory_space=pltpu.VMEM)
HBM = pl.BlockSpec(memory_space=pl.ANY)


def shards(sizes, volume, w_fine, w_down, w_lift, w_coarse, w_proj, w_up, cotangent):
    nx, ny, nz = sizes
    scale = 1.0 / math.sqrt(8 * nx * 16 * ny * 64 * nz)
    cells = 8 * nz
    parts = nx * nz
    per = 512 // parts
    grid = (nx, ny, 2, cells, 256)
    gathered = (ny, nx, cells, LANES)
    ins = {
        "wf_in": jnp.transpose(w_fine, (1, 2, 0)),
        "wd_in": w_down,
        "wu_in": jnp.transpose(w_up, (0, 2, 1)),
        "wl": w_lift,
        "wp": jnp.transpose(w_proj),
        "vol_in": volume,
        "cot_in": cotangent,
        "wc_in": w_coarse.reshape(9, 768, 256),
    }
    outs = {
        "red": ((parts, per, LANES), F32),
        "gwp": ((32, 256), F32),
        "dec_out": ((16, 8, 16, 64), BF),
        "gwc_out": ((27, 256, 256), BF),
    }
    narrow = {
        "vol": (16, 8, 16, 64),
        "cot": (16, 8, 16, 64),
        "dec": (16, 8, 16, 64),
        "v": (8, 8, 16, LANES),
        "ve": (2, 16, LANES),
        "vp": (10, 10, 16, LANES),
        "ver": (3, 3, 16, LANES),
        "vel": (3, 3, 16, LANES),
        "ct": (8, 8, 16, LANES),
        "sums": (8 * LANES, LANES),
        "pg": (4, 2, 16, LANES),
        "wf": (48, 144),
        "wd": (96, 144),
        "wu": (48, 288),
        "wdt": (48, 288),
        "wut": (96, 144),
        "v3": (10, 17, 48, LANES),
        "act": (8, 8, 16, LANES),
        "m": (4, 2, 32, LANES),
        "me": (2, 32, LANES),
        "mp": (12, 4, 32, LANES),
        "mer": (3, 3, 32, LANES),
        "mel": (3, 3, 32, LANES),
        "pm3": (12, 17, 48, LANES),
        "pgp": (12, 8, 16, LANES),
        "am": (10, 8, 32, LANES),
        "dsm": (10, 8, 32, LANES),
        "pcg": gathered,
        "gcg": gathered,
        "wc": (9, 768, 256),
        "wct": (9, 768, 256),
        "wide_lift": (2, LANES, 256),
        "wide_proj": (2, LANES, 256),
        "al3": (nx + 2, 2 * ny + 2, cells, 768),
        "gp3": (nx + 4, 2 * ny + 4, cells, 768),
        "alc": grid,
        "actc": grid,
        "dsc": grid,
        "j3": (10, 13, 96, LANES),
        "guo": (8, 6, 16, LANES),
        "gu3": (8, 11, 48, LANES),
        "su": (8, 6, 16, LANES),
        "plane": (16, 16, LANES),
        "gm3": (6, 9, 96, LANES),
        "gpm": (4, 64, LANES),
        "gf": (12, 16, 8 * LANES),
        "cells_t": (256, nx * ny * 2 * cells),
        "gwc": (27, 256, 256),
    }
    wide = {
        "wrows": (432, 16),
        "pre": (8, 8, 16, LANES),
        "pc": (8, LANES),
        "pstage": (nx, cells, LANES),
        "acc": (max(nx * 2 * min(3, ny), 12) * cells, 256),
        "cos": (3, 4, 32, LANES),
        "gj": (6, 5, 32, LANES),
        "gc": (8, LANES),
        "gstage": (nx, cells, LANES),
        "accu": (48, 3 * LANES),
        "accf": (48, 2 * LANES),
        "accd": (96, 2 * LANES),
        "pairs": (2, LANES, 256),
        "pay": (parts, per, LANES),
        "ra": (parts, per, LANES),
        "rb": (ny, per, LANES),
    }
    sems = {
        "vsend": 26,
        "vrecv": 26,
        "msend": 26,
        "mrecv": 26,
        "ga_send": parts,
        "ga_recv": parts,
        "gb_send": ny,
        "gb_recv": ny,
        "ha_send": parts,
        "ha_recv": parts,
        "hb_send": ny,
        "hb_recv": ny,
        "ra_send": parts,
        "ra_recv": parts,
        "rb_send": ny,
        "rb_recv": ny,
        "rc_send": parts,
        "rc_recv": parts,
        "kept": 9,
        "tap_send": 9,
        "tap_recv": 9,
        "fetched": 4,
    }
    far = {"far_send": (2, ny), "far_recv": (2, ny)}
    names = list(ins) + list(outs) + list(narrow) + list(wide) + list(sems) + list(far)
    red, gwp, dec, gwc = pl.pallas_call(
        functools.partial(step_kernel, sizes, scale, names),
        out_shape=[jax.ShapeDtypeStruct(shape, kind) for shape, kind in outs.values()],
        in_specs=[VMEM] * (len(ins) - 3) + [HBM] * 3,
        out_specs=[VMEM] * 2 + [HBM] * 2,
        scratch_shapes=[pltpu.VMEM(shape, BF) for shape in narrow.values()]
        + [pltpu.VMEM(shape, F32) for shape in wide.values()]
        + [pltpu.SemaphoreType.DMA((size,)) for size in sems.values()]
        + [pltpu.SemaphoreType.DMA(shape) for shape in far.values()],
        compiler_params=pltpu.CompilerParams(
            vmem_limit_bytes=62 * 1024 * 1024, collective_id=1, has_side_effects=True
        ),
    )(*ins.values())
    shapes = [(27, 256, 256), (16, 16, 27), (27, 16, 32), (32, 256), (32, 256), (27, 16, 32)]

    gwc, gwf, gwd, gwl, gwp, gwu = pl.pallas_call(
        last_kernel,
        out_shape=[jax.ShapeDtypeStruct(shape, F32) for shape in shapes],
        in_specs=[HBM, VMEM, VMEM],
        out_specs=[HBM] + [VMEM] * 5,
        scratch_shapes=[
            pltpu.VMEM((432, 16), F32),
            pltpu.VMEM((27, 256, 256), BF),
            pltpu.VMEM((27, 256, 256), F32),
            pltpu.SemaphoreType.DMA((9,)),
            pltpu.SemaphoreType.DMA((9,)),
        ],
        compiler_params=pltpu.CompilerParams(vmem_limit_bytes=32 * 1024 * 1024),
    )(gwc, red.reshape(512, LANES), gwp)
    gwf = jnp.transpose(gwf, (2, 0, 1))
    gwu = jnp.transpose(gwu, (0, 2, 1))
    return dec, gwf, gwd, gwl, gwc, jnp.transpose(gwp), gwu


def solution(mesh):
    sizes = tuple(mesh.shape[name] for name in ("gx", "gy", "gz"))
    block = P(None, "gx", "gy", "gz")
    return jax.shard_map(
        functools.partial(shards, sizes),
        mesh=mesh,
        in_specs=(block, P(), P(), P(), P(), P(), P(), block),
        out_specs=(block, P(), P(), P(), P(), P(), P()),
        check_vma=False,
    )
```

```python
import functools
import math
import types

import jax
import jax.numpy as jnp
from jax import lax
from jax.experimental import pallas as pl
from jax.experimental.pallas import tpu as pltpu
from jax.sharding import PartitionSpec as P

BF = jnp.bfloat16
F32 = jnp.float32
MESH = pl.DeviceIdType.MESH
LANES = 128


def dot(left, right):
    return jnp.dot(left, right, preferred_element_type=F32)


def dot_nt(left, right):
    return lax.dot_general(left, right, (((1,), (1,)), ((), ())), preferred_element_type=F32)


def dot_tn(left, right):
    return lax.dot_general(left, right, (((0,), (0,)), ((), ())), preferred_element_type=F32)


def sigmoid(values):
    return 0.5 * jnp.tanh(0.5 * values) + 0.5


def slope(values, sig):
    return sig * (1.0 + values * (1.0 - sig))


def lane_of(rows):
    return lax.broadcasted_iota(jnp.int32, (rows, LANES), 1)


def turn(tile, by):
    if isinstance(by, int):
        by = by % LANES
        return tile if by == 0 else pltpu.roll(tile, by, 1)
    return pltpu.roll(tile, lax.rem(by + 4 * LANES, LANES), 1)


def tap_rows(pair):
    return jnp.concatenate([turn(pair, 1), pair, turn(pair, -1)], axis=0)


def between(lower, upper):
    lane = lane_of(lower.shape[0])
    return jnp.where(lane < 64, turn(lower, 64), turn(upper, 64))


def store_taps(ref, x, pairs):
    stacks = [tap_rows(pair) for pair in pairs]
    for n, stack in enumerate(stacks):
        ref[x, 2 * n] = stack
        if n + 1 < len(stacks):
            ref[x, 2 * n + 1] = between(stack, stacks[n + 1])


def three(ref, x, y):
    block = ref[x, pl.ds(y, 3)]
    return block.reshape(3 * block.shape[1], LANES)


def conv(weight, ref, first, planes, starts):
    outs = weight.shape[0] // 3
    parts = []
    for n in range(planes + 2):
        tiles = [three(ref, first + n, y) for y in starts]
        block = tiles[0] if len(tiles) == 1 else jnp.concatenate(tiles, axis=1)
        parts.append(dot(weight, block))
        if n >= 2:
            yield (
                first + n - 2,
                parts[n - 2][:outs] + parts[n - 1][outs : 2 * outs] + parts[n][2 * outs :],
            )


def pool_matrix():
    row = lax.broadcasted_iota(jnp.int32, (8 * LANES, LANES), 0)
    col = lax.broadcasted_iota(jnp.int32, (8 * LANES, LANES), 1)
    hit = (row // 256 == col // 32) & (row % 64 // 2 == col % 32)
    return jnp.where(hit, 1.0, 0.0).astype(BF)


def pool_tiles(ref, sums):
    cells = [
        jnp.concatenate([ref[2 * x + a, 4 * half + q] for q in range(4) for a in range(2)], axis=1)
        for x in range(4)
        for half in range(2)
    ]
    return dot(jnp.concatenate(cells, axis=0), sums)


def grow_matrix():
    row = lax.broadcasted_iota(jnp.int32, (LANES, 2 * LANES), 0)
    col = lax.broadcasted_iota(jnp.int32, (LANES, 2 * LANES), 1)
    hit = (row // 64 == col // LANES) & (row % 64 - 8 == col % 64 // 2)
    return jnp.where(hit, 1.0, 0.0).astype(BF)


def coarse_sum_matrix(tiles):
    row = lax.broadcasted_iota(jnp.int32, (8, tiles * LANES), 0)
    cell = lax.broadcasted_iota(jnp.int32, (8, tiles * LANES), 1) % 64 - 8
    return (cell >= 0) & (cell < 32) & ((cell + 4) // 4 == row + 1)


def coarse_grow_matrix(cells, gz):
    row = lax.broadcasted_iota(jnp.int32, (cells, LANES), 0)
    cell = lax.broadcasted_iota(jnp.int32, (cells, LANES), 1) % 64 - 8
    mid = cell + gz * 32
    hit = (cell >= -3) & (cell < 35) & (mid >= 0) & (row == (mid + 4) // 4 - 1)
    return jnp.where(hit, 1.0, 0.0).astype(BF)


def plane_rows(block):
    rows = jnp.swapaxes(block, 0, 1)
    return [jnp.concatenate([rows[2 * t], rows[2 * t + 1]], axis=1) for t in range(8)]


def place_weight(ref, weight):
    for y2 in range(2):
        ref[y2] = jnp.zeros((LANES, 256), BF)
        ref[y2, pl.ds(32 * y2, 32)] = weight


def store_coarse_taps(ref, at, cells):
    count = cells.shape[0]
    row = lax.broadcasted_iota(jnp.int32, cells.shape, 0)
    before = jnp.where(row > 0, pltpu.roll(cells, 1, 0), 0.0)
    after = jnp.where(row < count - 1, pltpu.roll(cells, count - 1, 0), 0.0)
    ref[at + (slice(None), pl.ds(0, 256))] = before.astype(BF)
    ref[at + (slice(None), pl.ds(256, 256))] = cells.astype(BF)
    ref[at + (slice(None), pl.ds(512, 256))] = after.astype(BF)


def zero_rim(ref, rim):
    planes, rows = ref.shape[:2]

    def clear(x, _):
        for y in list(range(rim)) + list(range(rows - rim, rows)):
            ref[x, y] = jnp.zeros(ref.shape[2:], ref.dtype)
        return 0

    lax.fori_loop(0, planes, clear, 0)

    def clear_plane(y, _):
        for x in list(range(rim)) + list(range(planes - rim, planes)):
            ref[x, y] = jnp.zeros(ref.shape[2:], ref.dtype)
        return 0

    lax.fori_loop(0, rows, clear_plane, 0)


def clamp(at, count):
    return jnp.minimum(jnp.maximum(at, 0), count - 1)


def near_cells(sizes):
    nx, ny, _ = sizes
    gx, gy = lax.axis_index("gx"), lax.axis_index("gy")
    found = []
    for dx in range(3):
        for dy in range(4):
            x, y = gx - 1 + dx, gy + (dy + 1) // 2 - 1
            there = (x >= 0) & (x < nx) & (y >= 0) & (y < ny)
            keep = jnp.where(there, 1.0, 0.0)
            found.append((dx, dy, clamp(x, nx), clamp(y, ny), (dy + 1) % 2, keep))
    return found


def nothing():
    pass


NEIGHBOURS = [
    (dx, dy, dz)
    for dz in (-1, 1, 0)
    for dx in (-1, 0, 1)
    for dy in (-1, 0, 1)
    if (dx, dy, dz) != (0, 0, 0)
]


def position():
    return [lax.axis_index(name) for name in ("gx", "gy", "gz")]


def valid(sizes, steps):
    found = None
    for at, size, step in zip(position(), sizes, steps):
        if step != 0:
            test = at > 0 if step < 0 else at < size - 1
            found = test if found is None else found & test
    return found


def plane_peers(nx, nz):
    return [(ox, oz) for ox in range(nx) for oz in range(nz) if (ox, oz) != (0, 0)]


def greet(sizes, work):
    nx, ny, nz = sizes
    me = gx, gy, gz = position()
    barrier = pltpu.get_barrier_semaphore()
    peers = [(lax.rem(gx + ox, nx), gy, lax.rem(gz + oz, nz)) for ox, oz in plane_peers(nx, nz)]
    peers += [(gx, lax.rem(gy + oy, ny), gz) for oy in range(1, ny)]
    for peer in peers:
        pl.semaphore_signal(barrier, inc=1, device_id=peer, device_id_type=MESH)
    total = 1
    for axis in range(3):
        low = jnp.where(me[axis] > 0, 1, 0)
        high = jnp.where(me[axis] < sizes[axis] - 1, 1, 0)
        total = total * (1 + low + high)
    for steps in NEIGHBOURS:

        @pl.when(valid(sizes, steps))
        def _():
            pl.semaphore_signal(
                barrier,
                inc=1,
                device_id=tuple(me[axis] + steps[axis] for axis in range(3)),
                device_id_type=MESH,
            )

    work()
    pl.semaphore_wait(barrier, total - 1 + len(peers))


def halo_round(sizes, hx, ht, refs, meanwhile):
    a_ref, e_ref, p_ref, er_ref, el_ref, send_sem, recv_sem = refs
    me = [lax.axis_index(name) for name in ("gx", "gy", "gz")]
    planes, tiles = a_ref.shape[:2]

    def part(step, halo, count):
        if step == 0:
            return pl.ds(0, count), pl.ds(halo, count)
        if step > 0:
            return pl.ds(count - halo, halo), pl.ds(0, halo)
        return pl.ds(0, halo), pl.ds(count + halo, halo)

    def copy_of(k, steps):
        dx, dy, dz = steps
        if dz == 0:
            fx, tx = part(dx, hx, planes)
            fy, ty = part(dy, ht, tiles)
            src, dst = a_ref.at[fx, fy], p_ref.at[tx, ty]
        elif dz > 0:
            src, dst = e_ref.at[1], el_ref.at[1 - dx, 1 - dy]
        else:
            src, dst = e_ref.at[0], er_ref.at[1 - dx, 1 - dy]
        return pltpu.make_async_remote_copy(
            src_ref=src,
            dst_ref=dst,
            send_sem=send_sem.at[k],
            recv_sem=recv_sem.at[k],
            device_id=(me[0] + dx, me[1] + dy, me[2] + dz),
            device_id_type=MESH,
        )

    for k, steps in enumerate(NEIGHBOURS):

        @pl.when(valid(sizes, steps))
        def _():
            copy_of(k, steps).start()

    p_ref[pl.ds(hx, planes), pl.ds(ht, tiles)] = a_ref[...]
    for k, steps in enumerate(NEIGHBOURS):
        back = tuple(-step for step in steps)
        dx, dy, dz = steps

        @pl.when(jnp.logical_not(valid(sizes, back)))
        def _():
            if dz == 0:
                _, tx = part(dx, hx, planes)
                _, ty = part(dy, ht, tiles)
                into = p_ref.at[tx, ty]
            elif dz > 0:
                into = el_ref.at[1 - dx, 1 - dy]
            else:
                into = er_ref.at[1 - dx, 1 - dy]
            into[...] = jnp.zeros(into.shape, into.dtype)

    meanwhile()
    for k, steps in enumerate(NEIGHBOURS):
        back = tuple(-step for step in steps)

        @pl.when(valid(sizes, back))
        def _():
            copy_of(k, steps).wait_recv()

    for k, steps in enumerate(NEIGHBOURS):

        @pl.when(valid(sizes, steps))
        def _():
            copy_of(k, steps).wait_send()


def gather_round(sizes, refs, first_wait, second_wait):
    g_ref, all_ref, stage, send_a, recv_a, send_b, recv_b = refs
    nx, ny, nz = sizes
    gx, gy, gz = [lax.axis_index(name) for name in ("gx", "gy", "gz")]
    plane = plane_peers(nx, nz)

    def first(k, x, z, peer):
        return pltpu.make_async_remote_copy(
            src_ref=g_ref,
            dst_ref=stage.at[x, pl.ds(pl.multiple_of(z * 8, 8), 8)],
            send_sem=send_a.at[k],
            recv_sem=recv_a.at[k],
            device_id=peer,
            device_id_type=MESH,
        )

    def second(oy, y):
        return pltpu.make_async_remote_copy(
            src_ref=all_ref.at[gy],
            dst_ref=all_ref.at[y],
            send_sem=send_b.at[oy],
            recv_sem=recv_b.at[oy],
            device_id=(gx, lax.rem(gy + oy, ny), gz),
            device_id_type=MESH,
        )

    for k, (ox, oz) in enumerate(plane):
        first(k, gx, gz, (lax.rem(gx + ox, nx), gy, lax.rem(gz + oz, nz))).start()
    stage[gx, pl.ds(pl.multiple_of(gz * 8, 8), 8)] = g_ref[...]
    first_wait()
    for k, (ox, oz) in enumerate(plane):
        peer = (lax.rem(gx + ox, nx), gy, lax.rem(gz + oz, nz))
        first(k, lax.rem(gx + nx - ox, nx), lax.rem(gz + nz - oz, nz), peer).wait_recv()
    all_ref[gy] = stage[...].astype(BF)
    for oy in range(1, ny):
        second(oy, gy).start()
    second_wait()
    for k, (ox, oz) in enumerate(plane):
        first(k, gx, gz, (lax.rem(gx + ox, nx), gy, lax.rem(gz + oz, nz))).wait_send()
    for oy in range(1, ny):
        second(oy, lax.rem(gy + ny - oy, ny)).wait_recv()
    for oy in range(1, ny):
        second(oy, gy).wait_send()


def reduce_round(sizes, refs, waits):
    pay_ref, out_ref, ra, rb, send_a, recv_a, send_b, recv_b, send_c, recv_c = refs
    nx, ny, nz = sizes
    gx, gy, gz = [lax.axis_index(name) for name in ("gx", "gy", "gz")]
    mine = gx * nz + gz
    plane = plane_peers(nx, nz)

    def ahead(ox, oz):
        return lax.rem(gx + ox, nx), lax.rem(gz + oz, nz)

    def behind(ox, oz):
        return lax.rem(gx + nx - ox, nx), lax.rem(gz + nz - oz, nz)

    def scatter(k, ox, oz, slot):
        x, z = ahead(ox, oz)
        return pltpu.make_async_remote_copy(
            src_ref=pay_ref.at[x * nz + z],
            dst_ref=ra.at[slot],
            send_sem=send_a.at[k],
            recv_sem=recv_a.at[k],
            device_id=(x, gy, z),
            device_id_type=MESH,
        )

    def across(oy, slot):
        return pltpu.make_async_remote_copy(
            src_ref=rb.at[gy],
            dst_ref=rb.at[slot],
            send_sem=send_b.at[oy],
            recv_sem=recv_b.at[oy],
            device_id=(gx, lax.rem(gy + oy, ny), gz),
            device_id_type=MESH,
        )

    def spread(k, ox, oz, slot):
        x, z = ahead(ox, oz)
        return pltpu.make_async_remote_copy(
            src_ref=out_ref.at[mine],
            dst_ref=out_ref.at[slot],
            send_sem=send_c.at[k],
            recv_sem=recv_c.at[k],
            device_id=(x, gy, z),
            device_id_type=MESH,
        )

    for k, (ox, oz) in enumerate(plane):
        scatter(k, ox, oz, mine).start()
    ra[mine] = pay_ref[mine]
    waits[0]()
    for k, (ox, oz) in enumerate(plane):
        x, z = behind(ox, oz)
        scatter(k, ox, oz, x * nz + z).wait_recv()
    rb[gy] = jnp.sum(ra[...], axis=0)
    for oy in range(1, ny):
        across(oy, gy).start()
    waits[1]()
    for k, (ox, oz) in enumerate(plane):
        scatter(k, ox, oz, mine).wait_send()
    for oy in range(1, ny):
        across(oy, lax.rem(gy + ny - oy, ny)).wait_recv()
    out_ref[mine] = jnp.sum(rb[...], axis=0)
    for k, (ox, oz) in enumerate(plane):
        spread(k, ox, oz, mine).start()
    waits[2]()
    for oy in range(1, ny):
        across(oy, gy).wait_send()
    for k, (ox, oz) in enumerate(plane):
        x, z = behind(ox, oz)
        spread(k, ox, oz, x * nz + z).wait_recv()
    for k, (ox, oz) in enumerate(plane):
        spread(k, ox, oz, mine).wait_send()


def fold(ref, i, tiles):
    block = jnp.concatenate(tiles, axis=0)
    outs = block.shape[1]
    ref[pl.ds(i * outs, outs)] = block.T.astype(BF)


def prepare_weights(r):
    for c in range(16):
        r.wrows[pl.ds(c, 27, stride=16)] = r.wf_in[c].astype(F32).T
    for i in range(3):
        r.wf[pl.ds(16 * i, 16)] = r.wrows[pl.ds(144 * i, 144)].T.astype(BF)
        down = [r.wd_in[9 * i + jk].astype(F32) for jk in range(9)]
        up = [r.wu_in[9 * i + jk].astype(F32).T for jk in range(9)]
        down_back = [r.wd_in[26 - 9 * i - jk].astype(F32).T for jk in range(9)]
        up_back = [r.wu_in[26 - 9 * i - jk].astype(F32) for jk in range(9)]
        fold(r.wd, i, down)
        fold(r.wu, i, up)
        fold(r.wdt, i, down_back)
        fold(r.wut, i, up_back)


def arrange_volume(r):
    spot = lane_of(16) % 64

    def plane(x, edges):
        low, high = edges
        for t, tile in enumerate(plane_rows(r.vol[:, x])):
            r.v[x, t] = tile
            wide = tile.astype(F32)
            at = t * 8 + x
            low = jnp.where(spot == at, turn(wide, at), low)
            high = jnp.where(spot == at, turn(wide, at - 63), high)
        return low, high

    zero = jnp.zeros((16, LANES), F32)
    low, high = lax.fori_loop(0, 8, plane, (zero, zero))
    r.ve[0] = low.astype(BF)
    r.ve[1] = high.astype(BF)


def arrange_cotangent(r):
    def plane(x, _):
        for t, tile in enumerate(plane_rows(r.cot[:, x])):
            r.ct[x, t] = tile
        return 0

    lax.fori_loop(0, 8, plane, 0)
    sums = pool_matrix()
    r.sums[...] = sums
    r.pg[...] = pool_tiles(r.ct, sums).astype(BF).reshape(4, 2, 16, LANES)


def fine_forward(r):
    spot = lane_of(16) % 64

    def rows(x, _):
        dx, sx = (x + 7) // 8, lax.rem(x + 7, 8)
        stacks = []
        for t in range(10):
            dy, sy = (t + 7) // 8, (t + 7) % 8
            at = sy * 8 + sx
            tile = r.vp[x, t]
            left = turn(r.vel[dx, dy], -at)
            right = turn(r.ver[dx, dy], 63 - at)
            before = jnp.where(spot == 0, left, turn(tile, 1))
            after = jnp.where(spot == 63, right, turn(tile, -1))
            stacks.append(jnp.concatenate([before, tile, after], axis=0))
        for t in range(9):
            if t > 0:
                r.v3[x, 2 * t - 1] = stacks[t]
            r.v3[x, 2 * t] = between(stacks[t], stacks[t + 1])
        return 0

    lax.fori_loop(0, 10, rows, 0)
    weight = r.wf[...]

    def convs(g, _):
        for x, pre in conv(weight, r.v3, 0, 8, (4 * g, 4 * g + 2)):
            act = (pre * sigmoid(pre)).astype(BF)
            for b in range(2):
                r.pre[x, 2 * g + b] = pre[:, b * LANES : (b + 1) * LANES]
                r.act[x, 2 * g + b] = act[:, b * LANES : (b + 1) * LANES]
        return 0

    lax.fori_loop(0, 4, convs, 0)

    sums = r.sums[...]
    lane = lane_of(32)
    low = jnp.zeros((32, LANES), F32)
    high = low
    pooled = (pool_tiles(r.act, sums) * 0.125).astype(BF).reshape(4, 2, 16, LANES)
    for x in range(4):
        for half in range(2):
            tile = jnp.concatenate([pooled[x, half], r.pg[x, half]], axis=0)
            r.m[x, half] = tile
            wide = tile.astype(F32)
            for q in range(4):
                at = (q % 2) * 64 + (x * 4 + 2 * half + q // 2) * 4
                here = (lane >= at) & (lane < at + 4)
                low = jnp.where(here, turn(wide, at - 32 * q), low)
                high = jnp.where(here, turn(wide, at - 32 * q - 28), high)
    r.me[0] = low.astype(BF)
    r.me[1] = high.astype(BF)


def mid_rows(r, first, last):
    lane = lane_of(32)
    spot = lane % 64
    none = jnp.zeros((32, LANES), BF)

    def rows(x, _):
        dx, sx = x // 4, lax.rem(x, 4)
        pairs = []
        for a in range(8):
            dy, sy = (a + 2) // 4, (a + 2) % 4
            tile = r.mp[x, a // 2]
            q = 2 * (a % 2)
            base = jnp.where(lane < 64, turn(tile, 8 - 32 * q), turn(tile, 40 - 32 * q))
            at = (sx * 4 + sy) * 4
            right = turn(r.mer[dx, dy], 40 - at)
            left = turn(r.mel[dx, dy], 4 - at)
            row = jnp.where(spot < 44, right, none)
            row = jnp.where(spot < 40, base, row)
            row = jnp.where(spot < 8, left, row)
            row = jnp.where(spot < 4, none, row)
            r.pgp[x, a] = row[16:]
            pairs.append(row[:16])
        store_taps(r.pm3, x, pairs)
        r.pm3[x, 15] = jnp.zeros((48, LANES), BF)
        r.pm3[x, 16] = jnp.zeros((48, LANES), BF)
        return 0

    lax.fori_loop(first, last, rows, 0)


def mid_convs(r, sizes, first, planes, groups):
    nx, ny, nz = sizes
    gx, gy, gz = position()
    lane = lane_of(32)
    weight = r.wd[...]
    cell = lane % 64 - 8
    mid = cell + gz * 32
    inside = (cell >= -3) & (cell < 35) & (mid >= 0) & (mid < 32 * nz)
    second = lane // 64

    def convs(g, _):
        for x, both in conv(weight, r.pm3, first, planes, (4 * g, 4 * g + 2)):
            at_x = gx * 4 + x - 3
            for b in range(2):
                pre = both[:, b * LANES : (b + 1) * LANES]
                at_y = gy * 8 + 4 * g + 2 * b - 3 + second
                keep = inside & (at_y >= 0) & (at_y < 8 * ny)
                keep = keep & (at_x >= 0) & (at_x < 4 * nx)
                sig = sigmoid(pre)
                r.am[x, 2 * g + b] = jnp.where(keep, pre * sig, 0.0).astype(BF)
                r.dsm[x, 2 * g + b] = jnp.where(keep, slope(pre, sig), 0.0).astype(BF)
        return 0

    lax.fori_loop(*groups, convs, 0)


def mid_own(r, sizes):
    mid_rows(r, 3, 9)
    mid_convs(r, sizes, 3, 4, (0, 3))
    halves = [
        jnp.concatenate([r.am[3 + a, 1 + 2 * h + m] for a in range(4) for m in range(3)], axis=1)
        for h in range(2)
    ]
    cells = jnp.concatenate(halves + [jnp.zeros((64, 12 * LANES), BF)], axis=0)
    col = lax.broadcasted_iota(jnp.int32, (8, 12 * LANES), 1)
    third, upper = col // LANES % 3, col // 64 % 2
    hit = coarse_sum_matrix(12) & ((third == 1) | ((third == 0) == (upper == 1)))
    pooled = dot_nt(jnp.where(hit, 1.0, 0.0).astype(BF), cells) * (1.0 / 64.0)
    r.pc[...] = pooled.astype(BF).astype(F32)


def mid_halo(r, sizes):
    mid_rows(r, 0, 3)
    mid_rows(r, 9, 12)
    mid_convs(r, sizes, 0, 3, (0, 4))
    mid_convs(r, sizes, 7, 3, (0, 4))
    mid_convs(r, sizes, 3, 4, (3, 4))


def near_rows(sizes, count):
    ny = sizes[1]
    have = min(count, ny)
    start = lax.axis_index("gy") - count // 2
    return jnp.minimum(jnp.maximum(start, 0), ny - have), have


def lift_row(r, sizes, y):
    for x in range(sizes[0]):
        for y2 in range(2):
            pre = dot(r.pcg[y, x], r.wide_lift[y2])
            act = (pre * sigmoid(pre)).astype(BF)
            r.alc[x, y, y2] = act
            store_coarse_taps(r.al3, (x + 1, 2 * y + y2 + 1), act.astype(F32))


def coarse_forward(r, sizes, y, have):
    nx, cells = sizes[0], 8 * sizes[2]
    rows = nx * 2 * have * cells
    for i in range(3):
        for j in range(3):
            block = r.al3[pl.ds(i, nx), pl.ds(2 * y + j, 2 * have)].reshape(rows, 768)
            part = dot(block, r.wc[3 * i + j])
            if i + j == 0:
                r.acc[pl.ds(0, rows)] = part
            else:
                r.acc[pl.ds(0, rows)] += part
    per = 2 * have * cells
    for x in range(nx):
        pre = r.acc[pl.ds(x * per, per)]
        sig = sigmoid(pre)
        r.actc[x, pl.ds(y, have)] = (pre * sig).astype(BF).reshape(have, 2, cells, 256)
        r.dsc[x, pl.ds(y, have)] = slope(pre, sig).astype(BF).reshape(have, 2, cells, 256)


def join_planes(r, first, last):
    lower_row = lane_of(32) < 64

    def join(x, _):
        pairs = []
        for m in range(7):
            lower = r.cos[(x + 1) // 4, (2 * m + 1) // 4]
            upper = r.cos[(x + 1) // 4, (2 * m + 2) // 4]
            row = r.am[x, m].astype(F32) + jnp.where(lower_row, lower, upper)
            pairs.append(row.astype(BF))
        store_taps(r.j3, x, pairs)
        return 0

    lax.fori_loop(first, last, join, 0)


def up_planes(r, scale, first, planes):
    cell = lane_of(16) % 64 - 8
    near = (cell >= -2) & (cell < 34)
    weight = r.wu[...]

    def up(g, _):
        for x, both in conv(weight, r.j3, first, planes, (4 * g, 4 * g + 2)):
            for b in range(2):
                pre = both[:, b * LANES : (b + 1) * LANES]
                sig = sigmoid(pre)
                r.su[x, 2 * g + b] = (pre * sig).astype(BF)
                pooled = r.pgp[x + 2, 2 * g + b + 1].astype(F32) * scale
                grad = jnp.where(near, pooled * slope(pre, sig), 0.0)
                r.guo[x, 2 * g + b] = grad.astype(BF)
        return 0

    lax.fori_loop(0, 3, up, 0)

    def stack(x, _):
        store_taps(r.gu3, x, [r.guo[x, m] for m in range(6)])
        return 0

    lax.fori_loop(first, first + planes, stack, 0)


def up_back_planes(r, first, planes):
    weight_t = r.wut[...]
    for starts in ((0, 2), (4, 6), (8,)):
        for x, both in conv(weight_t, r.gu3, first, planes, starts):
            for b, y in enumerate(starts):
                r.gj[x, y // 2] = both[:, b * LANES : (b + 1) * LANES]


def up_halo(r, scale):
    join_planes(r, 0, 1)
    join_planes(r, 9, 10)
    for x in (0, 7):
        up_planes(r, scale, x, 1)
    for x in (0, 5):
        up_back_planes(r, x, 1)


def up_forward(r, sizes, scale):
    cells = 8 * sizes[2]
    gz = lax.axis_index("gz")
    start, have = near_rows(sizes, 5)

    def lift(o, _):
        lift_row(r, sizes, start + o)
        return 0

    lax.fori_loop(0, have, lift, 0)
    coarse_forward(r, sizes, *near_rows(sizes, 3))

    spread = coarse_grow_matrix(cells, gz)
    for dx, dy, x, y, y2, keep in near_cells(sizes):
        out = dot_nt(r.wp[...], r.actc[x, y, y2]).astype(BF)
        r.cos[dx, dy] = dot(out, spread) * keep

    join_planes(r, 1, 9)
    up_planes(r, scale, 1, 6)
    up_back_planes(r, 1, 4)

    first = lane_of(32) < 64
    totals = []
    for h in range(2):
        total = None
        for a in range(4):
            lower, middle, upper = [r.gj[1 + a, 2 * h + m] for m in range(3)]
            row = middle + jnp.where(first, upper, lower)
            total = row if total is None else total + row
        totals.append(total)
    total = jnp.concatenate(totals + [jnp.zeros((64, LANES), F32)], axis=0)
    head = total.astype(BF)
    tail = (total - head.astype(F32)).astype(BF)
    sums = jnp.where(coarse_sum_matrix(1), 1.0, 0.0).astype(BF)
    r.gc[...] = (dot_nt(sums, head) + dot_nt(sums, tail)).astype(BF).astype(F32)


def up_taps(r):
    cell = lane_of(16) % 64 - 8
    own = (cell >= 0) & (cell < 32)
    r.accu[...] = jnp.zeros(r.accu.shape, F32)
    grads = [
        jnp.concatenate(
            [jnp.where(own, r.guo[x + 2, m + 1].astype(F32), 0.0) for m in range(4)], axis=1
        ).astype(BF)
        for x in range(4)
    ]
    none = jnp.zeros((16, 4 * LANES), BF)
    for x in range(6):
        left = [grads[x - i] if 0 <= x - i < 4 else none for i in range(3)]
        right = [three(r.j3, x + 2, 2 * m + 2) for m in range(4)]
        r.accu[:, pl.ds(0, 288)] += dot_nt(
            jnp.concatenate(left, axis=0), jnp.concatenate(right, axis=1)
        )


def decode(r):
    grow = grow_matrix()

    def plane(x, _):
        rows = jnp.concatenate([r.su[x + 2, m + 1] for m in range(4)], axis=0)
        grown = dot(rows, grow)
        for a in range(2):
            for t in range(8):
                add = grown[16 * (t // 2) : 16 * (t // 2) + 16, (t % 2) * LANES :][:, :LANES]
                tile = r.act[2 * x + a, t].astype(F32) + add
                r.plane[2 * t] = tile.astype(BF)
                r.plane[2 * t + 1] = turn(tile, 64).astype(BF)
            r.dec[:, 2 * x + a] = jnp.swapaxes(r.plane[...], 0, 1)[:, :, :64]
        return 0

    lax.fori_loop(0, 4, plane, 0)


def coarse_grad_row(r, sizes, y):
    for x in range(sizes[0]):
        for y2 in range(2):
            grad = dot(r.gcg[y, x], r.wide_proj[y2]) * r.dsc[x, y, y2].astype(F32)
            grad = grad.astype(BF).astype(F32)
            store_coarse_taps(r.gp3, (x + 2, 2 * y + y2 + 2), grad)


def pay_rows(r, start, block):
    per = r.pay.shape[1]
    done = 0
    while done < block.shape[0]:
        part, at = divmod(start + done, per)
        size = min(per - at, block.shape[0] - done)
        r.pay[part, pl.ds(at, size)] = block[done : done + size]
        done += size


def backward(r, sizes, scale):
    cells = 8 * sizes[2]
    gx, gy, gz = position()
    start, have = near_rows(sizes, 3)

    def coarse(o, _):
        coarse_grad_row(r, sizes, start + o)
        return 0

    lax.fori_loop(0, have, coarse, 0)
    rows = 12 * cells
    for i in range(3):
        for j in range(3):
            block = r.gp3[pl.ds(gx + i, 3), pl.ds(2 * gy + j, 4)].reshape(rows, 768)
            part = dot(block, r.wct[3 * i + j])
            if i + j == 0:
                r.acc[pl.ds(0, rows)] = part
            else:
                r.acc[pl.ds(0, rows)] += part

    spread = coarse_grow_matrix(cells, gz)
    own = lax.broadcasted_iota(jnp.int32, (cells, 256), 0) // 8 == gz
    for at, (dx, dy, x, y, y2, keep) in enumerate(near_cells(sizes)):
        pre = dot(r.pcg[y, x], r.wide_lift[y2])
        grad = (r.acc[pl.ds(at * cells, cells)] * slope(pre, sigmoid(pre))).astype(BF)
        out = dot_nt(r.wl[...], grad).astype(BF)
        r.cos[dx, dy] = dot(out, spread) * (keep * (1.0 / 64.0))
        if dx == 1 and dy in (1, 2):
            masked = jnp.where(own, grad.astype(F32), 0.0).astype(BF)
            r.pairs[y2] = dot_tn(r.pcg[y, x], masked)
    lifts = r.pairs[0, :32] + r.pairs[1, 32:64]
    for b in range(2):
        pay_rows(r, 432 + 32 * b, lifts[:, b * LANES : (b + 1) * LANES])

    first = lane_of(32) < 64

    def join(x, _):
        pairs = []
        for n in range(5):
            lower = r.cos[(x + 3) // 4, (2 * n + 3) // 4]
            upper = r.cos[(x + 3) // 4, (2 * n + 4) // 4]
            row = r.gj[x, n] + jnp.where(first, lower, upper)
            row = row * r.dsm[x + 2, n + 1].astype(F32)
            pairs.append(row.astype(BF))
        store_taps(r.gm3, x, pairs)
        return 0

    lax.fori_loop(0, 6, join, 0)

    weight_t = r.wdt[...]
    for starts in ((0, 2), (4, 6)):
        for x, both in conv(weight_t, r.gm3, 0, 4, starts):
            for b, y in enumerate(starts):
                r.gpm[x, pl.ds(8 * y, 16)] = both[:, b * LANES : (b + 1) * LANES].astype(BF)

    grow = grow_matrix()
    for x in (0, 1, 10, 11):
        r.gf[x] = jnp.zeros(r.gf.shape[1:], BF)

    def fine(x, _):
        grown = dot(r.gpm[x], grow) * 0.125
        for a in range(2):
            for t in range(8):
                add = grown[16 * (t // 2) : 16 * (t // 2) + 16, (t % 2) * LANES :][:, :LANES]
                pre = r.pre[2 * x + a, t]
                grad = r.ct[2 * x + a, t].astype(F32) * scale + add
                grad = (grad * slope(pre, sigmoid(pre))).astype(BF)
                r.gf[2 * x + a + 2, :, pl.ds(t * LANES, LANES)] = grad
        return 0

    lax.fori_loop(0, 4, fine, 0)

    r.accd[...] = jnp.zeros(r.accd.shape, F32)
    spot = lane_of(32) % 64
    inner = (spot >= 8) & (spot < 40)
    grads = [
        jnp.concatenate(
            [
                jnp.where(inner, r.gm3[x + 1, 2 * m + 1, pl.ds(32, 32)].astype(F32), 0.0)
                for m in range(4)
            ],
            axis=1,
        ).astype(BF)
        for x in range(4)
    ]
    none = jnp.zeros((32, 4 * LANES), BF)
    for x in range(6):
        left = [grads[x - i] if 0 <= x - i < 4 else none for i in range(3)]
        right = [three(r.pm3, x + 3, 2 * m + 3) for m in range(4)]
        r.accd[:, pl.ds(0, 144)] += dot_nt(
            jnp.concatenate(left, axis=0), jnp.concatenate(right, axis=1)
        )

    r.accf[...] = jnp.zeros(r.accf.shape, F32)

    def taps_fine(n, _):
        planes = (2 * n, 2 * n + 1)
        left = [jnp.concatenate([r.gf[x + 2 - i] for x in planes], axis=1) for i in range(3)]
        right = [three(r.v3, x, 2 * t) for x in planes for t in range(8)]
        r.accf[:, pl.ds(0, 144)] += dot_nt(
            jnp.concatenate(left, axis=0), jnp.concatenate(right, axis=1)
        )
        return 0

    lax.fori_loop(0, 5, taps_fine, 0)

    for b in range(2):
        pay_rows(r, 48 * b, r.accf[:, b * LANES : (b + 1) * LANES])
    for b in range(3):
        pay_rows(r, 96 + 48 * b, r.accu[:, b * LANES : (b + 1) * LANES])
    for b in range(2):
        pay_rows(r, 240 + 96 * b, r.accd[:, b * LANES : (b + 1) * LANES])
    pay_rows(r, 496, jnp.zeros((16, LANES), F32))


def coarse_taps(r, sizes, t):
    nx, ny, nz = sizes
    count = nx * ny * 16 * nz
    i, j = t // 3, lax.rem(t, 3)
    block = r.gp3[pl.ds(3 - i, nx), pl.ds(3 - j, 2 * ny)].reshape(count, 768)
    out = dot(r.cells_t[...], block)
    for k in range(3):
        r.gwc[3 * t + k] = out[:, 256 * (2 - k) : 256 * (3 - k)].astype(BF)


def proj_grad(r, sizes):
    nx, ny, nz = sizes
    cells = 8 * nz
    r.pairs[...] = jnp.zeros(r.pairs.shape, F32)

    def plane(x, _):
        for y2 in range(2):
            grads = r.gcg[:, x].reshape(ny * cells, LANES)
            r.pairs[y2] += dot_tn(grads, r.actc[x, :, y2].reshape(ny * cells, 256))
        return 0

    lax.fori_loop(0, nx, plane, 0)
    r.gwp[...] = r.pairs[0, :32] + r.pairs[1, 32:64]


def step_kernel(sizes, scale, names, *refs):
    nx, ny, nz = sizes
    count = nx * ny * 16 * nz
    r = types.SimpleNamespace(**dict(zip(names, refs, strict=True)))
    gx, gy, gz = position()
    pair = nz % 2 == 0
    mine = lax.rem(gz, 2) if pair else 0
    other = (gx, gy, gz + 1 - 2 * mine) if pair else None

    fetch = [
        pltpu.make_async_copy(source, target, r.fetched.at[n])
        for n, (source, target) in enumerate(
            ((r.vol_in, r.vol), (r.cot_in, r.cot), (r.wc_in, r.wc))
        )
    ]
    for copy in fetch:
        copy.start()

    def arrange():
        fetch[0].wait()
        arrange_volume(r)

    greet(sizes, arrange)

    def first_wait():
        prepare_weights(r)
        fetch[1].wait()
        arrange_cotangent(r)
        place_weight(r.wide_lift, r.wl[...])
        place_weight(r.wide_proj, r.wp[...])

    halo_round(sizes, 1, 1, (r.v, r.ve, r.vp, r.ver, r.vel, r.vsend, r.vrecv), first_wait)
    fine_forward(r)

    def second_wait():
        zero_rim(r.al3, 1)
        zero_rim(r.gp3, 2)
        fetch[2].wait()

        def turn_weights(t, _):
            for k in range(3):
                block = r.wc[8 - t, pl.ds(256 * (2 - k), 256)]
                r.wct[t, pl.ds(256 * k, 256)] = block.T
            return 0

        lax.fori_loop(0, 9, turn_weights, 0)

    halo_round(sizes, 4, 1, (r.m, r.me, r.mp, r.mer, r.mel, r.msend, r.mrecv), second_wait)
    mid_own(r, sizes)
    sems = (r.ga_send, r.ga_recv, r.gb_send, r.gb_recv)
    gather_round(sizes, (r.pc, r.pcg, r.pstage) + sems, lambda: mid_halo(r, sizes), nothing)
    up_forward(r, sizes, scale)

    decoded = pltpu.make_async_copy(r.dec, r.dec_out, r.fetched.at[3])

    def third_wait():
        up_halo(r, scale)
        up_taps(r)
        decode(r)
        decoded.start()

    far_start, far_first = near_rows(sizes, 3)

    def far_row(n, whose):
        step = 2 if pair else 1
        return lax.rem(far_start + far_first + step * n + whose, ny)

    def far_count(whose):
        return (ny - far_first + 1 - whose) // 2 if pair else ny - far_first

    def far_copies(n, whose):
        y = far_row(n, whose)
        return [
            pltpu.make_async_remote_copy(
                src_ref=ref.at[:, pl.ds(y, 1)],
                dst_ref=ref.at[:, pl.ds(y, 1)],
                send_sem=r.far_send.at[part, n],
                recv_sem=r.far_recv.at[part, n],
                device_id=other,
                device_id_type=MESH,
            )
            for part, ref in enumerate((r.actc, r.dsc))
        ]

    def fourth_wait():
        start, have = near_rows(sizes, 5)

        def lift(o, _):
            lift_row(r, sizes, lax.rem(start + o, ny))
            return 0

        lax.fori_loop(have, ny, lift, 0)

        def coarse(n, _):
            coarse_forward(r, sizes, far_row(n, mine), 1)
            if pair:
                for copy in far_copies(n, mine):
                    copy.start()
            return 0

        lax.fori_loop(0, far_count(mine), coarse, 0)

    sems = (r.ha_send, r.ha_recv, r.hb_send, r.hb_recv)
    gather_round(sizes, (r.gc, r.gcg, r.gstage) + sems, third_wait, fourth_wait)
    backward(r, sizes, scale)

    half = 5 if pair else 9

    def taps_count(whose):
        return half - whose

    def keep_taps(n):
        taps = pl.ds(3 * (n + half * mine), 3)
        return pltpu.make_async_copy(r.gwc.at[taps], r.gwc_out.at[taps], r.kept.at[n])

    def send_taps(n, whose):
        taps = pl.ds(3 * (n + half * whose), 3)
        return pltpu.make_async_remote_copy(
            src_ref=r.gwc.at[taps],
            dst_ref=r.gwc_out.at[taps],
            send_sem=r.tap_send.at[n],
            recv_sem=r.tap_recv.at[n],
            device_id=other,
            device_id_type=MESH,
        )

    def do_taps(first, last):
        def taps(n, _):
            coarse_taps(r, sizes, n + half * mine)
            keep_taps(n).start()
            if pair:
                send_taps(n, mine).start()
            return 0

        lax.fori_loop(first, last, taps, 0)

    def wait_a():
        if pair:

            def arrived(n, _):
                for copy in far_copies(n, 1 - mine):
                    copy.wait_recv()
                return 0

            lax.fori_loop(0, far_count(1 - mine), arrived, 0)
        start, have = near_rows(sizes, 3)

        def coarse(o, _):
            coarse_grad_row(r, sizes, lax.rem(start + o, ny))
            return 0

        lax.fori_loop(have, ny, coarse, 0)
        r.cells_t[...] = r.alc[...].reshape(count, 256).T
        do_taps(0, 1)

    def wait_b():
        do_taps(1, 3)

    def wait_c():
        do_taps(3, taps_count(mine))
        proj_grad(r, sizes)

    sems = (r.ra_send, r.ra_recv, r.rb_send, r.rb_recv, r.rc_send, r.rc_recv)
    reduce_round(sizes, (r.pay, r.red, r.ra, r.rb) + sems, (wait_a, wait_b, wait_c))

    def finish(n, _):
        keep_taps(n).wait()
        if pair:
            send_taps(n, mine).wait_send()
        return 0

    lax.fori_loop(0, taps_count(mine), finish, 0)
    decoded.wait()
    if pair:

        def sent(n, _):
            for copy in far_copies(n, mine):
                copy.wait_send()
            return 0

        def landed(n, _):
            send_taps(n, 1 - mine).wait_recv()
            return 0

        lax.fori_loop(0, far_count(mine), sent, 0)
        lax.fori_loop(0, taps_count(1 - mine), landed, 0)


def last_kernel(
    gwc_in,
    red_ref,
    gwp_ref,
    wc_out,
    wf_out,
    wd_out,
    wl_out,
    wp_out,
    wu_out,
    rows,
    narrow,
    wide,
    load_sem,
    store_sem,
):
    blocks = [pl.ds(3 * n, 3) for n in range(9)]
    loads = [
        pltpu.make_async_copy(gwc_in.at[block], narrow.at[block], load_sem.at[n])
        for n, block in enumerate(blocks)
    ]
    stores = [
        pltpu.make_async_copy(wide.at[block], wc_out.at[block], store_sem.at[n])
        for n, block in enumerate(blocks)
    ]
    for load in loads:
        load.start()
    for n, block in enumerate(blocks):
        loads[n].wait()
        wide[block] = narrow[block].astype(F32)
        stores[n].start()

    def columns(start, blocks, count):
        return jnp.concatenate(
            [red_ref[pl.ds(start + count * b, count)] for b in range(blocks)], axis=1
        )

    table = columns(0, 2, 48)
    for i in range(3):
        rows[pl.ds(144 * i, 144)] = table[16 * i : 16 * i + 16, :144].T
    for c in range(16):
        wf_out[c] = rows[pl.ds(c, 27, stride=16)].T
    table = columns(96, 3, 48)
    for i in range(3):
        for jk in range(9):
            wu_out[9 * i + jk] = table[16 * i : 16 * i + 16, 32 * jk : 32 * jk + 32]
    table = columns(240, 2, 96)
    for i in range(3):
        part = table[32 * i : 32 * i + 32, :144]
        wd_out[pl.ds(9 * i, 9)] = part.T.reshape(9, 16, 32)
    wl_out[...] = columns(432, 2, 32)
    wp_out[...] = gwp_ref[...]
    for store in stores:
        store.wait()


VMEM = pl.BlockSpec(memory_space=pltpu.VMEM)
HBM = pl.BlockSpec(memory_space=pl.ANY)


def shards(sizes, volume, w_fine, w_down, w_lift, w_coarse, w_proj, w_up, cotangent):
    nx, ny, nz = sizes
    scale = 1.0 / math.sqrt(8 * nx * 16 * ny * 64 * nz)
    cells = 8 * nz
    parts = nx * nz
    per = 512 // parts
    grid = (nx, ny, 2, cells, 256)
    gathered = (ny, nx, cells, LANES)
    ins = {
        "wf_in": jnp.transpose(w_fine, (1, 2, 0)),
        "wd_in": w_down,
        "wu_in": jnp.transpose(w_up, (0, 2, 1)),
        "wl": w_lift,
        "wp": jnp.transpose(w_proj),
        "vol_in": volume,
        "cot_in": cotangent,
        "wc_in": w_coarse.reshape(9, 768, 256),
    }
    outs = {
        "red": ((parts, per, LANES), F32),
        "gwp": ((32, 256), F32),
        "dec_out": ((16, 8, 16, 64), BF),
        "gwc_out": ((27, 256, 256), BF),
    }
    narrow = {
        "vol": (16, 8, 16, 64),
        "cot": (16, 8, 16, 64),
        "dec": (16, 8, 16, 64),
        "v": (8, 8, 16, LANES),
        "ve": (2, 16, LANES),
        "vp": (10, 10, 16, LANES),
        "ver": (3, 3, 16, LANES),
        "vel": (3, 3, 16, LANES),
        "ct": (8, 8, 16, LANES),
        "sums": (8 * LANES, LANES),
        "pg": (4, 2, 16, LANES),
        "wf": (48, 144),
        "wd": (96, 144),
        "wu": (48, 288),
        "wdt": (48, 288),
        "wut": (96, 144),
        "v3": (10, 17, 48, LANES),
        "act": (8, 8, 16, LANES),
        "m": (4, 2, 32, LANES),
        "me": (2, 32, LANES),
        "mp": (12, 4, 32, LANES),
        "mer": (3, 3, 32, LANES),
        "mel": (3, 3, 32, LANES),
        "pm3": (12, 17, 48, LANES),
        "pgp": (12, 8, 16, LANES),
        "am": (10, 8, 32, LANES),
        "dsm": (10, 8, 32, LANES),
        "pcg": gathered,
        "gcg": gathered,
        "wc": (9, 768, 256),
        "wct": (9, 768, 256),
        "wide_lift": (2, LANES, 256),
        "wide_proj": (2, LANES, 256),
        "al3": (nx + 2, 2 * ny + 2, cells, 768),
        "gp3": (nx + 4, 2 * ny + 4, cells, 768),
        "alc": grid,
        "actc": grid,
        "dsc": grid,
        "j3": (10, 13, 96, LANES),
        "guo": (8, 6, 16, LANES),
        "gu3": (8, 11, 48, LANES),
        "su": (8, 6, 16, LANES),
        "plane": (16, 16, LANES),
        "gm3": (6, 9, 96, LANES),
        "gpm": (4, 64, LANES),
        "gf": (12, 16, 8 * LANES),
        "cells_t": (256, nx * ny * 2 * cells),
        "gwc": (27, 256, 256),
    }
    wide = {
        "wrows": (432, 16),
        "pre": (8, 8, 16, LANES),
        "pc": (8, LANES),
        "pstage": (nx, cells, LANES),
        "acc": (max(nx * 2 * min(3, ny), 12) * cells, 256),
        "cos": (3, 4, 32, LANES),
        "gj": (6, 5, 32, LANES),
        "gc": (8, LANES),
        "gstage": (nx, cells, LANES),
        "accu": (48, 3 * LANES),
        "accf": (48, 2 * LANES),
        "accd": (96, 2 * LANES),
        "pairs": (2, LANES, 256),
        "pay": (parts, per, LANES),
        "ra": (parts, per, LANES),
        "rb": (ny, per, LANES),
    }
    sems = {
        "vsend": 26,
        "vrecv": 26,
        "msend": 26,
        "mrecv": 26,
        "ga_send": parts,
        "ga_recv": parts,
        "gb_send": ny,
        "gb_recv": ny,
        "ha_send": parts,
        "ha_recv": parts,
        "hb_send": ny,
        "hb_recv": ny,
        "ra_send": parts,
        "ra_recv": parts,
        "rb_send": ny,
        "rb_recv": ny,
        "rc_send": parts,
        "rc_recv": parts,
        "kept": 9,
        "tap_send": 9,
        "tap_recv": 9,
        "fetched": 4,
    }
    far = {"far_send": (2, ny), "far_recv": (2, ny)}
    names = list(ins) + list(outs) + list(narrow) + list(wide) + list(sems) + list(far)
    red, gwp, dec, gwc = pl.pallas_call(
        functools.partial(step_kernel, sizes, scale, names),
        out_shape=[jax.ShapeDtypeStruct(shape, kind) for shape, kind in outs.values()],
        in_specs=[VMEM] * (len(ins) - 3) + [HBM] * 3,
        out_specs=[VMEM] * 2 + [HBM] * 2,
        scratch_shapes=[pltpu.VMEM(shape, BF) for shape in narrow.values()]
        + [pltpu.VMEM(shape, F32) for shape in wide.values()]
        + [pltpu.SemaphoreType.DMA((size,)) for size in sems.values()]
        + [pltpu.SemaphoreType.DMA(shape) for shape in far.values()],
        compiler_params=pltpu.CompilerParams(
            vmem_limit_bytes=62 * 1024 * 1024, collective_id=1, has_side_effects=True
        ),
    )(*ins.values())
    shapes = [(27, 256, 256), (16, 16, 27), (27, 16, 32), (32, 256), (32, 256), (27, 16, 32)]

    gwc, gwf, gwd, gwl, gwp, gwu = pl.pallas_call(
        last_kernel,
        out_shape=[jax.ShapeDtypeStruct(shape, F32) for shape in shapes],
        in_specs=[HBM, VMEM, VMEM],
        out_specs=[HBM] + [VMEM] * 5,
        scratch_shapes=[
            pltpu.VMEM((432, 16), F32),
            pltpu.VMEM((27, 256, 256), BF),
            pltpu.VMEM((27, 256, 256), F32),
            pltpu.SemaphoreType.DMA((9,)),
            pltpu.SemaphoreType.DMA((9,)),
        ],
        compiler_params=pltpu.CompilerParams(vmem_limit_bytes=62 * 1024 * 1024),
    )(gwc, red.reshape(512, LANES), gwp)
    gwf = jnp.transpose(gwf, (2, 0, 1))
    gwu = jnp.transpose(gwu, (0, 2, 1))
    return dec, gwf, gwd, gwl, gwc, jnp.transpose(gwp), gwu


def solution(mesh):
    sizes = tuple(mesh.shape[name] for name in ("gx", "gy", "gz"))
    block = P(None, "gx", "gy", "gz")
    return jax.shard_map(
        functools.partial(shards, sizes),
        mesh=mesh,
        in_specs=(block, P(), P(), P(), P(), P(), P(), block),
        out_specs=(block, P(), P(), P(), P(), P(), P()),
        check_vma=False,
    )
```

```python
import functools
import math
import types

import jax
import jax.numpy as jnp
from jax import lax
from jax.experimental import pallas as pl
from jax.experimental.pallas import tpu as pltpu
from jax.sharding import PartitionSpec as P

BF = jnp.bfloat16
F32 = jnp.float32
MESH = pl.DeviceIdType.MESH
LANES = 128


def dot(left, right):
    return jnp.dot(left, right, preferred_element_type=F32)


def dot_nt(left, right):
    return lax.dot_general(left, right, (((1,), (1,)), ((), ())), preferred_element_type=F32)


def dot_tn(left, right):
    return lax.dot_general(left, right, (((0,), (0,)), ((), ())), preferred_element_type=F32)


def sigmoid(values):
    return 0.5 * jnp.tanh(0.5 * values) + 0.5


def slope(values, sig):
    return sig * (1.0 + values * (1.0 - sig))


def lane_of(rows):
    return lax.broadcasted_iota(jnp.int32, (rows, LANES), 1)


def turn(tile, by):
    if isinstance(by, int):
        by = by % LANES
        return tile if by == 0 else pltpu.roll(tile, by, 1)
    return pltpu.roll(tile, lax.rem(by + 4 * LANES, LANES), 1)


def tap_rows(pair):
    return jnp.concatenate([turn(pair, 1), pair, turn(pair, -1)], axis=0)


def between(lower, upper):
    lane = lane_of(lower.shape[0])
    return jnp.where(lane < 64, turn(lower, 64), turn(upper, 64))


def store_taps(ref, x, pairs):
    stacks = [tap_rows(pair) for pair in pairs]
    for n, stack in enumerate(stacks):
        ref[x, 2 * n] = stack
        if n + 1 < len(stacks):
            ref[x, 2 * n + 1] = between(stack, stacks[n + 1])


def three(ref, x, y):
    block = ref[x, pl.ds(y, 3)]
    return block.reshape(3 * block.shape[1], LANES)


def conv(weight, ref, first, planes, starts):
    outs = weight.shape[0] // 3
    parts = []
    for n in range(planes + 2):
        tiles = [three(ref, first + n, y) for y in starts]
        block = tiles[0] if len(tiles) == 1 else jnp.concatenate(tiles, axis=1)
        parts.append(dot(weight, block))
        if n >= 2:
            yield (
                first + n - 2,
                parts[n - 2][:outs] + parts[n - 1][outs : 2 * outs] + parts[n][2 * outs :],
            )


def pool_matrix():
    row = lax.broadcasted_iota(jnp.int32, (8 * LANES, LANES), 0)
    col = lax.broadcasted_iota(jnp.int32, (8 * LANES, LANES), 1)
    hit = (row // 256 == col // 32) & (row % 64 // 2 == col % 32)
    return jnp.where(hit, 1.0, 0.0).astype(BF)


def pool_tiles(ref, sums):
    cells = [
        jnp.concatenate([ref[2 * x + a, 4 * half + q] for q in range(4) for a in range(2)], axis=1)
        for x in range(4)
        for half in range(2)
    ]
    return dot(jnp.concatenate(cells, axis=0), sums)


def grow_matrix():
    row = lax.broadcasted_iota(jnp.int32, (LANES, 2 * LANES), 0)
    col = lax.broadcasted_iota(jnp.int32, (LANES, 2 * LANES), 1)
    hit = (row // 64 == col // LANES) & (row % 64 - 8 == col % 64 // 2)
    return jnp.where(hit, 1.0, 0.0).astype(BF)


def coarse_sum_matrix(tiles):
    row = lax.broadcasted_iota(jnp.int32, (8, tiles * LANES), 0)
    cell = lax.broadcasted_iota(jnp.int32, (8, tiles * LANES), 1) % 64 - 8
    return (cell >= 0) & (cell < 32) & ((cell + 4) // 4 == row + 1)


def coarse_grow_matrix(cells, gz):
    row = lax.broadcasted_iota(jnp.int32, (cells, LANES), 0)
    cell = lax.broadcasted_iota(jnp.int32, (cells, LANES), 1) % 64 - 8
    mid = cell + gz * 32
    hit = (cell >= -3) & (cell < 35) & (mid >= 0) & (row == (mid + 4) // 4 - 1)
    return jnp.where(hit, 1.0, 0.0).astype(BF)


def plane_rows(block):
    rows = jnp.swapaxes(block, 0, 1)
    return [jnp.concatenate([rows[2 * t], rows[2 * t + 1]], axis=1) for t in range(8)]


def place_weight(ref, weight):
    for y2 in range(2):
        ref[y2] = jnp.zeros((LANES, 256), BF)
        ref[y2, pl.ds(32 * y2, 32)] = weight


def store_coarse_taps(ref, at, cells):
    count = cells.shape[0]
    row = lax.broadcasted_iota(jnp.int32, cells.shape, 0)
    before = jnp.where(row > 0, pltpu.roll(cells, 1, 0), 0.0)
    after = jnp.where(row < count - 1, pltpu.roll(cells, count - 1, 0), 0.0)
    ref[at + (slice(None), pl.ds(0, 256))] = before.astype(BF)
    ref[at + (slice(None), pl.ds(256, 256))] = cells.astype(BF)
    ref[at + (slice(None), pl.ds(512, 256))] = after.astype(BF)


def zero_rim(ref, rim):
    planes, rows = ref.shape[:2]

    def clear(x, _):
        for y in list(range(rim)) + list(range(rows - rim, rows)):
            ref[x, y] = jnp.zeros(ref.shape[2:], ref.dtype)
        return 0

    lax.fori_loop(0, planes, clear, 0)

    def clear_plane(y, _):
        for x in list(range(rim)) + list(range(planes - rim, planes)):
            ref[x, y] = jnp.zeros(ref.shape[2:], ref.dtype)
        return 0

    lax.fori_loop(0, rows, clear_plane, 0)


def clamp(at, count):
    return jnp.minimum(jnp.maximum(at, 0), count - 1)


def near_cells(sizes):
    nx, ny, _ = sizes
    gx, gy = lax.axis_index("gx"), lax.axis_index("gy")
    found = []
    for dx in range(3):
        for dy in range(4):
            x, y = gx - 1 + dx, gy + (dy + 1) // 2 - 1
            there = (x >= 0) & (x < nx) & (y >= 0) & (y < ny)
            keep = jnp.where(there, 1.0, 0.0)
            found.append((dx, dy, clamp(x, nx), clamp(y, ny), (dy + 1) % 2, keep))
    return found


def nothing():
    pass


NEIGHBOURS = [
    (dx, dy, dz)
    for dz in (-1, 1, 0)
    for dx in (-1, 0, 1)
    for dy in (-1, 0, 1)
    if (dx, dy, dz) != (0, 0, 0)
]


def position():
    return [lax.axis_index(name) for name in ("gx", "gy", "gz")]


def valid(sizes, steps):
    found = None
    for at, size, step in zip(position(), sizes, steps):
        if step != 0:
            test = at > 0 if step < 0 else at < size - 1
            found = test if found is None else found & test
    return found


def plane_peers(nx, nz):
    return [(ox, oz) for ox in range(nx) for oz in range(nz) if (ox, oz) != (0, 0)]


def greet(sizes, work):
    nx, ny, nz = sizes
    me = gx, gy, gz = position()
    barrier = pltpu.get_barrier_semaphore()
    peers = [(lax.rem(gx + ox, nx), gy, lax.rem(gz + oz, nz)) for ox, oz in plane_peers(nx, nz)]
    peers += [(gx, lax.rem(gy + oy, ny), gz) for oy in range(1, ny)]
    for peer in peers:
        pl.semaphore_signal(barrier, inc=1, device_id=peer, device_id_type=MESH)
    total = 1
    for axis in range(3):
        low = jnp.where(me[axis] > 0, 1, 0)
        high = jnp.where(me[axis] < sizes[axis] - 1, 1, 0)
        total = total * (1 + low + high)
    for steps in NEIGHBOURS:

        @pl.when(valid(sizes, steps))
        def _():
            pl.semaphore_signal(
                barrier,
                inc=1,
                device_id=tuple(me[axis] + steps[axis] for axis in range(3)),
                device_id_type=MESH,
            )

    work()
    pl.semaphore_wait(barrier, total - 1 + len(peers))


def halo_round(sizes, hx, ht, refs, meanwhile):
    a_ref, e_ref, p_ref, er_ref, el_ref, send_sem, recv_sem = refs
    me = [lax.axis_index(name) for name in ("gx", "gy", "gz")]
    planes, tiles = a_ref.shape[:2]

    def part(step, halo, count):
        if step == 0:
            return pl.ds(0, count), pl.ds(halo, count)
        if step > 0:
            return pl.ds(count - halo, halo), pl.ds(0, halo)
        return pl.ds(0, halo), pl.ds(count + halo, halo)

    def copy_of(k, steps):
        dx, dy, dz = steps
        if dz == 0:
            fx, tx = part(dx, hx, planes)
            fy, ty = part(dy, ht, tiles)
            src, dst = a_ref.at[fx, fy], p_ref.at[tx, ty]
        elif dz > 0:
            src, dst = e_ref.at[1], el_ref.at[1 - dx, 1 - dy]
        else:
            src, dst = e_ref.at[0], er_ref.at[1 - dx, 1 - dy]
        return pltpu.make_async_remote_copy(
            src_ref=src,
            dst_ref=dst,
            send_sem=send_sem.at[k],
            recv_sem=recv_sem.at[k],
            device_id=(me[0] + dx, me[1] + dy, me[2] + dz),
            device_id_type=MESH,
        )

    for k, steps in enumerate(NEIGHBOURS):

        @pl.when(valid(sizes, steps))
        def _():
            copy_of(k, steps).start()

    p_ref[pl.ds(hx, planes), pl.ds(ht, tiles)] = a_ref[...]
    for k, steps in enumerate(NEIGHBOURS):
        back = tuple(-step for step in steps)
        dx, dy, dz = steps

        @pl.when(jnp.logical_not(valid(sizes, back)))
        def _():
            if dz == 0:
                _, tx = part(dx, hx, planes)
                _, ty = part(dy, ht, tiles)
                into = p_ref.at[tx, ty]
            elif dz > 0:
                into = el_ref.at[1 - dx, 1 - dy]
            else:
                into = er_ref.at[1 - dx, 1 - dy]
            into[...] = jnp.zeros(into.shape, into.dtype)

    meanwhile()
    for k, steps in enumerate(NEIGHBOURS):
        back = tuple(-step for step in steps)

        @pl.when(valid(sizes, back))
        def _():
            copy_of(k, steps).wait_recv()

    for k, steps in enumerate(NEIGHBOURS):

        @pl.when(valid(sizes, steps))
        def _():
            copy_of(k, steps).wait_send()


def gather_round(sizes, refs, first_wait, second_wait):
    g_ref, all_ref, stage, send_a, recv_a, send_b, recv_b = refs
    nx, ny, nz = sizes
    gx, gy, gz = [lax.axis_index(name) for name in ("gx", "gy", "gz")]
    plane = plane_peers(nx, nz)

    def first(k, x, z, peer):
        return pltpu.make_async_remote_copy(
            src_ref=g_ref,
            dst_ref=stage.at[x, pl.ds(pl.multiple_of(z * 8, 8), 8)],
            send_sem=send_a.at[k],
            recv_sem=recv_a.at[k],
            device_id=peer,
            device_id_type=MESH,
        )

    def second(oy, y):
        return pltpu.make_async_remote_copy(
            src_ref=all_ref.at[gy],
            dst_ref=all_ref.at[y],
            send_sem=send_b.at[oy],
            recv_sem=recv_b.at[oy],
            device_id=(gx, lax.rem(gy + oy, ny), gz),
            device_id_type=MESH,
        )

    for k, (ox, oz) in enumerate(plane):
        first(k, gx, gz, (lax.rem(gx + ox, nx), gy, lax.rem(gz + oz, nz))).start()
    stage[gx, pl.ds(pl.multiple_of(gz * 8, 8), 8)] = g_ref[...]
    first_wait()
    for k, (ox, oz) in enumerate(plane):
        peer = (lax.rem(gx + ox, nx), gy, lax.rem(gz + oz, nz))
        first(k, lax.rem(gx + nx - ox, nx), lax.rem(gz + nz - oz, nz), peer).wait_recv()
    all_ref[gy] = stage[...].astype(BF)
    for oy in range(1, ny):
        second(oy, gy).start()
    second_wait()
    near = sorted({1, ny - 1}) if ny > 1 else []
    for oy in near:
        second(oy, lax.rem(gy + ny - oy, ny)).wait_recv()

    def rest():
        for k, (ox, oz) in enumerate(plane):
            first(k, gx, gz, (lax.rem(gx + ox, nx), gy, lax.rem(gz + oz, nz))).wait_send()
        for oy in range(1, ny):
            if oy not in near:
                second(oy, lax.rem(gy + ny - oy, ny)).wait_recv()
        for oy in range(1, ny):
            second(oy, gy).wait_send()

    return rest


def reduce_round(sizes, refs, waits):
    pay_ref, out_ref, ra, rb, send_a, recv_a, send_b, recv_b, send_c, recv_c = refs
    nx, ny, nz = sizes
    gx, gy, gz = [lax.axis_index(name) for name in ("gx", "gy", "gz")]
    mine = gx * nz + gz
    plane = plane_peers(nx, nz)

    def ahead(ox, oz):
        return lax.rem(gx + ox, nx), lax.rem(gz + oz, nz)

    def behind(ox, oz):
        return lax.rem(gx + nx - ox, nx), lax.rem(gz + nz - oz, nz)

    def scatter(k, ox, oz, slot):
        x, z = ahead(ox, oz)
        return pltpu.make_async_remote_copy(
            src_ref=pay_ref.at[x * nz + z],
            dst_ref=ra.at[slot],
            send_sem=send_a.at[k],
            recv_sem=recv_a.at[k],
            device_id=(x, gy, z),
            device_id_type=MESH,
        )

    def across(oy, slot):
        return pltpu.make_async_remote_copy(
            src_ref=rb.at[gy],
            dst_ref=rb.at[slot],
            send_sem=send_b.at[oy],
            recv_sem=recv_b.at[oy],
            device_id=(gx, lax.rem(gy + oy, ny), gz),
            device_id_type=MESH,
        )

    def spread(k, ox, oz, slot):
        x, z = ahead(ox, oz)
        return pltpu.make_async_remote_copy(
            src_ref=out_ref.at[mine],
            dst_ref=out_ref.at[slot],
            send_sem=send_c.at[k],
            recv_sem=recv_c.at[k],
            device_id=(x, gy, z),
            device_id_type=MESH,
        )

    for k, (ox, oz) in enumerate(plane):
        scatter(k, ox, oz, mine).start()
    ra[mine] = pay_ref[mine]
    waits[0]()
    for k, (ox, oz) in enumerate(plane):
        x, z = behind(ox, oz)
        scatter(k, ox, oz, x * nz + z).wait_recv()
    rb[gy] = jnp.sum(ra[...], axis=0)
    for oy in range(1, ny):
        across(oy, gy).start()
    waits[1]()
    for k, (ox, oz) in enumerate(plane):
        scatter(k, ox, oz, mine).wait_send()
    for oy in range(1, ny):
        across(oy, lax.rem(gy + ny - oy, ny)).wait_recv()
    out_ref[mine] = jnp.sum(rb[...], axis=0)
    for k, (ox, oz) in enumerate(plane):
        spread(k, ox, oz, mine).start()
    waits[2]()
    for oy in range(1, ny):
        across(oy, gy).wait_send()
    for k, (ox, oz) in enumerate(plane):
        x, z = behind(ox, oz)
        spread(k, ox, oz, x * nz + z).wait_recv()
    for k, (ox, oz) in enumerate(plane):
        spread(k, ox, oz, mine).wait_send()


def fold(ref, i, tiles):
    block = jnp.concatenate(tiles, axis=0)
    outs = block.shape[1]
    ref[pl.ds(i * outs, outs)] = block.T.astype(BF)


def prepare_weights(r):
    for c in range(16):
        r.wrows[pl.ds(c, 27, stride=16)] = r.wf_in[c].astype(F32).T
    for i in range(3):
        r.wf[pl.ds(16 * i, 16)] = r.wrows[pl.ds(144 * i, 144)].T.astype(BF)
        down = [r.wd_in[9 * i + jk].astype(F32) for jk in range(9)]
        up = [r.wu_in[9 * i + jk].astype(F32).T for jk in range(9)]
        down_back = [r.wd_in[26 - 9 * i - jk].astype(F32).T for jk in range(9)]
        up_back = [r.wu_in[26 - 9 * i - jk].astype(F32) for jk in range(9)]
        fold(r.wd, i, down)
        fold(r.wu, i, up)
        fold(r.wdt, i, down_back)
        fold(r.wut, i, up_back)


def arrange_volume(r):
    spot = lane_of(16) % 64

    def plane(x, edges):
        low, high = edges
        for t, tile in enumerate(plane_rows(r.vol[:, x])):
            r.v[x, t] = tile
            wide = tile.astype(F32)
            at = t * 8 + x
            low = jnp.where(spot == at, turn(wide, at), low)
            high = jnp.where(spot == at, turn(wide, at - 63), high)
        return low, high

    zero = jnp.zeros((16, LANES), F32)
    low, high = lax.fori_loop(0, 8, plane, (zero, zero))
    r.ve[0] = low.astype(BF)
    r.ve[1] = high.astype(BF)


def arrange_cotangent(r):
    def plane(x, _):
        for t, tile in enumerate(plane_rows(r.cot[:, x])):
            r.ct[x, t] = tile
        return 0

    lax.fori_loop(0, 8, plane, 0)
    sums = pool_matrix()
    r.sums[...] = sums
    r.pg[...] = pool_tiles(r.ct, sums).astype(BF).reshape(4, 2, 16, LANES)


def fine_forward(r):
    spot = lane_of(16) % 64

    def rows(x, _):
        dx, sx = (x + 7) // 8, lax.rem(x + 7, 8)
        stacks = []
        for t in range(10):
            dy, sy = (t + 7) // 8, (t + 7) % 8
            at = sy * 8 + sx
            tile = r.vp[x, t]
            left = turn(r.vel[dx, dy], -at)
            right = turn(r.ver[dx, dy], 63 - at)
            before = jnp.where(spot == 0, left, turn(tile, 1))
            after = jnp.where(spot == 63, right, turn(tile, -1))
            stacks.append(jnp.concatenate([before, tile, after], axis=0))
        for t in range(9):
            if t > 0:
                r.v3[x, 2 * t - 1] = stacks[t]
            r.v3[x, 2 * t] = between(stacks[t], stacks[t + 1])
        return 0

    lax.fori_loop(0, 10, rows, 0)
    weight = r.wf[...]

    def convs(g, _):
        for x, pre in conv(weight, r.v3, 0, 8, (4 * g, 4 * g + 2)):
            act = (pre * sigmoid(pre)).astype(BF)
            for b in range(2):
                r.pre[x, 2 * g + b] = pre[:, b * LANES : (b + 1) * LANES]
                r.act[x, 2 * g + b] = act[:, b * LANES : (b + 1) * LANES]
        return 0

    lax.fori_loop(0, 4, convs, 0)

    sums = r.sums[...]
    lane = lane_of(32)
    low = jnp.zeros((32, LANES), F32)
    high = low
    pooled = (pool_tiles(r.act, sums) * 0.125).astype(BF).reshape(4, 2, 16, LANES)
    for x in range(4):
        for half in range(2):
            tile = jnp.concatenate([pooled[x, half], r.pg[x, half]], axis=0)
            r.m[x, half] = tile
            wide = tile.astype(F32)
            for q in range(4):
                at = (q % 2) * 64 + (x * 4 + 2 * half + q // 2) * 4
                here = (lane >= at) & (lane < at + 4)
                low = jnp.where(here, turn(wide, at - 32 * q), low)
                high = jnp.where(here, turn(wide, at - 32 * q - 28), high)
    r.me[0] = low.astype(BF)
    r.me[1] = high.astype(BF)


def mid_rows(r, first, last):
    lane = lane_of(32)
    spot = lane % 64
    none = jnp.zeros((32, LANES), BF)

    def rows(x, _):
        dx, sx = x // 4, lax.rem(x, 4)
        pairs = []
        for a in range(8):
            dy, sy = (a + 2) // 4, (a + 2) % 4
            tile = r.mp[x, a // 2]
            q = 2 * (a % 2)
            base = jnp.where(lane < 64, turn(tile, 8 - 32 * q), turn(tile, 40 - 32 * q))
            at = (sx * 4 + sy) * 4
            right = turn(r.mer[dx, dy], 40 - at)
            left = turn(r.mel[dx, dy], 4 - at)
            row = jnp.where(spot < 44, right, none)
            row = jnp.where(spot < 40, base, row)
            row = jnp.where(spot < 8, left, row)
            row = jnp.where(spot < 4, none, row)
            r.pgp[x, a] = row[16:]
            pairs.append(row[:16])
        store_taps(r.pm3, x, pairs)
        r.pm3[x, 15] = jnp.zeros((48, LANES), BF)
        r.pm3[x, 16] = jnp.zeros((48, LANES), BF)
        return 0

    lax.fori_loop(first, last, rows, 0)


def mid_convs(r, sizes, first, planes, groups):
    nx, ny, nz = sizes
    gx, gy, gz = position()
    lane = lane_of(32)
    weight = r.wd[...]
    cell = lane % 64 - 8
    mid = cell + gz * 32
    inside = (cell >= -3) & (cell < 35) & (mid >= 0) & (mid < 32 * nz)
    second = lane // 64

    def convs(g, _):
        for x, both in conv(weight, r.pm3, first, planes, (4 * g, 4 * g + 2)):
            at_x = gx * 4 + x - 3
            for b in range(2):
                pre = both[:, b * LANES : (b + 1) * LANES]
                at_y = gy * 8 + 4 * g + 2 * b - 3 + second
                keep = inside & (at_y >= 0) & (at_y < 8 * ny)
                keep = keep & (at_x >= 0) & (at_x < 4 * nx)
                sig = sigmoid(pre)
                r.am[x, 2 * g + b] = jnp.where(keep, pre * sig, 0.0).astype(BF)
                r.dsm[x, 2 * g + b] = jnp.where(keep, slope(pre, sig), 0.0).astype(BF)
        return 0

    lax.fori_loop(*groups, convs, 0)


def mid_own(r, sizes):
    mid_rows(r, 3, 9)
    mid_convs(r, sizes, 3, 4, (0, 3))
    halves = [
        jnp.concatenate([r.am[3 + a, 1 + 2 * h + m] for a in range(4) for m in range(3)], axis=1)
        for h in range(2)
    ]
    cells = jnp.concatenate(halves + [jnp.zeros((64, 12 * LANES), BF)], axis=0)
    col = lax.broadcasted_iota(jnp.int32, (8, 12 * LANES), 1)
    third, upper = col // LANES % 3, col // 64 % 2
    hit = coarse_sum_matrix(12) & ((third == 1) | ((third == 0) == (upper == 1)))
    pooled = dot_nt(jnp.where(hit, 1.0, 0.0).astype(BF), cells) * (1.0 / 64.0)
    r.pc[...] = pooled.astype(BF).astype(F32)


def mid_halo(r, sizes):
    mid_rows(r, 0, 3)
    mid_rows(r, 9, 12)
    mid_convs(r, sizes, 0, 3, (0, 4))
    mid_convs(r, sizes, 7, 3, (0, 4))
    mid_convs(r, sizes, 3, 4, (3, 4))


def coarse_pair(sizes, o):
    ny = sizes[1]
    return lax.rem(lax.axis_index("gy") + o + ny - 1, ny)


def lift_row(r, sizes, y):
    for x in range(sizes[0]):
        for y2 in range(2):
            pre = dot(r.pcg[y, x], r.wide_lift[y2])
            act = (pre * sigmoid(pre)).astype(BF)
            r.alc[x, y, y2] = act
            store_coarse_taps(r.al3, (x + 2, 2 * y + y2 + 2), act.astype(F32))


def coarse_conv(r, source, weight, x, planes, y, rows, cells):
    count = planes * rows * cells
    for i in range(3):
        for j in range(3):
            block = source[pl.ds(x + i, planes), pl.ds(y + j, rows)].reshape(count, 768)
            part = dot(block, weight[3 * i + j])
            if i + j == 0:
                r.acc[pl.ds(0, count)] = part
            else:
                r.acc[pl.ds(0, count)] += part


def coarse_forward(r, sizes, y):
    nx, cells = sizes[0], 8 * sizes[2]
    coarse_conv(r, r.al3, r.wc, 1, nx, 2 * y + 1, 2, cells)
    per = 2 * cells
    for x in range(nx):
        pre = r.acc[pl.ds(x * per, per)]
        sig = sigmoid(pre)
        r.actc[x, y] = (pre * sig).astype(BF).reshape(2, cells, 256)
        r.dsc[x, y] = slope(pre, sig).astype(BF).reshape(2, cells, 256)


def join_planes(r, first, last):
    lower_row = lane_of(32) < 64

    def join(x, _):
        pairs = []
        for m in range(7):
            lower = r.cos[(x + 1) // 4, (2 * m + 1) // 4]
            upper = r.cos[(x + 1) // 4, (2 * m + 2) // 4]
            row = r.am[x, m].astype(F32) + jnp.where(lower_row, lower, upper)
            pairs.append(row.astype(BF))
        store_taps(r.j3, x, pairs)
        return 0

    lax.fori_loop(first, last, join, 0)


def up_planes(r, scale, first, planes):
    cell = lane_of(16) % 64 - 8
    near = (cell >= -2) & (cell < 34)
    weight = r.wu[...]

    def up(g, _):
        for x, both in conv(weight, r.j3, first, planes, (4 * g, 4 * g + 2)):
            for b in range(2):
                pre = both[:, b * LANES : (b + 1) * LANES]
                sig = sigmoid(pre)
                r.su[x, 2 * g + b] = (pre * sig).astype(BF)
                pooled = r.pgp[x + 2, 2 * g + b + 1].astype(F32) * scale
                grad = jnp.where(near, pooled * slope(pre, sig), 0.0)
                r.guo[x, 2 * g + b] = grad.astype(BF)
        return 0

    lax.fori_loop(0, 3, up, 0)

    def stack(x, _):
        store_taps(r.gu3, x, [r.guo[x, m] for m in range(6)])
        return 0

    lax.fori_loop(first, first + planes, stack, 0)


def up_back_planes(r, first, planes):
    weight_t = r.wut[...]
    for starts in ((0, 2), (4, 6), (8,)):
        for x, both in conv(weight_t, r.gu3, first, planes, starts):
            for b, y in enumerate(starts):
                r.gj[x, y // 2] = both[:, b * LANES : (b + 1) * LANES]


def up_halo(r, scale):
    join_planes(r, 0, 1)
    join_planes(r, 9, 10)
    for x in (0, 7):
        up_planes(r, scale, x, 1)
    for x in (0, 5):
        up_back_planes(r, x, 1)


def up_forward(r, sizes, scale):
    cells = 8 * sizes[2]
    gx, gy, gz = position()

    def lift(o, _):
        lift_row(r, sizes, coarse_pair(sizes, o))
        return 0

    lax.fori_loop(0, min(3, sizes[1]), lift, 0)
    coarse_conv(r, r.al3, r.wc, gx, 3, 2 * gy, 4, cells)

    spread = coarse_grow_matrix(cells, gz)
    for at, (dx, dy, _, _, _, keep) in enumerate(near_cells(sizes)):
        pre = r.acc[pl.ds(at * cells, cells)]
        out = dot_nt(r.wp[...], (pre * sigmoid(pre)).astype(BF)).astype(BF)
        r.cos[dx, dy] = dot(out, spread) * keep

    join_planes(r, 1, 9)
    up_planes(r, scale, 1, 6)
    up_back_planes(r, 1, 4)

    first = lane_of(32) < 64
    totals = []
    for h in range(2):
        total = None
        for a in range(4):
            lower, middle, upper = [r.gj[1 + a, 2 * h + m] for m in range(3)]
            row = middle + jnp.where(first, upper, lower)
            total = row if total is None else total + row
        totals.append(total)
    total = jnp.concatenate(totals + [jnp.zeros((64, LANES), F32)], axis=0)
    head = total.astype(BF)
    tail = (total - head.astype(F32)).astype(BF)
    sums = jnp.where(coarse_sum_matrix(1), 1.0, 0.0).astype(BF)
    r.gc[...] = (dot_nt(sums, head) + dot_nt(sums, tail)).astype(BF).astype(F32)


def up_taps(r):
    cell = lane_of(16) % 64 - 8
    own = (cell >= 0) & (cell < 32)
    r.accu[...] = jnp.zeros(r.accu.shape, F32)
    grads = [
        jnp.concatenate(
            [jnp.where(own, r.guo[x + 2, m + 1].astype(F32), 0.0) for m in range(4)], axis=1
        ).astype(BF)
        for x in range(4)
    ]
    none = jnp.zeros((16, 4 * LANES), BF)
    for x in range(6):
        left = [grads[x - i] if 0 <= x - i < 4 else none for i in range(3)]
        right = [three(r.j3, x + 2, 2 * m + 2) for m in range(4)]
        r.accu[:, pl.ds(0, 288)] += dot_nt(
            jnp.concatenate(left, axis=0), jnp.concatenate(right, axis=1)
        )


def decode(r):
    grow = grow_matrix()

    def plane(x, _):
        rows = jnp.concatenate([r.su[x + 2, m + 1] for m in range(4)], axis=0)
        grown = dot(rows, grow)
        for a in range(2):
            for t in range(8):
                add = grown[16 * (t // 2) : 16 * (t // 2) + 16, (t % 2) * LANES :][:, :LANES]
                tile = r.act[2 * x + a, t].astype(F32) + add
                r.plane[2 * t] = tile.astype(BF)
                r.plane[2 * t + 1] = turn(tile, 64).astype(BF)
            r.dec[:, 2 * x + a] = jnp.swapaxes(r.plane[...], 0, 1)[:, :, :64]
        return 0

    lax.fori_loop(0, 4, plane, 0)


def coarse_grad_row(r, sizes, y):
    for x in range(sizes[0]):
        for y2 in range(2):
            grad = dot(r.gcg[y, x], r.wide_proj[y2]) * r.dsc[x, y, y2].astype(F32)
            grad = grad.astype(BF).astype(F32)
            store_coarse_taps(r.gp3, (x + 2, 2 * y + y2 + 2), grad)


def pay_rows(r, start, block):
    per = r.pay.shape[1]
    done = 0
    while done < block.shape[0]:
        part, at = divmod(start + done, per)
        size = min(per - at, block.shape[0] - done)
        r.pay[part, pl.ds(at, size)] = block[done : done + size]
        done += size


def backward(r, sizes, scale):
    cells = 8 * sizes[2]
    gx, gy, gz = position()

    def coarse(o, _):
        coarse_grad_row(r, sizes, coarse_pair(sizes, o))
        return 0

    lax.fori_loop(0, min(3, sizes[1]), coarse, 0)
    coarse_conv(r, r.gp3, r.wct, gx, 3, 2 * gy, 4, cells)

    spread = coarse_grow_matrix(cells, gz)
    own = lax.broadcasted_iota(jnp.int32, (cells, 256), 0) // 8 == gz
    for at, (dx, dy, x, y, y2, keep) in enumerate(near_cells(sizes)):
        pre = dot(r.pcg[y, x], r.wide_lift[y2])
        grad = (r.acc[pl.ds(at * cells, cells)] * slope(pre, sigmoid(pre))).astype(BF)
        out = dot_nt(r.wl[...], grad).astype(BF)
        r.cos[dx, dy] = dot(out, spread) * (keep * (1.0 / 64.0))
        if dx == 1 and dy in (1, 2):
            masked = jnp.where(own, grad.astype(F32), 0.0).astype(BF)
            r.pairs[y2] = dot_tn(r.pcg[y, x], masked)
    lifts = r.pairs[0, :32] + r.pairs[1, 32:64]
    for b in range(2):
        pay_rows(r, 432 + 32 * b, lifts[:, b * LANES : (b + 1) * LANES])

    first = lane_of(32) < 64

    def join(x, _):
        pairs = []
        for n in range(5):
            lower = r.cos[(x + 3) // 4, (2 * n + 3) // 4]
            upper = r.cos[(x + 3) // 4, (2 * n + 4) // 4]
            row = r.gj[x, n] + jnp.where(first, lower, upper)
            row = row * r.dsm[x + 2, n + 1].astype(F32)
            pairs.append(row.astype(BF))
        store_taps(r.gm3, x, pairs)
        return 0

    lax.fori_loop(0, 6, join, 0)

    weight_t = r.wdt[...]
    for starts in ((0, 2), (4, 6)):
        for x, both in conv(weight_t, r.gm3, 0, 4, starts):
            for b, y in enumerate(starts):
                r.gpm[x, pl.ds(8 * y, 16)] = both[:, b * LANES : (b + 1) * LANES].astype(BF)

    grow = grow_matrix()
    for x in (0, 1, 10, 11):
        r.gf[x] = jnp.zeros(r.gf.shape[1:], BF)

    def fine(x, _):
        grown = dot(r.gpm[x], grow) * 0.125
        for a in range(2):
            for t in range(8):
                add = grown[16 * (t // 2) : 16 * (t // 2) + 16, (t % 2) * LANES :][:, :LANES]
                pre = r.pre[2 * x + a, t]
                grad = r.ct[2 * x + a, t].astype(F32) * scale + add
                grad = (grad * slope(pre, sigmoid(pre))).astype(BF)
                r.gf[2 * x + a + 2, :, pl.ds(t * LANES, LANES)] = grad
        return 0

    lax.fori_loop(0, 4, fine, 0)

    r.accd[...] = jnp.zeros(r.accd.shape, F32)
    spot = lane_of(32) % 64
    inner = (spot >= 8) & (spot < 40)
    grads = [
        jnp.concatenate(
            [
                jnp.where(inner, r.gm3[x + 1, 2 * m + 1, pl.ds(32, 32)].astype(F32), 0.0)
                for m in range(4)
            ],
            axis=1,
        ).astype(BF)
        for x in range(4)
    ]
    none = jnp.zeros((32, 4 * LANES), BF)
    for x in range(6):
        left = [grads[x - i] if 0 <= x - i < 4 else none for i in range(3)]
        right = [three(r.pm3, x + 3, 2 * m + 3) for m in range(4)]
        r.accd[:, pl.ds(0, 144)] += dot_nt(
            jnp.concatenate(left, axis=0), jnp.concatenate(right, axis=1)
        )

    r.accf[...] = jnp.zeros(r.accf.shape, F32)

    def taps_fine(n, _):
        planes = (2 * n, 2 * n + 1)
        left = [jnp.concatenate([r.gf[x + 2 - i] for x in planes], axis=1) for i in range(3)]
        right = [three(r.v3, x, 2 * t) for x in planes for t in range(8)]
        r.accf[:, pl.ds(0, 144)] += dot_nt(
            jnp.concatenate(left, axis=0), jnp.concatenate(right, axis=1)
        )
        return 0

    lax.fori_loop(0, 5, taps_fine, 0)

    for b in range(2):
        pay_rows(r, 48 * b, r.accf[:, b * LANES : (b + 1) * LANES])
    for b in range(3):
        pay_rows(r, 96 + 48 * b, r.accu[:, b * LANES : (b + 1) * LANES])
    for b in range(2):
        pay_rows(r, 240 + 96 * b, r.accd[:, b * LANES : (b + 1) * LANES])
    pay_rows(r, 496, jnp.zeros((16, LANES), F32))


def coarse_taps(r, sizes, t):
    nx, ny, nz = sizes
    count = nx * ny * 16 * nz
    i, j = t // 3, lax.rem(t, 3)
    block = r.gp3[pl.ds(3 - i, nx), pl.ds(3 - j, 2 * ny)].reshape(count, 768)
    out = dot(r.cells_t[...], block)
    for k in range(3):
        r.gwc[3 * t + k] = out[:, 256 * (2 - k) : 256 * (3 - k)].astype(BF)


def proj_grad(r, sizes):
    nx, ny, nz = sizes
    cells = 8 * nz
    r.pairs[...] = jnp.zeros(r.pairs.shape, F32)

    def plane(x, _):
        for y2 in range(2):
            grads = r.gcg[:, x].reshape(ny * cells, LANES)
            r.pairs[y2] += dot_tn(grads, r.actc[x, :, y2].reshape(ny * cells, 256))
        return 0

    lax.fori_loop(0, nx, plane, 0)
    r.gwp[...] = r.pairs[0, :32] + r.pairs[1, 32:64]


def step_kernel(sizes, scale, names, *refs):
    nx, ny, nz = sizes
    count = nx * ny * 16 * nz
    r = types.SimpleNamespace(**dict(zip(names, refs, strict=True)))
    gx, gy, gz = position()
    pair = nz % 2 == 0
    mine = lax.rem(gz, 2) if pair else 0
    other = (gx, gy, gz + 1 - 2 * mine) if pair else None

    fetch = [
        pltpu.make_async_copy(source, target, r.fetched.at[n])
        for n, (source, target) in enumerate(
            ((r.vol_in, r.vol), (r.cot_in, r.cot), (r.wc_in, r.wc))
        )
    ]
    for copy in fetch:
        copy.start()

    def arrange():
        fetch[0].wait()
        arrange_volume(r)

    greet(sizes, arrange)

    def first_wait():
        prepare_weights(r)
        fetch[1].wait()
        arrange_cotangent(r)
        place_weight(r.wide_lift, r.wl[...])
        place_weight(r.wide_proj, r.wp[...])

    halo_round(sizes, 1, 1, (r.v, r.ve, r.vp, r.ver, r.vel, r.vsend, r.vrecv), first_wait)
    fine_forward(r)

    def second_wait():
        zero_rim(r.al3, 2)
        zero_rim(r.gp3, 2)
        fetch[2].wait()

        def turn_weights(t, _):
            for k in range(3):
                block = r.wc[8 - t, pl.ds(256 * (2 - k), 256)]
                r.wct[t, pl.ds(256 * k, 256)] = block.T
            return 0

        lax.fori_loop(0, 9, turn_weights, 0)

    halo_round(sizes, 4, 1, (r.m, r.me, r.mp, r.mer, r.mel, r.msend, r.mrecv), second_wait)
    mid_own(r, sizes)
    sems = (r.ga_send, r.ga_recv, r.gb_send, r.gb_recv)
    pooled_rest = gather_round(
        sizes, (r.pc, r.pcg, r.pstage) + sems, lambda: mid_halo(r, sizes), nothing
    )
    up_forward(r, sizes, scale)

    decoded = pltpu.make_async_copy(r.dec, r.dec_out, r.fetched.at[3])

    def third_wait():
        up_halo(r, scale)
        up_taps(r)

    near = min(3, ny)

    def far_row(n, whose):
        return coarse_pair(sizes, 2 * n + whose if pair else n)

    def far_count(whose, count=ny):
        return (count + 1 - whose) // 2 if pair else count

    def far_copies(n, whose):
        y = far_row(n, whose)
        return [
            pltpu.make_async_remote_copy(
                src_ref=ref.at[:, pl.ds(y, 1)],
                dst_ref=ref.at[:, pl.ds(y, 1)],
                send_sem=r.far_send.at[part, n],
                recv_sem=r.far_recv.at[part, n],
                device_id=other,
                device_id_type=MESH,
            )
            for part, ref in enumerate((r.actc, r.dsc))
        ]

    def fourth_wait():
        pooled_rest()

        def lift(o, _):
            lift_row(r, sizes, coarse_pair(sizes, o))
            return 0

        lax.fori_loop(near, ny, lift, 0)

        def coarse(n, _):
            coarse_forward(r, sizes, far_row(n, mine))
            if pair:
                for copy in far_copies(n, mine):
                    copy.start()
            return 0

        lax.fori_loop(0, far_count(mine), coarse, 0)

    def arrived(n, _):
        for copy in far_copies(n, 1 - mine):
            copy.wait_recv()
        return 0

    sems = (r.ha_send, r.ha_recv, r.hb_send, r.hb_recv)
    grads_rest = gather_round(sizes, (r.gc, r.gcg, r.gstage) + sems, third_wait, fourth_wait)
    if pair:
        lax.fori_loop(0, far_count(1 - mine, near), arrived, 0)
    backward(r, sizes, scale)

    half = 5 if pair else 9

    def taps_count(whose):
        return half - whose

    def keep_taps(n):
        taps = pl.ds(3 * (n + half * mine), 3)
        return pltpu.make_async_copy(r.gwc.at[taps], r.gwc_out.at[taps], r.kept.at[n])

    def send_taps(n, whose):
        taps = pl.ds(3 * (n + half * whose), 3)
        return pltpu.make_async_remote_copy(
            src_ref=r.gwc.at[taps],
            dst_ref=r.gwc_out.at[taps],
            send_sem=r.tap_send.at[n],
            recv_sem=r.tap_recv.at[n],
            device_id=other,
            device_id_type=MESH,
        )

    def do_taps(first, last):
        def taps(n, _):
            coarse_taps(r, sizes, n + half * mine)
            keep_taps(n).start()
            if pair:
                send_taps(n, mine).start()
            return 0

        lax.fori_loop(first, last, taps, 0)

    def wait_a():
        grads_rest()
        if pair:
            lax.fori_loop(far_count(1 - mine, near), far_count(1 - mine), arrived, 0)

        def coarse(o, _):
            coarse_grad_row(r, sizes, coarse_pair(sizes, o))
            return 0

        lax.fori_loop(near, ny, coarse, 0)
        r.cells_t[...] = r.alc[...].reshape(count, 256).T
        do_taps(0, 1)

    def wait_b():
        decode(r)
        decoded.start()
        do_taps(1, 3)

    def wait_c():
        do_taps(3, taps_count(mine))
        proj_grad(r, sizes)

    sems = (r.ra_send, r.ra_recv, r.rb_send, r.rb_recv, r.rc_send, r.rc_recv)
    reduce_round(sizes, (r.pay, r.red, r.ra, r.rb) + sems, (wait_a, wait_b, wait_c))

    def finish(n, _):
        keep_taps(n).wait()
        if pair:
            send_taps(n, mine).wait_send()
        return 0

    lax.fori_loop(0, taps_count(mine), finish, 0)
    decoded.wait()
    if pair:

        def sent(n, _):
            for copy in far_copies(n, mine):
                copy.wait_send()
            return 0

        def landed(n, _):
            send_taps(n, 1 - mine).wait_recv()
            return 0

        lax.fori_loop(0, far_count(mine), sent, 0)
        lax.fori_loop(0, taps_count(1 - mine), landed, 0)


def last_kernel(
    gwc_in,
    red_in,
    gwp_in,
    wc_out,
    wf_out,
    wd_out,
    wl_out,
    wp_out,
    wu_out,
    rows,
    narrow,
    wide,
    red_ref,
    load_sem,
    store_sem,
):
    blocks = [pl.ds(3 * n, 3) for n in range(9)]
    loads = [
        pltpu.make_async_copy(gwc_in.at[block], narrow.at[block], load_sem.at[n])
        for n, block in enumerate(blocks)
    ]
    stores = [
        pltpu.make_async_copy(wide.at[block], wc_out.at[block], store_sem.at[n])
        for n, block in enumerate(blocks)
    ]
    loads.append(pltpu.make_async_copy(red_in, red_ref, load_sem.at[9]))
    loads.append(pltpu.make_async_copy(gwp_in, wp_out, load_sem.at[10]))
    for load in loads:
        load.start()
    for n, block in enumerate(blocks):
        loads[n].wait()
        wide[block] = narrow[block].astype(F32)
        stores[n].start()

    loads[9].wait()
    loads[10].wait()

    def columns(start, blocks, count):
        return jnp.concatenate(
            [red_ref[pl.ds(start + count * b, count)] for b in range(blocks)], axis=1
        )

    table = columns(0, 2, 48)
    for i in range(3):
        rows[pl.ds(144 * i, 144)] = table[16 * i : 16 * i + 16, :144].T
    for c in range(16):
        wf_out[c] = rows[pl.ds(c, 27, stride=16)].T
    table = columns(96, 3, 48)
    for i in range(3):
        for jk in range(9):
            wu_out[9 * i + jk] = table[16 * i : 16 * i + 16, 32 * jk : 32 * jk + 32]
    table = columns(240, 2, 96)
    for i in range(3):
        part = table[32 * i : 32 * i + 32, :144]
        wd_out[pl.ds(9 * i, 9)] = part.T.reshape(9, 16, 32)
    wl_out[...] = columns(432, 2, 32)
    for store in stores:
        store.wait()


VMEM = pl.BlockSpec(memory_space=pltpu.VMEM)
HBM = pl.BlockSpec(memory_space=pl.ANY)


def shards(sizes, volume, w_fine, w_down, w_lift, w_coarse, w_proj, w_up, cotangent):
    nx, ny, nz = sizes
    scale = 1.0 / math.sqrt(8 * nx * 16 * ny * 64 * nz)
    cells = 8 * nz
    parts = nx * nz
    per = 512 // parts
    grid = (nx, ny, 2, cells, 256)
    gathered = (ny, nx, cells, LANES)
    ins = {
        "wf_in": jnp.transpose(w_fine, (1, 2, 0)),
        "wd_in": w_down,
        "wu_in": jnp.transpose(w_up, (0, 2, 1)),
        "wl": w_lift,
        "wp": jnp.transpose(w_proj),
        "vol_in": volume,
        "cot_in": cotangent,
        "wc_in": w_coarse.reshape(9, 768, 256),
    }
    outs = {
        "red": ((parts, per, LANES), F32),
        "gwp": ((32, 256), F32),
        "dec_out": ((16, 8, 16, 64), BF),
        "gwc_out": ((27, 256, 256), BF),
    }
    narrow = {
        "vol": (16, 8, 16, 64),
        "cot": (16, 8, 16, 64),
        "dec": (16, 8, 16, 64),
        "v": (8, 8, 16, LANES),
        "ve": (2, 16, LANES),
        "vp": (10, 10, 16, LANES),
        "ver": (3, 3, 16, LANES),
        "vel": (3, 3, 16, LANES),
        "ct": (8, 8, 16, LANES),
        "sums": (8 * LANES, LANES),
        "pg": (4, 2, 16, LANES),
        "wf": (48, 144),
        "wd": (96, 144),
        "wu": (48, 288),
        "wdt": (48, 288),
        "wut": (96, 144),
        "v3": (10, 17, 48, LANES),
        "act": (8, 8, 16, LANES),
        "m": (4, 2, 32, LANES),
        "me": (2, 32, LANES),
        "mp": (12, 4, 32, LANES),
        "mer": (3, 3, 32, LANES),
        "mel": (3, 3, 32, LANES),
        "pm3": (12, 17, 48, LANES),
        "pgp": (12, 8, 16, LANES),
        "am": (10, 8, 32, LANES),
        "dsm": (10, 8, 32, LANES),
        "pcg": gathered,
        "gcg": gathered,
        "wc": (9, 768, 256),
        "wct": (9, 768, 256),
        "wide_lift": (2, LANES, 256),
        "wide_proj": (2, LANES, 256),
        "al3": (nx + 4, 2 * ny + 4, cells, 768),
        "gp3": (nx + 4, 2 * ny + 4, cells, 768),
        "alc": grid,
        "actc": grid,
        "dsc": grid,
        "j3": (10, 13, 96, LANES),
        "guo": (8, 6, 16, LANES),
        "gu3": (8, 11, 48, LANES),
        "su": (8, 6, 16, LANES),
        "plane": (16, 16, LANES),
        "gm3": (6, 9, 96, LANES),
        "gpm": (4, 64, LANES),
        "gf": (12, 16, 8 * LANES),
        "cells_t": (256, nx * ny * 2 * cells),
        "gwc": (27, 256, 256),
    }
    wide = {
        "wrows": (432, 16),
        "pre": (8, 8, 16, LANES),
        "pc": (8, LANES),
        "pstage": (nx, cells, LANES),
        "acc": (max(nx * 2, 12) * cells, 256),
        "cos": (3, 4, 32, LANES),
        "gj": (6, 5, 32, LANES),
        "gc": (8, LANES),
        "gstage": (nx, cells, LANES),
        "accu": (48, 3 * LANES),
        "accf": (48, 2 * LANES),
        "accd": (96, 2 * LANES),
        "pairs": (2, LANES, 256),
        "pay": (parts, per, LANES),
        "ra": (parts, per, LANES),
        "rb": (ny, per, LANES),
    }
    sems = {
        "vsend": 26,
        "vrecv": 26,
        "msend": 26,
        "mrecv": 26,
        "ga_send": parts,
        "ga_recv": parts,
        "gb_send": ny,
        "gb_recv": ny,
        "ha_send": parts,
        "ha_recv": parts,
        "hb_send": ny,
        "hb_recv": ny,
        "ra_send": parts,
        "ra_recv": parts,
        "rb_send": ny,
        "rb_recv": ny,
        "rc_send": parts,
        "rc_recv": parts,
        "kept": 9,
        "tap_send": 9,
        "tap_recv": 9,
        "fetched": 4,
    }
    far = {"far_send": (2, ny), "far_recv": (2, ny)}
    names = list(ins) + list(outs) + list(narrow) + list(wide) + list(sems) + list(far)
    red, gwp, dec, gwc = pl.pallas_call(
        functools.partial(step_kernel, sizes, scale, names),
        out_shape=[jax.ShapeDtypeStruct(shape, kind) for shape, kind in outs.values()],
        in_specs=[VMEM] * (len(ins) - 3) + [HBM] * 3,
        out_specs=[VMEM] * 2 + [HBM] * 2,
        scratch_shapes=[pltpu.VMEM(shape, BF) for shape in narrow.values()]
        + [pltpu.VMEM(shape, F32) for shape in wide.values()]
        + [pltpu.SemaphoreType.DMA((size,)) for size in sems.values()]
        + [pltpu.SemaphoreType.DMA(shape) for shape in far.values()],
        compiler_params=pltpu.CompilerParams(
            vmem_limit_bytes=62 * 1024 * 1024, collective_id=1, has_side_effects=True
        ),
    )(*ins.values())
    shapes = [(27, 256, 256), (16, 16, 27), (27, 16, 32), (32, 256), (32, 256), (27, 16, 32)]

    gwc, gwf, gwd, gwl, gwp, gwu = pl.pallas_call(
        last_kernel,
        out_shape=[jax.ShapeDtypeStruct(shape, F32) for shape in shapes],
        in_specs=[HBM] * 3,
        out_specs=[HBM] + [VMEM] * 5,
        scratch_shapes=[
            pltpu.VMEM((432, 16), F32),
            pltpu.VMEM((27, 256, 256), BF),
            pltpu.VMEM((27, 256, 256), F32),
            pltpu.VMEM((512, LANES), F32),
            pltpu.SemaphoreType.DMA((11,)),
            pltpu.SemaphoreType.DMA((9,)),
        ],
        compiler_params=pltpu.CompilerParams(vmem_limit_bytes=62 * 1024 * 1024),
    )(gwc, red.reshape(512, LANES), gwp)
    gwf = jnp.transpose(gwf, (2, 0, 1))
    gwu = jnp.transpose(gwu, (0, 2, 1))
    return dec, gwf, gwd, gwl, gwc, jnp.transpose(gwp), gwu


def solution(mesh):
    sizes = tuple(mesh.shape[name] for name in ("gx", "gy", "gz"))
    block = P(None, "gx", "gy", "gz")
    return jax.shard_map(
        functools.partial(shards, sizes),
        mesh=mesh,
        in_specs=(block, P(), P(), P(), P(), P(), P(), block),
        out_specs=(block, P(), P(), P(), P(), P(), P()),
        check_vma=False,
    )
```

```python
import functools
import math
import types

import jax
import jax.numpy as jnp
from jax import lax
from jax.experimental import pallas as pl
from jax.experimental.pallas import tpu as pltpu
from jax.sharding import PartitionSpec as P

BF = jnp.bfloat16
F32 = jnp.float32
MESH = pl.DeviceIdType.MESH
LANES = 128


def dot(left, right):
    return jnp.dot(left, right, preferred_element_type=F32)


def dot_nt(left, right):
    return lax.dot_general(left, right, (((1,), (1,)), ((), ())), preferred_element_type=F32)


def dot_tn(left, right):
    return lax.dot_general(left, right, (((0,), (0,)), ((), ())), preferred_element_type=F32)


def sigmoid(values):
    return 0.5 * jnp.tanh(0.5 * values) + 0.5


def slope(values, sig):
    return sig * (1.0 + values * (1.0 - sig))


def lane_of(rows):
    return lax.broadcasted_iota(jnp.int32, (rows, LANES), 1)


def turn(tile, by):
    if isinstance(by, int):
        by = by % LANES
        return tile if by == 0 else pltpu.roll(tile, by, 1)
    return pltpu.roll(tile, lax.rem(by + 4 * LANES, LANES), 1)


def tap_rows(pair):
    return jnp.concatenate([turn(pair, 1), pair, turn(pair, -1)], axis=0)


def between(lower, upper):
    lane = lane_of(lower.shape[0])
    return jnp.where(lane < 64, turn(lower, 64), turn(upper, 64))


def store_taps(ref, x, pairs):
    stacks = [tap_rows(pair) for pair in pairs]
    for n, stack in enumerate(stacks):
        ref[x, 2 * n] = stack
        if n + 1 < len(stacks):
            ref[x, 2 * n + 1] = between(stack, stacks[n + 1])


def three(ref, x, y):
    block = ref[x, pl.ds(y, 3)]
    return block.reshape(3 * block.shape[1], LANES)


def conv(weight, ref, first, planes, starts):
    outs = weight.shape[0] // 3
    parts = []
    for n in range(planes + 2):
        tiles = [three(ref, first + n, y) for y in starts]
        block = tiles[0] if len(tiles) == 1 else jnp.concatenate(tiles, axis=1)
        parts.append(dot(weight, block))
        if n >= 2:
            yield (
                first + n - 2,
                parts[n - 2][:outs] + parts[n - 1][outs : 2 * outs] + parts[n][2 * outs :],
            )


def pool_matrix():
    row = lax.broadcasted_iota(jnp.int32, (8 * LANES, LANES), 0)
    col = lax.broadcasted_iota(jnp.int32, (8 * LANES, LANES), 1)
    hit = (row // 256 == col // 32) & (row % 64 // 2 == col % 32)
    return jnp.where(hit, 1.0, 0.0).astype(BF)


def pool_tiles(ref, sums):
    cells = [
        jnp.concatenate([ref[2 * x + a, 4 * half + q] for q in range(4) for a in range(2)], axis=1)
        for x in range(4)
        for half in range(2)
    ]
    return dot(jnp.concatenate(cells, axis=0), sums)


def grow_matrix():
    row = lax.broadcasted_iota(jnp.int32, (LANES, 2 * LANES), 0)
    col = lax.broadcasted_iota(jnp.int32, (LANES, 2 * LANES), 1)
    hit = (row // 64 == col // LANES) & (row % 64 - 8 == col % 64 // 2)
    return jnp.where(hit, 1.0, 0.0).astype(BF)


def coarse_sum_matrix(tiles):
    row = lax.broadcasted_iota(jnp.int32, (8, tiles * LANES), 0)
    cell = lax.broadcasted_iota(jnp.int32, (8, tiles * LANES), 1) % 64 - 8
    return (cell >= 0) & (cell < 32) & ((cell + 4) // 4 == row + 1)


def coarse_grow_matrix(cells, gz):
    row = lax.broadcasted_iota(jnp.int32, (cells, LANES), 0)
    cell = lax.broadcasted_iota(jnp.int32, (cells, LANES), 1) % 64 - 8
    mid = cell + gz * 32
    hit = (cell >= -3) & (cell < 35) & (mid >= 0) & (row == (mid + 4) // 4 - 1)
    return jnp.where(hit, 1.0, 0.0).astype(BF)


def plane_rows(block):
    rows = jnp.swapaxes(block, 0, 1)
    return [jnp.concatenate([rows[2 * t], rows[2 * t + 1]], axis=1) for t in range(8)]


def place_weight(ref, weight):
    for y2 in range(2):
        ref[y2] = jnp.zeros((LANES, 256), BF)
        ref[y2, pl.ds(32 * y2, 32)] = weight


def store_coarse_taps(ref, at, cells):
    count = cells.shape[0]
    row = lax.broadcasted_iota(jnp.int32, cells.shape, 0)
    before = jnp.where(row > 0, pltpu.roll(cells, 1, 0), 0.0)
    after = jnp.where(row < count - 1, pltpu.roll(cells, count - 1, 0), 0.0)
    ref[at + (slice(None), pl.ds(0, 256))] = before.astype(BF)
    ref[at + (slice(None), pl.ds(256, 256))] = cells.astype(BF)
    ref[at + (slice(None), pl.ds(512, 256))] = after.astype(BF)


def zero_rim(ref, rim):
    planes, rows = ref.shape[:2]

    def clear(x, _):
        for y in list(range(rim)) + list(range(rows - rim, rows)):
            ref[x, y] = jnp.zeros(ref.shape[2:], ref.dtype)
        return 0

    lax.fori_loop(0, planes, clear, 0)

    def clear_plane(y, _):
        for x in list(range(rim)) + list(range(planes - rim, planes)):
            ref[x, y] = jnp.zeros(ref.shape[2:], ref.dtype)
        return 0

    lax.fori_loop(0, rows, clear_plane, 0)


def clamp(at, count):
    return jnp.minimum(jnp.maximum(at, 0), count - 1)


def near_cells(sizes):
    nx, ny, _ = sizes
    gx, gy = lax.axis_index("gx"), lax.axis_index("gy")
    found = []
    for dx in range(3):
        for dy in range(4):
            x, y = gx - 1 + dx, gy + (dy + 1) // 2 - 1
            there = (x >= 0) & (x < nx) & (y >= 0) & (y < ny)
            keep = jnp.where(there, 1.0, 0.0)
            found.append((dx, dy, clamp(x, nx), clamp(y, ny), (dy + 1) % 2, keep))
    return found


NEIGHBOURS = [
    (dx, dy, dz)
    for dz in (-1, 1, 0)
    for dx in (-1, 0, 1)
    for dy in (-1, 0, 1)
    if (dx, dy, dz) != (0, 0, 0)
]


def position():
    return [lax.axis_index(name) for name in ("gx", "gy", "gz")]


def valid(sizes, steps):
    found = None
    for at, size, step in zip(position(), sizes, steps):
        if step != 0:
            test = at > 0 if step < 0 else at < size - 1
            found = test if found is None else found & test
    return found


def plane_peers(nx, nz):
    return [(ox, oz) for ox in range(nx) for oz in range(nz) if (ox, oz) != (0, 0)]


def greet(sizes, work):
    nx, ny, nz = sizes
    me = gx, gy, gz = position()
    barrier = pltpu.get_barrier_semaphore()
    peers = [(lax.rem(gx + ox, nx), gy, lax.rem(gz + oz, nz)) for ox, oz in plane_peers(nx, nz)]
    peers += [(gx, lax.rem(gy + oy, ny), gz) for oy in range(1, ny)]
    for peer in peers:
        pl.semaphore_signal(barrier, inc=1, device_id=peer, device_id_type=MESH)
    total = 1
    for axis in range(3):
        low = jnp.where(me[axis] > 0, 1, 0)
        high = jnp.where(me[axis] < sizes[axis] - 1, 1, 0)
        total = total * (1 + low + high)
    for steps in NEIGHBOURS:

        @pl.when(valid(sizes, steps))
        def _():
            pl.semaphore_signal(
                barrier,
                inc=1,
                device_id=tuple(me[axis] + steps[axis] for axis in range(3)),
                device_id_type=MESH,
            )

    work()
    pl.semaphore_wait(barrier, total - 1 + len(peers))


def halo_round(sizes, hx, ht, refs, meanwhile):
    a_ref, e_ref, p_ref, er_ref, el_ref, send_sem, recv_sem = refs
    me = [lax.axis_index(name) for name in ("gx", "gy", "gz")]
    planes, tiles = a_ref.shape[:2]

    def part(step, halo, count):
        if step == 0:
            return pl.ds(0, count), pl.ds(halo, count)
        if step > 0:
            return pl.ds(count - halo, halo), pl.ds(0, halo)
        return pl.ds(0, halo), pl.ds(count + halo, halo)

    def copy_of(k, steps):
        dx, dy, dz = steps
        if dz == 0:
            fx, tx = part(dx, hx, planes)
            fy, ty = part(dy, ht, tiles)
            src, dst = a_ref.at[fx, fy], p_ref.at[tx, ty]
        elif dz > 0:
            src, dst = e_ref.at[1], el_ref.at[1 - dx, 1 - dy]
        else:
            src, dst = e_ref.at[0], er_ref.at[1 - dx, 1 - dy]
        return pltpu.make_async_remote_copy(
            src_ref=src,
            dst_ref=dst,
            send_sem=send_sem.at[k],
            recv_sem=recv_sem.at[k],
            device_id=(me[0] + dx, me[1] + dy, me[2] + dz),
            device_id_type=MESH,
        )

    for k, steps in enumerate(NEIGHBOURS):

        @pl.when(valid(sizes, steps))
        def _():
            copy_of(k, steps).start()

    p_ref[pl.ds(hx, planes), pl.ds(ht, tiles)] = a_ref[...]
    for k, steps in enumerate(NEIGHBOURS):
        back = tuple(-step for step in steps)
        dx, dy, dz = steps

        @pl.when(jnp.logical_not(valid(sizes, back)))
        def _():
            if dz == 0:
                _, tx = part(dx, hx, planes)
                _, ty = part(dy, ht, tiles)
                into = p_ref.at[tx, ty]
            elif dz > 0:
                into = el_ref.at[1 - dx, 1 - dy]
            else:
                into = er_ref.at[1 - dx, 1 - dy]
            into[...] = jnp.zeros(into.shape, into.dtype)

    meanwhile()
    for k, steps in enumerate(NEIGHBOURS):
        back = tuple(-step for step in steps)

        @pl.when(valid(sizes, back))
        def _():
            copy_of(k, steps).wait_recv()

    for k, steps in enumerate(NEIGHBOURS):

        @pl.when(valid(sizes, steps))
        def _():
            copy_of(k, steps).wait_send()


def gather_round(sizes, refs, first_wait, second_wait):
    g_ref, all_ref, stage, send_a, recv_a, send_b, recv_b = refs
    nx, ny, nz = sizes
    gx, gy, gz = [lax.axis_index(name) for name in ("gx", "gy", "gz")]
    plane = plane_peers(nx, nz)

    def first(k, x, z, peer):
        return pltpu.make_async_remote_copy(
            src_ref=g_ref,
            dst_ref=stage.at[x, pl.ds(pl.multiple_of(z * 8, 8), 8)],
            send_sem=send_a.at[k],
            recv_sem=recv_a.at[k],
            device_id=peer,
            device_id_type=MESH,
        )

    def second(oy, y):
        return pltpu.make_async_remote_copy(
            src_ref=all_ref.at[gy],
            dst_ref=all_ref.at[y],
            send_sem=send_b.at[oy],
            recv_sem=recv_b.at[oy],
            device_id=(gx, lax.rem(gy + oy, ny), gz),
            device_id_type=MESH,
        )

    for k, (ox, oz) in enumerate(plane):
        first(k, gx, gz, (lax.rem(gx + ox, nx), gy, lax.rem(gz + oz, nz))).start()
    stage[gx, pl.ds(pl.multiple_of(gz * 8, 8), 8)] = g_ref[...]
    first_wait()
    for k, (ox, oz) in enumerate(plane):
        peer = (lax.rem(gx + ox, nx), gy, lax.rem(gz + oz, nz))
        first(k, lax.rem(gx + nx - ox, nx), lax.rem(gz + nz - oz, nz), peer).wait_recv()
    all_ref[gy] = stage[...].astype(BF)
    for oy in range(1, ny):
        second(oy, gy).start()
    second_wait()
    near = sorted({1, ny - 1}) if ny > 1 else []
    for oy in near:
        second(oy, lax.rem(gy + ny - oy, ny)).wait_recv()

    def rest():
        for k, (ox, oz) in enumerate(plane):
            first(k, gx, gz, (lax.rem(gx + ox, nx), gy, lax.rem(gz + oz, nz))).wait_send()
        for oy in range(1, ny):
            if oy not in near:
                second(oy, lax.rem(gy + ny - oy, ny)).wait_recv()
        for oy in range(1, ny):
            second(oy, gy).wait_send()

    return rest


def reduce_round(sizes, refs, waits):
    pay_ref, out_ref, ra, rb, send_a, recv_a, send_b, recv_b, send_c, recv_c = refs
    nx, ny, nz = sizes
    gx, gy, gz = [lax.axis_index(name) for name in ("gx", "gy", "gz")]
    mine = gx * nz + gz
    plane = plane_peers(nx, nz)

    def ahead(ox, oz):
        return lax.rem(gx + ox, nx), lax.rem(gz + oz, nz)

    def behind(ox, oz):
        return lax.rem(gx + nx - ox, nx), lax.rem(gz + nz - oz, nz)

    def scatter(k, ox, oz, slot):
        x, z = ahead(ox, oz)
        return pltpu.make_async_remote_copy(
            src_ref=pay_ref.at[x * nz + z],
            dst_ref=ra.at[slot],
            send_sem=send_a.at[k],
            recv_sem=recv_a.at[k],
            device_id=(x, gy, z),
            device_id_type=MESH,
        )

    def across(oy, slot):
        return pltpu.make_async_remote_copy(
            src_ref=rb.at[gy],
            dst_ref=rb.at[slot],
            send_sem=send_b.at[oy],
            recv_sem=recv_b.at[oy],
            device_id=(gx, lax.rem(gy + oy, ny), gz),
            device_id_type=MESH,
        )

    def spread(k, ox, oz, slot):
        x, z = ahead(ox, oz)
        return pltpu.make_async_remote_copy(
            src_ref=out_ref.at[mine],
            dst_ref=out_ref.at[slot],
            send_sem=send_c.at[k],
            recv_sem=recv_c.at[k],
            device_id=(x, gy, z),
            device_id_type=MESH,
        )

    for k, (ox, oz) in enumerate(plane):
        scatter(k, ox, oz, mine).start()
    ra[mine] = pay_ref[mine]
    waits[0]()
    for k, (ox, oz) in enumerate(plane):
        x, z = behind(ox, oz)
        scatter(k, ox, oz, x * nz + z).wait_recv()
    rb[gy] = jnp.sum(ra[...], axis=0)
    for oy in range(1, ny):
        across(oy, gy).start()
    waits[1]()
    for k, (ox, oz) in enumerate(plane):
        scatter(k, ox, oz, mine).wait_send()
    for oy in range(1, ny):
        across(oy, lax.rem(gy + ny - oy, ny)).wait_recv()
    out_ref[mine] = jnp.sum(rb[...], axis=0)
    for k, (ox, oz) in enumerate(plane):
        spread(k, ox, oz, mine).start()
    waits[2]()
    for oy in range(1, ny):
        across(oy, gy).wait_send()
    for k, (ox, oz) in enumerate(plane):
        x, z = behind(ox, oz)
        spread(k, ox, oz, x * nz + z).wait_recv()
    for k, (ox, oz) in enumerate(plane):
        spread(k, ox, oz, mine).wait_send()


def fold(ref, i, tiles):
    block = jnp.concatenate(tiles, axis=0)
    outs = block.shape[1]
    ref[pl.ds(i * outs, outs)] = block.T.astype(BF)


def prepare_weights(r):
    for c in range(16):
        r.wrows[pl.ds(c, 27, stride=16)] = r.wf_in[c].astype(F32).T
    for i in range(3):
        r.wf[pl.ds(16 * i, 16)] = r.wrows[pl.ds(144 * i, 144)].T.astype(BF)
        fold(r.wd, i, [r.wd_in[9 * i + jk].astype(F32) for jk in range(9)])


def prepare_later_weights(r):
    for i in range(3):
        fold(r.wu, i, [r.wu_in[9 * i + jk].astype(F32).T for jk in range(9)])
        fold(r.wdt, i, [r.wd_in[26 - 9 * i - jk].astype(F32).T for jk in range(9)])
        fold(r.wut, i, [r.wu_in[26 - 9 * i - jk].astype(F32) for jk in range(9)])


def arrange_volume(r):
    spot = lane_of(16) % 64

    def plane(x, edges):
        low, high = edges
        for t, tile in enumerate(plane_rows(r.vol[:, x])):
            r.v[x, t] = tile
            wide = tile.astype(F32)
            at = t * 8 + x
            low = jnp.where(spot == at, turn(wide, at), low)
            high = jnp.where(spot == at, turn(wide, at - 63), high)
        return low, high

    zero = jnp.zeros((16, LANES), F32)
    low, high = lax.fori_loop(0, 8, plane, (zero, zero))
    r.ve[0] = low.astype(BF)
    r.ve[1] = high.astype(BF)


def arrange_cotangent(r):
    def plane(x, _):
        for t, tile in enumerate(plane_rows(r.cot[:, x])):
            r.ct[x, t] = tile
        return 0

    lax.fori_loop(0, 8, plane, 0)
    sums = pool_matrix()
    r.sums[...] = sums
    r.pg[...] = pool_tiles(r.ct, sums).astype(BF).reshape(4, 2, 16, LANES)


def fine_forward(r):
    spot = lane_of(16) % 64

    def rows(x, _):
        dx, sx = (x + 7) // 8, lax.rem(x + 7, 8)
        stacks = []
        for t in range(10):
            dy, sy = (t + 7) // 8, (t + 7) % 8
            at = sy * 8 + sx
            tile = r.vp[x, t]
            left = turn(r.vel[dx, dy], -at)
            right = turn(r.ver[dx, dy], 63 - at)
            before = jnp.where(spot == 0, left, turn(tile, 1))
            after = jnp.where(spot == 63, right, turn(tile, -1))
            stacks.append(jnp.concatenate([before, tile, after], axis=0))
        for t in range(9):
            if t > 0:
                r.v3[x, 2 * t - 1] = stacks[t]
            r.v3[x, 2 * t] = between(stacks[t], stacks[t + 1])
        return 0

    lax.fori_loop(0, 10, rows, 0)
    weight = r.wf[...]

    def convs(g, _):
        for x, pre in conv(weight, r.v3, 0, 8, (4 * g, 4 * g + 2)):
            act = (pre * sigmoid(pre)).astype(BF)
            for b in range(2):
                r.pre[x, 2 * g + b] = pre[:, b * LANES : (b + 1) * LANES]
                r.act[x, 2 * g + b] = act[:, b * LANES : (b + 1) * LANES]
        return 0

    for g in range(4):
        convs(g, 0)

    sums = r.sums[...]
    lane = lane_of(32)
    low = jnp.zeros((32, LANES), F32)
    high = low
    pooled = (pool_tiles(r.act, sums) * 0.125).astype(BF).reshape(4, 2, 16, LANES)
    for x in range(4):
        for half in range(2):
            tile = jnp.concatenate([pooled[x, half], r.pg[x, half]], axis=0)
            r.m[x, half] = tile
            wide = tile.astype(F32)
            for q in range(4):
                at = (q % 2) * 64 + (x * 4 + 2 * half + q // 2) * 4
                here = (lane >= at) & (lane < at + 4)
                low = jnp.where(here, turn(wide, at - 32 * q), low)
                high = jnp.where(here, turn(wide, at - 32 * q - 28), high)
    r.me[0] = low.astype(BF)
    r.me[1] = high.astype(BF)


def mid_rows(r, first, last):
    lane = lane_of(32)
    spot = lane % 64
    none = jnp.zeros((32, LANES), BF)

    def rows(x, _):
        dx, sx = x // 4, lax.rem(x, 4)
        pairs = []
        for a in range(8):
            dy, sy = (a + 2) // 4, (a + 2) % 4
            tile = r.mp[x, a // 2]
            q = 2 * (a % 2)
            base = jnp.where(lane < 64, turn(tile, 8 - 32 * q), turn(tile, 40 - 32 * q))
            at = (sx * 4 + sy) * 4
            right = turn(r.mer[dx, dy], 40 - at)
            left = turn(r.mel[dx, dy], 4 - at)
            row = jnp.where(spot < 44, right, none)
            row = jnp.where(spot < 40, base, row)
            row = jnp.where(spot < 8, left, row)
            row = jnp.where(spot < 4, none, row)
            r.pgp[x, a] = row[16:]
            pairs.append(row[:16])
        store_taps(r.pm3, x, pairs)
        r.pm3[x, 15] = jnp.zeros((48, LANES), BF)
        r.pm3[x, 16] = jnp.zeros((48, LANES), BF)
        return 0

    lax.fori_loop(first, last, rows, 0)


def mid_convs(r, sizes, first, planes, groups):
    nx, ny, nz = sizes
    gx, gy, gz = position()
    lane = lane_of(32)
    weight = r.wd[...]
    cell = lane % 64 - 8
    mid = cell + gz * 32
    inside = (cell >= -3) & (cell < 35) & (mid >= 0) & (mid < 32 * nz)
    second = lane // 64

    def convs(g, _):
        for x, both in conv(weight, r.pm3, first, planes, (4 * g, 4 * g + 2)):
            at_x = gx * 4 + x - 3
            for b in range(2):
                pre = both[:, b * LANES : (b + 1) * LANES]
                at_y = gy * 8 + 4 * g + 2 * b - 3 + second
                keep = inside & (at_y >= 0) & (at_y < 8 * ny)
                keep = keep & (at_x >= 0) & (at_x < 4 * nx)
                sig = sigmoid(pre)
                r.am[x, 2 * g + b] = jnp.where(keep, pre * sig, 0.0).astype(BF)
                r.dsm[x, 2 * g + b] = jnp.where(keep, slope(pre, sig), 0.0).astype(BF)
        return 0

    for g in range(*groups):
        convs(g, 0)


def mid_own(r, sizes):
    mid_rows(r, 3, 9)
    mid_convs(r, sizes, 3, 4, (0, 3))
    halves = [
        jnp.concatenate([r.am[3 + a, 1 + 2 * h + m] for a in range(4) for m in range(3)], axis=1)
        for h in range(2)
    ]
    cells = jnp.concatenate(halves + [jnp.zeros((64, 12 * LANES), BF)], axis=0)
    col = lax.broadcasted_iota(jnp.int32, (8, 12 * LANES), 1)
    third, upper = col // LANES % 3, col // 64 % 2
    hit = coarse_sum_matrix(12) & ((third == 1) | ((third == 0) == (upper == 1)))
    pooled = dot_nt(jnp.where(hit, 1.0, 0.0).astype(BF), cells) * (1.0 / 64.0)
    r.pc[...] = pooled.astype(BF).astype(F32)


def mid_halo(r, sizes):
    mid_rows(r, 0, 3)
    mid_rows(r, 9, 12)
    mid_convs(r, sizes, 0, 3, (0, 4))
    mid_convs(r, sizes, 7, 3, (0, 4))
    mid_convs(r, sizes, 3, 4, (3, 4))


def coarse_pair(sizes, o):
    ny = sizes[1]
    return lax.rem(lax.axis_index("gy") + o + ny - 1, ny)


def lift_row(r, sizes, y):
    for x in range(sizes[0]):
        for y2 in range(2):
            pre = dot(r.pcg[y, x], r.wide_lift[y2])
            act = (pre * sigmoid(pre)).astype(BF)
            r.alc[x, y, y2] = act
            store_coarse_taps(r.al3, (x + 2, 2 * y + y2 + 2), act.astype(F32))


def coarse_conv(r, source, weight, x, planes, y, rows, cells):
    count = planes * rows * cells
    for i in range(3):
        for j in range(3):
            block = source[pl.ds(x + i, planes), pl.ds(y + j, rows)].reshape(count, 768)
            part = dot(block, weight[3 * i + j])
            if i + j == 0:
                r.acc[pl.ds(0, count)] = part
            else:
                r.acc[pl.ds(0, count)] += part


def coarse_forward(r, sizes, y):
    nx, cells = sizes[0], 8 * sizes[2]
    coarse_conv(r, r.al3, r.wc, 1, nx, 2 * y + 1, 2, cells)
    per = 2 * cells
    for x in range(nx):
        pre = r.acc[pl.ds(x * per, per)]
        sig = sigmoid(pre)
        r.actc[x, y] = (pre * sig).astype(BF).reshape(2, cells, 256)
        r.dsc[x, y] = slope(pre, sig).astype(BF).reshape(2, cells, 256)


def join_planes(r, first, last):
    lower_row = lane_of(32) < 64

    def join(x, _):
        pairs = []
        for m in range(7):
            lower = r.cos[(x + 1) // 4, (2 * m + 1) // 4]
            upper = r.cos[(x + 1) // 4, (2 * m + 2) // 4]
            row = r.am[x, m].astype(F32) + jnp.where(lower_row, lower, upper)
            pairs.append(row.astype(BF))
        store_taps(r.j3, x, pairs)
        return 0

    lax.fori_loop(first, last, join, 0)


def up_planes(r, scale, first, planes):
    cell = lane_of(16) % 64 - 8
    near = (cell >= -2) & (cell < 34)
    weight = r.wu[...]

    def up(g, _):
        for x, both in conv(weight, r.j3, first, planes, (4 * g, 4 * g + 2)):
            for b in range(2):
                pre = both[:, b * LANES : (b + 1) * LANES]
                sig = sigmoid(pre)
                r.su[x, 2 * g + b] = (pre * sig).astype(BF)
                pooled = r.pgp[x + 2, 2 * g + b + 1].astype(F32) * scale
                grad = jnp.where(near, pooled * slope(pre, sig), 0.0)
                r.guo[x, 2 * g + b] = grad.astype(BF)
        return 0

    for g in range(3):
        up(g, 0)

    def stack(x, _):
        store_taps(r.gu3, x, [r.guo[x, m] for m in range(6)])
        return 0

    lax.fori_loop(first, first + planes, stack, 0)


def up_back_planes(r, first, planes):
    weight_t = r.wut[...]
    for starts in ((0, 2), (4, 6), (8,)):
        for x, both in conv(weight_t, r.gu3, first, planes, starts):
            for b, y in enumerate(starts):
                r.gj[x, y // 2] = both[:, b * LANES : (b + 1) * LANES]


def up_halo(r, scale):
    join_planes(r, 0, 1)
    join_planes(r, 9, 10)
    for x in (0, 7):
        up_planes(r, scale, x, 1)
    for x in (0, 5):
        up_back_planes(r, x, 1)


def up_forward(r, sizes, scale):
    cells = 8 * sizes[2]
    gx, gy, gz = position()

    def lift(o, _):
        lift_row(r, sizes, coarse_pair(sizes, o))
        return 0

    lax.fori_loop(0, min(3, sizes[1]), lift, 0)
    coarse_conv(r, r.al3, r.wc, gx, 3, 2 * gy, 4, cells)

    spread = coarse_grow_matrix(cells, gz)
    for at, (dx, dy, _, _, _, keep) in enumerate(near_cells(sizes)):
        pre = r.acc[pl.ds(at * cells, cells)]
        out = dot_nt(r.wp[...], (pre * sigmoid(pre)).astype(BF)).astype(BF)
        r.cos[dx, dy] = dot(out, spread) * keep

    join_planes(r, 1, 9)
    up_planes(r, scale, 1, 6)
    up_back_planes(r, 1, 4)

    first = lane_of(32) < 64
    totals = []
    for h in range(2):
        total = None
        for a in range(4):
            lower, middle, upper = [r.gj[1 + a, 2 * h + m] for m in range(3)]
            row = middle + jnp.where(first, upper, lower)
            total = row if total is None else total + row
        totals.append(total)
    total = jnp.concatenate(totals + [jnp.zeros((64, LANES), F32)], axis=0)
    head = total.astype(BF)
    tail = (total - head.astype(F32)).astype(BF)
    sums = jnp.where(coarse_sum_matrix(1), 1.0, 0.0).astype(BF)
    r.gc[...] = (dot_nt(sums, head) + dot_nt(sums, tail)).astype(BF).astype(F32)


def up_taps(r):
    cell = lane_of(16) % 64 - 8
    own = (cell >= 0) & (cell < 32)
    r.accu[...] = jnp.zeros(r.accu.shape, F32)
    grads = [
        jnp.concatenate(
            [jnp.where(own, r.guo[x + 2, m + 1].astype(F32), 0.0) for m in range(4)], axis=1
        ).astype(BF)
        for x in range(4)
    ]
    none = jnp.zeros((16, 4 * LANES), BF)
    for x in range(6):
        left = [grads[x - i] if 0 <= x - i < 4 else none for i in range(3)]
        right = [three(r.j3, x + 2, 2 * m + 2) for m in range(4)]
        r.accu[:, pl.ds(0, 288)] += dot_nt(
            jnp.concatenate(left, axis=0), jnp.concatenate(right, axis=1)
        )


def decode(r):
    grow = grow_matrix()

    def plane(x, _):
        rows = jnp.concatenate([r.su[x + 2, m + 1] for m in range(4)], axis=0)
        grown = dot(rows, grow)
        for a in range(2):
            for t in range(8):
                add = grown[16 * (t // 2) : 16 * (t // 2) + 16, (t % 2) * LANES :][:, :LANES]
                tile = r.act[2 * x + a, t].astype(F32) + add
                r.plane[2 * t] = tile.astype(BF)
                r.plane[2 * t + 1] = turn(tile, 64).astype(BF)
            r.dec[:, 2 * x + a] = jnp.swapaxes(r.plane[...], 0, 1)[:, :, :64]
        return 0

    lax.fori_loop(0, 4, plane, 0)


def coarse_grad_row(r, sizes, y):
    for x in range(sizes[0]):
        for y2 in range(2):
            grad = dot(r.gcg[y, x], r.wide_proj[y2]) * r.dsc[x, y, y2].astype(F32)
            grad = grad.astype(BF).astype(F32)
            store_coarse_taps(r.gp3, (x + 2, 2 * y + y2 + 2), grad)


def pay_rows(r, start, block):
    per = r.pay.shape[1]
    done = 0
    while done < block.shape[0]:
        part, at = divmod(start + done, per)
        size = min(per - at, block.shape[0] - done)
        r.pay[part, pl.ds(at, size)] = block[done : done + size]
        done += size


def backward(r, sizes, scale):
    cells = 8 * sizes[2]
    gx, gy, gz = position()

    def coarse(o, _):
        coarse_grad_row(r, sizes, coarse_pair(sizes, o))
        return 0

    lax.fori_loop(0, min(3, sizes[1]), coarse, 0)
    coarse_conv(r, r.gp3, r.wct, gx, 3, 2 * gy, 4, cells)

    spread = coarse_grow_matrix(cells, gz)
    own = lax.broadcasted_iota(jnp.int32, (cells, 256), 0) // 8 == gz
    for at, (dx, dy, x, y, y2, keep) in enumerate(near_cells(sizes)):
        pre = dot(r.pcg[y, x], r.wide_lift[y2])
        grad = (r.acc[pl.ds(at * cells, cells)] * slope(pre, sigmoid(pre))).astype(BF)
        out = dot_nt(r.wl[...], grad).astype(BF)
        r.cos[dx, dy] = dot(out, spread) * (keep * (1.0 / 64.0))
        if dx == 1 and dy in (1, 2):
            masked = jnp.where(own, grad.astype(F32), 0.0).astype(BF)
            r.pairs[y2] = dot_tn(r.pcg[y, x], masked)
    lifts = r.pairs[0, :32] + r.pairs[1, 32:64]
    for b in range(2):
        pay_rows(r, 432 + 32 * b, lifts[:, b * LANES : (b + 1) * LANES])

    first = lane_of(32) < 64

    def join(x, _):
        pairs = []
        for n in range(5):
            lower = r.cos[(x + 3) // 4, (2 * n + 3) // 4]
            upper = r.cos[(x + 3) // 4, (2 * n + 4) // 4]
            row = r.gj[x, n] + jnp.where(first, lower, upper)
            row = row * r.dsm[x + 2, n + 1].astype(F32)
            pairs.append(row.astype(BF))
        store_taps(r.gm3, x, pairs)
        return 0

    lax.fori_loop(0, 6, join, 0)

    weight_t = r.wdt[...]
    for starts in ((0, 2), (4, 6)):
        for x, both in conv(weight_t, r.gm3, 0, 4, starts):
            for b, y in enumerate(starts):
                r.gpm[x, pl.ds(8 * y, 16)] = both[:, b * LANES : (b + 1) * LANES].astype(BF)

    grow = grow_matrix()
    for x in (0, 1, 10, 11):
        r.gf[x] = jnp.zeros(r.gf.shape[1:], BF)

    def fine(x, _):
        grown = dot(r.gpm[x], grow) * 0.125
        for a in range(2):
            for t in range(8):
                add = grown[16 * (t // 2) : 16 * (t // 2) + 16, (t % 2) * LANES :][:, :LANES]
                pre = r.pre[2 * x + a, t]
                grad = r.ct[2 * x + a, t].astype(F32) * scale + add
                grad = (grad * slope(pre, sigmoid(pre))).astype(BF)
                r.gf[2 * x + a + 2, :, pl.ds(t * LANES, LANES)] = grad
        return 0

    lax.fori_loop(0, 4, fine, 0)

    r.accd[...] = jnp.zeros(r.accd.shape, F32)
    spot = lane_of(32) % 64
    inner = (spot >= 8) & (spot < 40)
    grads = [
        jnp.concatenate(
            [
                jnp.where(inner, r.gm3[x + 1, 2 * m + 1, pl.ds(32, 32)].astype(F32), 0.0)
                for m in range(4)
            ],
            axis=1,
        ).astype(BF)
        for x in range(4)
    ]
    none = jnp.zeros((32, 4 * LANES), BF)
    for x in range(6):
        left = [grads[x - i] if 0 <= x - i < 4 else none for i in range(3)]
        right = [three(r.pm3, x + 3, 2 * m + 3) for m in range(4)]
        r.accd[:, pl.ds(0, 144)] += dot_nt(
            jnp.concatenate(left, axis=0), jnp.concatenate(right, axis=1)
        )

    r.accf[...] = jnp.zeros(r.accf.shape, F32)

    def taps_fine(n, _):
        planes = (2 * n, 2 * n + 1)
        left = [jnp.concatenate([r.gf[x + 2 - i] for x in planes], axis=1) for i in range(3)]
        right = [three(r.v3, x, 2 * t) for x in planes for t in range(8)]
        r.accf[:, pl.ds(0, 144)] += dot_nt(
            jnp.concatenate(left, axis=0), jnp.concatenate(right, axis=1)
        )
        return 0

    for n in range(5):
        taps_fine(n, 0)

    for b in range(2):
        pay_rows(r, 48 * b, r.accf[:, b * LANES : (b + 1) * LANES])
    for b in range(3):
        pay_rows(r, 96 + 48 * b, r.accu[:, b * LANES : (b + 1) * LANES])
    for b in range(2):
        pay_rows(r, 240 + 96 * b, r.accd[:, b * LANES : (b + 1) * LANES])
    pay_rows(r, 496, jnp.zeros((16, LANES), F32))


def coarse_taps(r, sizes, t):
    nx, ny, nz = sizes
    count = nx * ny * 16 * nz
    i, j = t // 3, lax.rem(t, 3)
    block = r.gp3[pl.ds(3 - i, nx), pl.ds(3 - j, 2 * ny)].reshape(count, 768)
    out = dot(r.cells_t[...], block)
    for k in range(3):
        r.gwc[3 * t + k] = out[:, 256 * (2 - k) : 256 * (3 - k)].astype(BF)


def proj_grad(r, sizes):
    nx, ny, nz = sizes
    cells = 8 * nz
    r.pairs[...] = jnp.zeros(r.pairs.shape, F32)

    def plane(x, _):
        for y2 in range(2):
            grads = r.gcg[:, x].reshape(ny * cells, LANES)
            r.pairs[y2] += dot_tn(grads, r.actc[x, :, y2].reshape(ny * cells, 256))
        return 0

    lax.fori_loop(0, nx, plane, 0)
    r.gwp[...] = r.pairs[0, :32] + r.pairs[1, 32:64]


def step_kernel(sizes, scale, names, *refs):
    nx, ny, nz = sizes
    count = nx * ny * 16 * nz
    r = types.SimpleNamespace(**dict(zip(names, refs, strict=True)))
    gx, gy, gz = position()
    pair = nz % 2 == 0
    mine = lax.rem(gz, 2) if pair else 0
    other = (gx, gy, gz + 1 - 2 * mine) if pair else None

    fetch = [
        pltpu.make_async_copy(source, target, r.fetched.at[n])
        for n, (source, target) in enumerate(
            ((r.vol_in, r.vol), (r.cot_in, r.cot), (r.wc_in, r.wc))
        )
    ]
    for copy in fetch:
        copy.start()

    def arrange():
        fetch[0].wait()
        arrange_volume(r)

    greet(sizes, arrange)

    def first_wait():
        prepare_weights(r)
        fetch[1].wait()
        arrange_cotangent(r)
        place_weight(r.wide_lift, r.wl[...])
        place_weight(r.wide_proj, r.wp[...])

    halo_round(sizes, 1, 1, (r.v, r.ve, r.vp, r.ver, r.vel, r.vsend, r.vrecv), first_wait)
    fine_forward(r)

    def second_wait():
        zero_rim(r.al3, 2)
        zero_rim(r.gp3, 2)
        fetch[2].wait()

        def turn_weights(t, _):
            for k in range(3):
                block = r.wc[8 - t, pl.ds(256 * (2 - k), 256)]
                r.wct[t, pl.ds(256 * k, 256)] = block.T
            return 0

        lax.fori_loop(0, 9, turn_weights, 0)

    halo_round(sizes, 4, 1, (r.m, r.me, r.mp, r.mer, r.mel, r.msend, r.mrecv), second_wait)
    mid_own(r, sizes)
    sems = (r.ga_send, r.ga_recv, r.gb_send, r.gb_recv)
    pooled_rest = gather_round(
        sizes,
        (r.pc, r.pcg, r.pstage) + sems,
        lambda: mid_halo(r, sizes),
        lambda: prepare_later_weights(r),
    )
    up_forward(r, sizes, scale)

    decoded = pltpu.make_async_copy(r.dec, r.dec_out, r.fetched.at[3])

    def third_wait():
        up_halo(r, scale)
        up_taps(r)

    near = min(3, ny)
    soon = max(near, ny - 2)

    def far_row(n, whose):
        return coarse_pair(sizes, 2 * n + whose if pair else n)

    def far_count(whose, count=ny):
        return (count + 1 - whose) // 2 if pair else count

    def far_copies(n, whose):
        y = far_row(n, whose)
        return [
            pltpu.make_async_remote_copy(
                src_ref=ref.at[:, pl.ds(y, 1)],
                dst_ref=ref.at[:, pl.ds(y, 1)],
                send_sem=r.far_send.at[part, n],
                recv_sem=r.far_recv.at[part, n],
                device_id=other,
                device_id_type=MESH,
            )
            for part, ref in enumerate((r.actc, r.dsc))
        ]

    def fourth_wait():
        pooled_rest()

        def lift(o, _):
            lift_row(r, sizes, coarse_pair(sizes, o))
            return 0

        lax.fori_loop(near, ny, lift, 0)

        lax.fori_loop(0, far_count(mine, soon), coarse_share, 0)

    def coarse_share(n, _):
        coarse_forward(r, sizes, far_row(n, mine))
        if pair:
            for copy in far_copies(n, mine):
                copy.start()
        return 0

    def arrived(n, _):
        for copy in far_copies(n, 1 - mine):
            copy.wait_recv()
        return 0

    sems = (r.ha_send, r.ha_recv, r.hb_send, r.hb_recv)
    grads_rest = gather_round(sizes, (r.gc, r.gcg, r.gstage) + sems, third_wait, fourth_wait)
    if pair:
        lax.fori_loop(0, far_count(1 - mine, near), arrived, 0)
    backward(r, sizes, scale)

    half = 5 if pair else 9

    def taps_count(whose):
        return half - whose

    def keep_taps(n):
        taps = pl.ds(3 * (n + half * mine), 3)
        return pltpu.make_async_copy(r.gwc.at[taps], r.gwc_out.at[taps], r.kept.at[n])

    def send_taps(n, whose):
        taps = pl.ds(3 * (n + half * whose), 3)
        return pltpu.make_async_remote_copy(
            src_ref=r.gwc.at[taps],
            dst_ref=r.gwc_out.at[taps],
            send_sem=r.tap_send.at[n],
            recv_sem=r.tap_recv.at[n],
            device_id=other,
            device_id_type=MESH,
        )

    def do_taps(first, last):
        def taps(n, _):
            coarse_taps(r, sizes, n + half * mine)
            keep_taps(n).start()
            if pair:
                send_taps(n, mine).start()
            return 0

        lax.fori_loop(first, last, taps, 0)

    def coarse_grads(first, last):
        if pair:
            lax.fori_loop(far_count(1 - mine, first), far_count(1 - mine, last), arrived, 0)

        def coarse(o, _):
            coarse_grad_row(r, sizes, coarse_pair(sizes, o))
            return 0

        lax.fori_loop(first, last, coarse, 0)

    def wait_a():
        lax.fori_loop(far_count(mine, soon), far_count(mine), coarse_share, 0)
        grads_rest()
        coarse_grads(near, soon)
        r.cells_t[...] = r.alc[...].reshape(count, 256).T
        coarse_grads(soon, ny)
        do_taps(0, 1)

    def wait_b():
        do_taps(1, 4)

    def wait_c():
        do_taps(4, taps_count(mine))
        decode(r)
        decoded.start()
        proj_grad(r, sizes)

    sems = (r.ra_send, r.ra_recv, r.rb_send, r.rb_recv, r.rc_send, r.rc_recv)
    reduce_round(sizes, (r.pay, r.red, r.ra, r.rb) + sems, (wait_a, wait_b, wait_c))

    def finish(n, _):
        keep_taps(n).wait()
        if pair:
            send_taps(n, mine).wait_send()
        return 0

    lax.fori_loop(0, taps_count(mine), finish, 0)
    decoded.wait()
    if pair:

        def sent(n, _):
            for copy in far_copies(n, mine):
                copy.wait_send()
            return 0

        def landed(n, _):
            send_taps(n, 1 - mine).wait_recv()
            return 0

        lax.fori_loop(0, far_count(mine), sent, 0)
        lax.fori_loop(0, taps_count(1 - mine), landed, 0)


def last_kernel(
    gwc_in,
    red_in,
    gwp_in,
    wc_out,
    wf_out,
    wd_out,
    wl_out,
    wp_out,
    wu_out,
    rows,
    narrow,
    wide,
    red_ref,
    load_sem,
    store_sem,
):
    blocks = [pl.ds(3 * n, 3) for n in range(9)]
    loads = [
        pltpu.make_async_copy(gwc_in.at[block], narrow.at[block], load_sem.at[n])
        for n, block in enumerate(blocks)
    ]
    stores = [
        pltpu.make_async_copy(wide.at[block], wc_out.at[block], store_sem.at[n])
        for n, block in enumerate(blocks)
    ]
    loads.append(pltpu.make_async_copy(red_in, red_ref, load_sem.at[9]))
    loads.append(pltpu.make_async_copy(gwp_in, wp_out, load_sem.at[10]))
    for load in loads:
        load.start()
    for n, block in enumerate(blocks):
        loads[n].wait()
        wide[block] = narrow[block].astype(F32)
        stores[n].start()

    loads[9].wait()
    loads[10].wait()

    def columns(start, blocks, count):
        return jnp.concatenate(
            [red_ref[pl.ds(start + count * b, count)] for b in range(blocks)], axis=1
        )

    table = columns(0, 2, 48)
    for i in range(3):
        rows[pl.ds(144 * i, 144)] = table[16 * i : 16 * i + 16, :144].T
    for c in range(16):
        wf_out[c] = rows[pl.ds(c, 27, stride=16)].T
    table = columns(96, 3, 48)
    for i in range(3):
        for jk in range(9):
            wu_out[9 * i + jk] = table[16 * i : 16 * i + 16, 32 * jk : 32 * jk + 32]
    table = columns(240, 2, 96)
    for i in range(3):
        part = table[32 * i : 32 * i + 32, :144]
        wd_out[pl.ds(9 * i, 9)] = part.T.reshape(9, 16, 32)
    wl_out[...] = columns(432, 2, 32)
    for store in stores:
        store.wait()


VMEM = pl.BlockSpec(memory_space=pltpu.VMEM)
HBM = pl.BlockSpec(memory_space=pl.ANY)


def shards(sizes, volume, w_fine, w_down, w_lift, w_coarse, w_proj, w_up, cotangent):
    nx, ny, nz = sizes
    scale = 1.0 / math.sqrt(8 * nx * 16 * ny * 64 * nz)
    cells = 8 * nz
    parts = nx * nz
    per = 512 // parts
    grid = (nx, ny, 2, cells, 256)
    gathered = (ny, nx, cells, LANES)
    ins = {
        "wf_in": jnp.transpose(w_fine, (1, 2, 0)),
        "wd_in": w_down,
        "wu_in": jnp.transpose(w_up, (0, 2, 1)),
        "wl": w_lift,
        "wp": jnp.transpose(w_proj),
        "vol_in": volume,
        "cot_in": cotangent,
        "wc_in": w_coarse.reshape(9, 768, 256),
    }
    outs = {
        "red": ((parts, per, LANES), F32),
        "gwp": ((32, 256), F32),
        "dec_out": ((16, 8, 16, 64), BF),
        "gwc_out": ((27, 256, 256), BF),
    }
    narrow = {
        "vol": (16, 8, 16, 64),
        "cot": (16, 8, 16, 64),
        "dec": (16, 8, 16, 64),
        "v": (8, 8, 16, LANES),
        "ve": (2, 16, LANES),
        "vp": (10, 10, 16, LANES),
        "ver": (3, 3, 16, LANES),
        "vel": (3, 3, 16, LANES),
        "ct": (8, 8, 16, LANES),
        "sums": (8 * LANES, LANES),
        "pg": (4, 2, 16, LANES),
        "wf": (48, 144),
        "wd": (96, 144),
        "wu": (48, 288),
        "wdt": (48, 288),
        "wut": (96, 144),
        "v3": (10, 17, 48, LANES),
        "act": (8, 8, 16, LANES),
        "m": (4, 2, 32, LANES),
        "me": (2, 32, LANES),
        "mp": (12, 4, 32, LANES),
        "mer": (3, 3, 32, LANES),
        "mel": (3, 3, 32, LANES),
        "pm3": (12, 17, 48, LANES),
        "pgp": (12, 8, 16, LANES),
        "am": (10, 8, 32, LANES),
        "dsm": (10, 8, 32, LANES),
        "pcg": gathered,
        "gcg": gathered,
        "wc": (9, 768, 256),
        "wct": (9, 768, 256),
        "wide_lift": (2, LANES, 256),
        "wide_proj": (2, LANES, 256),
        "al3": (nx + 4, 2 * ny + 4, cells, 768),
        "gp3": (nx + 4, 2 * ny + 4, cells, 768),
        "alc": grid,
        "actc": grid,
        "dsc": grid,
        "j3": (10, 13, 96, LANES),
        "guo": (8, 6, 16, LANES),
        "gu3": (8, 11, 48, LANES),
        "su": (8, 6, 16, LANES),
        "plane": (16, 16, LANES),
        "gm3": (6, 9, 96, LANES),
        "gpm": (4, 64, LANES),
        "gf": (12, 16, 8 * LANES),
        "cells_t": (256, nx * ny * 2 * cells),
        "gwc": (27, 256, 256),
    }
    wide = {
        "wrows": (432, 16),
        "pre": (8, 8, 16, LANES),
        "pc": (8, LANES),
        "pstage": (nx, cells, LANES),
        "acc": (max(nx * 2, 12) * cells, 256),
        "cos": (3, 4, 32, LANES),
        "gj": (6, 5, 32, LANES),
        "gc": (8, LANES),
        "gstage": (nx, cells, LANES),
        "accu": (48, 3 * LANES),
        "accf": (48, 2 * LANES),
        "accd": (96, 2 * LANES),
        "pairs": (2, LANES, 256),
        "pay": (parts, per, LANES),
        "ra": (parts, per, LANES),
        "rb": (ny, per, LANES),
    }
    sems = {
        "vsend": 26,
        "vrecv": 26,
        "msend": 26,
        "mrecv": 26,
        "ga_send": parts,
        "ga_recv": parts,
        "gb_send": ny,
        "gb_recv": ny,
        "ha_send": parts,
        "ha_recv": parts,
        "hb_send": ny,
        "hb_recv": ny,
        "ra_send": parts,
        "ra_recv": parts,
        "rb_send": ny,
        "rb_recv": ny,
        "rc_send": parts,
        "rc_recv": parts,
        "kept": 9,
        "tap_send": 9,
        "tap_recv": 9,
        "fetched": 4,
    }
    far = {"far_send": (2, ny), "far_recv": (2, ny)}
    names = list(ins) + list(outs) + list(narrow) + list(wide) + list(sems) + list(far)
    red, gwp, dec, gwc = pl.pallas_call(
        functools.partial(step_kernel, sizes, scale, names),
        out_shape=[jax.ShapeDtypeStruct(shape, kind) for shape, kind in outs.values()],
        in_specs=[VMEM] * (len(ins) - 3) + [HBM] * 3,
        out_specs=[VMEM] * 2 + [HBM] * 2,
        scratch_shapes=[pltpu.VMEM(shape, BF) for shape in narrow.values()]
        + [pltpu.VMEM(shape, F32) for shape in wide.values()]
        + [pltpu.SemaphoreType.DMA((size,)) for size in sems.values()]
        + [pltpu.SemaphoreType.DMA(shape) for shape in far.values()],
        compiler_params=pltpu.CompilerParams(
            vmem_limit_bytes=62 * 1024 * 1024, collective_id=1, has_side_effects=True
        ),
    )(*ins.values())
    shapes = [(27, 256, 256), (16, 16, 27), (27, 16, 32), (32, 256), (32, 256), (27, 16, 32)]

    gwc, gwf, gwd, gwl, gwp, gwu = pl.pallas_call(
        last_kernel,
        out_shape=[jax.ShapeDtypeStruct(shape, F32) for shape in shapes],
        in_specs=[HBM] * 3,
        out_specs=[HBM] + [VMEM] * 5,
        scratch_shapes=[
            pltpu.VMEM((432, 16), F32),
            pltpu.VMEM((27, 256, 256), BF),
            pltpu.VMEM((27, 256, 256), F32),
            pltpu.VMEM((512, LANES), F32),
            pltpu.SemaphoreType.DMA((11,)),
            pltpu.SemaphoreType.DMA((9,)),
        ],
        compiler_params=pltpu.CompilerParams(vmem_limit_bytes=62 * 1024 * 1024),
    )(gwc, red.reshape(512, LANES), gwp)
    gwf = jnp.transpose(gwf, (2, 0, 1))
    gwu = jnp.transpose(gwu, (0, 2, 1))
    return dec, gwf, gwd, gwl, gwc, jnp.transpose(gwp), gwu


def solution(mesh):
    sizes = tuple(mesh.shape[name] for name in ("gx", "gy", "gz"))
    block = P(None, "gx", "gy", "gz")
    return jax.shard_map(
        functools.partial(shards, sizes),
        mesh=mesh,
        in_specs=(block, P(), P(), P(), P(), P(), P(), block),
        out_specs=(block, P(), P(), P(), P(), P(), P()),
        check_vma=False,
    )
```
